32 devices in a mesh: groups: 2 (over y), seq: 4 (over z), tp: 4 (over x, core).
Axes of the slice: x: 2, y: 2, z: 4, core: 2. Of those that a mesh axis runs over, the one named last changes fastest.
Arguments:
- queries: bfloat16 [8, 128, 5120], P('groups', 'seq', 'tp'), parts along dimension 0, may hold values from -40 to 40
- key_vectors: bfloat16 [8, 128, 5120], P('groups', 'seq', 'tp'), parts along dimension 0, may hold values from -40 to 40
- value_vectors: bfloat16 [8, 128, 5120], P('groups', 'seq', 'tp'), parts along dimension 0, may hold values from -6 to 6
- block_mask: int32 [40, 4, 4], P('tp'), may hold values from 0 to 1, as said below
- out_weight: bfloat16 [40, 128, 2560], P('tp', 'seq'), may hold values from -0.5 to 0.5
Outputs:
- projected: bfloat16 [8, 128, 2560], P('groups', 'seq', 'tp'), parts along dimension 0
The draws below stay inside these ranges and needn't reach their ends.
There are 2 independent parts, one for each index of `groups`. The reference program is written for one: setup_inputs(seed, part) draws one part's arguments, and reference() takes and returns one part's arrays. A program takes and returns all parts, laid end to end along the dimension named above; an argument that names none is the same for every part. Nothing has to cross between parts.
Inputs may be any that keep to these rules, and one draw needn't show every extreme that they name: block_mask[h, b, b] = 1 for every head and block; every row of a head's mask has at most 4 ones, and every head has a row with exactly 4.
All inputs are finite; a program needn't handle non-finite values.
Results may differ from the reference program's by a relative error of at most 0.012.
Values may be sent and summed in bfloat16 or wider, within the bound.
A program may use at most 64 MiB of HBM per device.

```python
import jax
import jax.numpy as jnp
from jax import lax

HEADS = 40
HD = 128
DOUT = 2560
BLOCK = 128
NB = 4
KMAX = 4


def query_key_pair(key):
    base = jax.random.fold_in(key, 11)
    first_key, second_key = jax.random.split(base)
    shape = (NB, BLOCK, HEADS * HD)
    spread = 2.0 ** 0.5
    query_raw = jnp.clip(jax.random.normal(first_key, shape, jnp.float32) * spread, -6.0 * spread, 6.0 * spread)
    key_raw = jnp.clip(jax.random.normal(second_key, shape, jnp.float32) * spread, -6.0 * spread, 6.0 * spread)
    return (query_raw, key_raw)


def draw_queries(key, part):
    query_raw, key_raw = query_key_pair(key)
    return query_raw.astype(jnp.bfloat16)


def draw_key_vectors(key, part):
    query_raw, key_raw = query_key_pair(key)
    return key_raw.astype(jnp.bfloat16)


def draw_block_mask(key, part):
    first_key, second_key, third_key, fourth_key = jax.random.split(jax.random.fold_in(key, 23), 4)
    lowest = jax.random.randint(first_key, (HEADS, 1), 1, KMAX + 1)
    uniform_bits = jax.random.randint(second_key, (HEADS, NB), 0, 1 << 20)
    wanted = lowest + uniform_bits % (KMAX - lowest + 1)
    forced_row = jax.random.randint(fourth_key, (HEADS, 1), 0, NB)
    row_ids = jnp.arange(NB, dtype=jnp.int32)
    wanted = jnp.where(row_ids[None, :] == forced_row, KMAX, wanted)
    noise = jax.random.randint(third_key, (HEADS, NB, NB), 0, 1 << 20)
    ranking = noise * NB + row_ids[None, None, :]
    diagonal = row_ids[:, None] == row_ids[None, :]
    ranking = jnp.where(diagonal[None, :, :], -1, ranking)
    position = jnp.argsort(jnp.argsort(ranking, axis=-1), axis=-1)
    return (position < wanted[:, :, None]).astype(jnp.int32)


def shard_levels(stream_key, extent, shards, smallest, high):
    gain = 1.0
    for dim, blocks in shards:
        draws = jax.random.uniform(jax.random.fold_in(jax.random.fold_in(stream_key, 6), dim), (blocks,), jnp.float32, smallest / len(shards), high / len(shards))
        gain = gain * jnp.repeat(jnp.exp(draws), extent[dim] // blocks).reshape((-1,) + (1,) * (len(extent) - 1 - dim))
    return gain


def normal_values(own_key, shape, width, most, cuts=(), kind=jnp.bfloat16):
    result = jax.random.normal(own_key, shape, jnp.float32) * width
    if len(cuts) > 0:
        result = shard_levels(own_key, shape, cuts, -0.22, 0.18) * result
    return jnp.clip(result, min=-most, max=most).astype(kind)


def setup_inputs(seed: int = 0, part: int = 0) -> dict:
    streams_of = jax.random.split(jax.random.key(seed), 6)
    own_keys = jax.random.split(jax.random.fold_in(streams_of[5], part), 6)
    return {
        "queries": draw_queries(jax.random.fold_in(jax.random.fold_in(streams_of[5], part), 71), part),
        "key_vectors": draw_key_vectors(jax.random.fold_in(jax.random.fold_in(streams_of[5], part), 71), part),
        "value_vectors": normal_values(own_keys[2], (NB, BLOCK, HEADS * HD), 1.0, 6.0, ((1, 4), (2, 4))),
        "block_mask": draw_block_mask(jax.random.fold_in(streams_of[5], 71), part),
        "out_weight": normal_values(streams_of[4], (HEADS, HD, DOUT), HD ** -0.5, 0.5, ((0, 4), (1, 4))),
    }


def attend_head(head_queries, head_keys, head_values, head_mask):
    column_ids = jnp.arange(NB, dtype=jnp.int32)
    ranking = (1 - head_mask) * NB + column_ids[None, :]
    key_pick = jnp.argsort(ranking, axis=-1)[:, :KMAX].astype(jnp.int32)
    key_live = jnp.take_along_axis(head_mask, key_pick, axis=-1)
    chosen_keys = head_keys[key_pick].astype(jnp.float32)
    chosen_values = head_values[key_pick].astype(jnp.float32)
    scores = jnp.einsum("qid,qkjd->qikj", head_queries.astype(jnp.float32), chosen_keys) * (HD ** -0.5)
    scores = jnp.where((key_live > 0)[:, None, :, None], scores, -jnp.inf)
    largest = jnp.max(scores, axis=(2, 3), keepdims=True)
    weights = jnp.exp(scores - largest)
    totals = jnp.sum(weights, axis=(2, 3))
    rounded = lax.optimization_barrier(weights.astype(jnp.bfloat16)).astype(jnp.float32)
    blended = jnp.einsum("qikj,qkjd->qid", rounded, chosen_values)
    return (blended / totals[..., None]).astype(jnp.bfloat16)


def reference(queries, key_vectors, value_vectors, block_mask, out_weight):
    def one_head(head_index):
        start_col = (head_index * HD).astype(jnp.int32)
        head_queries = lax.dynamic_slice_in_dim(queries, start_col, HD, 2)
        head_keys = lax.dynamic_slice_in_dim(key_vectors, start_col, HD, 2)
        head_values = lax.dynamic_slice_in_dim(value_vectors, start_col, HD, 2)
        return attend_head(head_queries, head_keys, head_values, block_mask[head_index])

    per_head = lax.map(one_head, jnp.arange(HEADS, dtype=jnp.int32))
    joined = per_head.transpose(1, 2, 0, 3).reshape(NB * BLOCK, HEADS * HD)
    product = jnp.dot(joined, out_weight.reshape(HEADS * HD, DOUT), preferred_element_type=jnp.float32)
    return product.astype(jnp.bfloat16).reshape(NB, BLOCK, DOUT)
```

```python
import functools

import jax
import jax.numpy as jnp
import numpy as np
from jax import lax
from jax.experimental import pallas as pl
from jax.experimental.pallas import tpu as pltpu
from jax.sharding import PartitionSpec as P

MESH = pl.DeviceIdType.MESH

KEYS = 28


def strip_tables(heads_local, blocks, slot_total):
    slot_ids = np.arange(slot_total)
    head_of = slot_ids * heads_local // slot_total
    per_head = np.bincount(head_of, minlength=heads_local)
    head_begin = np.cumsum(per_head) - per_head
    order_in_head = slot_ids - head_begin[head_of]
    head_share = per_head[head_of]
    first_block = order_in_head * blocks // head_share
    block_count = (order_in_head + 1) * blocks // head_share - first_block
    return (head_of, first_block, block_count)


def plain_body(queries, key_vectors, value_vectors, block_mask, out_weight):
    rank_count = lax.axis_size("seq")
    my_rank = lax.axis_index("seq")
    block_total, row_share, feature_width = queries.shape
    heads_local = block_mask.shape[0]
    head_size = feature_width // heads_local
    block_rows = row_share * rank_count
    per_rank = (heads_local + rank_count - 1) // rank_count
    slot_total = rank_count * per_rank
    least_share = slot_total // heads_local
    strip_cap = ((block_total + least_share - 1) // least_share + 1) // 2 * 2
    key_cap = min(KEYS, block_total)
    head_of, first_block, block_count = strip_tables(heads_local, block_total, slot_total)
    slot_grid = np.arange(slot_total).reshape(rank_count, per_rank).T
    paired = jnp.concatenate(
        [
            key_vectors.reshape(block_total, row_share, heads_local, head_size),
            value_vectors.reshape(block_total, row_share, heads_local, head_size),
        ],
        axis=3,
    )
    send_heads = jnp.asarray(head_of[slot_grid].reshape(-1), jnp.int32)
    chosen = jnp.take(paired, send_heads, axis=2)
    chosen = chosen.reshape(block_total, row_share, per_rank, rank_count, 2 * head_size)
    outgoing_pairs = chosen.transpose(2, 0, 3, 1, 4).reshape(
        per_rank, block_total, block_rows, 2 * head_size
    )
    flat_queries = queries.reshape(block_total, row_share, heads_local, head_size).transpose(
        0, 2, 1, 3
    )
    flat_queries = flat_queries.reshape(block_total * heads_local, row_share, head_size)
    positions = np.arange(strip_cap)
    unit_block = first_block[slot_grid][:, None, :] + positions[None, :, None]
    is_live = positions[None, :, None] < block_count[slot_grid][:, None, :]
    unit_index = np.where(is_live, unit_block * heads_local + head_of[slot_grid][:, None, :], 0)
    picked = jnp.take(flat_queries, jnp.asarray(unit_index.reshape(-1), jnp.int32), axis=0)
    picked = jnp.where(
        jnp.asarray(is_live.reshape(-1))[:, None, None], picked, jnp.zeros_like(picked)
    )
    outgoing_queries = picked.reshape(per_rank, strip_cap, block_rows, head_size)
    strip_queries, strip_pairs = (
        lax.all_to_all(outgoing_queries, "seq", split_axis=2, concat_axis=2, tiled=True),
        lax.all_to_all(outgoing_pairs, "seq", split_axis=2, concat_axis=2, tiled=True),
    )
    my_slots = my_rank * per_rank + jnp.arange(per_rank, dtype=jnp.int32)
    my_heads = jnp.asarray(head_of, jnp.int32)[my_slots]
    my_first = jnp.asarray(first_block, jnp.int32)[my_slots]
    query_blocks = jnp.minimum(
        my_first[:, None] + jnp.arange(strip_cap, dtype=jnp.int32)[None, :], block_total - 1
    )
    mask_rows = block_mask[my_heads[:, None], query_blocks]
    column_ids = jnp.arange(block_total, dtype=jnp.int32)
    ranking = (1 - mask_rows) * block_total + column_ids
    key_pick = jnp.argsort(ranking, axis=-1)[..., :key_cap]
    key_live = jnp.take_along_axis(mask_rows, key_pick, axis=-1)
    group_total = per_rank * strip_cap // 2
    query_groups = strip_queries.reshape(group_total, 2, block_rows, head_size)
    pick_groups = key_pick.reshape(group_total, 2, key_cap)
    live_groups = key_live.reshape(group_total, 2, key_cap)
    slot_of_group = jnp.arange(group_total, dtype=jnp.int32) // (strip_cap // 2)
    score_scale = head_size ** (-0.5)

    def attend_group(inputs):
        query_tile, pick_tile, live_tile, slot_index = inputs
        pairs_here = strip_pairs[slot_index]
        gathered = pairs_here[pick_tile]
        scores = (
            jnp.einsum(
                "qid,qkjd->qikj",
                query_tile,
                gathered[..., :head_size],
                preferred_element_type=jnp.float32,
            )
            * score_scale
        )
        allowed = (live_tile > 0)[:, None, :, None]
        scores = jnp.where(allowed, scores, -jnp.inf)
        largest = jnp.max(scores, axis=(2, 3), keepdims=True)
        weights = jnp.exp(scores - largest)
        totals = jnp.sum(weights, axis=(2, 3))
        blended = jnp.einsum(
            "qikj,qkjd->qid",
            weights.astype(jnp.bfloat16),
            gathered[..., head_size:],
            preferred_element_type=jnp.float32,
        )
        return (blended / totals[..., None]).astype(jnp.bfloat16)

    strip_out = lax.map(attend_group, (query_groups, pick_groups, live_groups, slot_of_group))
    outgoing_out = strip_out.reshape(per_rank, strip_cap, block_rows, head_size)
    returned = lax.all_to_all(outgoing_out, "seq", split_axis=2, concat_axis=2, tiled=True)
    slot_mesh, step_mesh = np.meshgrid(np.arange(slot_total), positions, indexing="ij")
    live_slot = step_mesh < block_count[slot_mesh]
    placement_index = np.zeros((block_total, heads_local), np.int64)
    source_index = (
        slot_mesh % per_rank * strip_cap + step_mesh
    ) * rank_count + slot_mesh // per_rank
    placement_index[
        first_block[slot_mesh][live_slot] + step_mesh[live_slot], head_of[slot_mesh][live_slot]
    ] = source_index[live_slot]
    flat_back = returned.reshape(per_rank * strip_cap * rank_count, row_share, head_size)
    own_out = jnp.take(flat_back, jnp.asarray(placement_index.reshape(-1), jnp.int32), axis=0)
    own_out = own_out.reshape(block_total, heads_local, row_share, head_size)
    token_total = block_total * row_share
    token_out = own_out.transpose(0, 2, 1, 3).reshape(token_total, heads_local, head_size)
    partial_sum = jnp.einsum(
        "thd,hdo->to",
        token_out,
        lax.all_gather(out_weight, "seq", axis=1, tiled=True),
        preferred_element_type=jnp.float32,
    )
    summed = lax.psum_scatter(
        partial_sum.astype(jnp.bfloat16), "tp", scatter_dimension=1, tiled=True
    ).astype(jnp.float32)
    return summed.astype(jnp.bfloat16).reshape(block_total, row_share, summed.shape[1])


def fused_kernel(
    n,
    q_ref,
    k_ref,
    v_ref,
    mask_ref,
    w_ref,
    out_ref,
    q_buf,
    k_buf,
    v_buf,
    q_ext,
    k_ext,
    v_ext,
    swap,
    o_buf,
    feat,
    w_cat,
    mixed,
    own_sum,
    core_out,
    core_in,
    z_out,
    z_in,
    local_sem,
    main_send,
    main_recv,
    ext_send,
    ext_recv,
    w_send,
    w_recv,
    o_send,
    o_recv,
    x_send,
    x_recv,
    core_send,
    core_recv,
    z_send,
    z_recv,
):
    me = lax.axis_index("seq")
    tp = lax.axis_index("tp")
    heads = mask_ref.shape[0]
    blocks, rows, _ = q_ref.shape
    size = n * rows
    base, extra = heads // n, heads % n
    width = base * size
    share = out_ref.shape[2]
    core = lax.rem(tp, 2)
    chip = lax.div(tp, 2)
    core_mate = tp + 1 - 2 * core
    chip_mate = lax.rem(tp + 2, 4)
    shift = lax.rem(tp * extra, n)
    peers = [lax.rem(me + k, n) for k in range(n)]

    def extra_rank(rank):
        return lax.rem(rank - shift + n, n)

    barrier = pltpu.get_barrier_semaphore()
    for k in range(1, n):
        pl.semaphore_signal(
            barrier, inc=1, device_id={"seq": peers[k]}, device_id_type=MESH
        )
    for mate in (core_mate, chip_mate):
        pl.semaphore_signal(barrier, inc=1, device_id={"tp": mate}, device_id_type=MESH)
    pl.semaphore_wait(barrier, n + 1)

    triples = ((q_ref, q_buf, q_ext), (k_ref, k_buf, k_ext), (v_ref, v_buf, v_ext))

    def main_copy(i, k):
        source, buf, _ = triples[i]
        return pltpu.make_async_remote_copy(
            src_ref=source.at[:, :, pl.ds(pl.multiple_of(peers[k] * width, size), width)],
            dst_ref=buf.at[me],
            send_sem=main_send.at[i, k],
            recv_sem=main_recv.at[i, k],
            device_id={"seq": peers[k]},
            device_id_type=MESH,
        )

    def ext_column(rank):
        return pl.ds(pl.multiple_of((n * base + extra_rank(rank)) * size, size), size)

    def ext_copy(i, k):
        source, _, buf = triples[i]
        return pltpu.make_async_remote_copy(
            src_ref=source.at[:, :, ext_column(peers[k])],
            dst_ref=buf.at[me],
            send_sem=ext_send.at[i, k],
            recv_sem=ext_recv.at[i, k],
            device_id={"seq": peers[k]},
            device_id_type=MESH,
        )

    def ext_recv_wait(i, k):
        _, _, buf = triples[i]
        pltpu.make_async_remote_copy(
            src_ref=buf.at[me],
            dst_ref=buf.at[me],
            send_sem=ext_send.at[i, k],
            recv_sem=ext_recv.at[i, k],
            device_id={"seq": peers[k]},
            device_id_type=MESH,
        ).wait_recv()

    has_extra = extra_rank(me) < extra
    order = sorted(range(1, n), key=lambda k: -min(k, n - k))
    mains = {}
    for i in (1, 0, 2):
        for k in order:
            mains[i, k] = main_copy(i, k)
            mains[i, k].start()
    for i in (1, 0, 2):
        for k in order:

            @pl.when(extra_rank(peers[k]) < extra)
            def _():
                ext_copy(i, k).start()

    def w_columns(to_chip, half):
        which = core if half == 0 else 1 - core
        return pl.ds(pl.multiple_of((to_chip * 2 + which) * share, size), share)

    w_copies = []
    for half in range(2):
        columns = pl.ds(half * share, share)
        w_copies.append(
            pltpu.make_async_remote_copy(
                src_ref=w_ref.at[:, :, w_columns(1 - chip, half)],
                dst_ref=w_cat.at[pl.ds(heads, heads), :, columns],
                send_sem=w_send.at[half],
                recv_sem=w_recv.at[half],
                device_id={"tp": chip_mate},
                device_id_type=MESH,
            )
        )
        w_copies[-1].start()
    locals_main, locals_w = [], []
    for i in range(3):
        source, buf, _ = triples[i]
        locals_main.append(
            pltpu.make_async_copy(
                source.at[:, :, pl.ds(pl.multiple_of(me * width, size), width)],
                buf.at[me],
                local_sem.at[i],
            )
        )
        locals_main[-1].start()

    def local_ext(i):
        source, _, buf = triples[i]
        return pltpu.make_async_copy(
            source.at[:, :, ext_column(me)], buf.at[me], local_sem.at[3 + i]
        )

    @pl.when(has_extra)
    def _():
        for i in range(3):
            local_ext(i).start()

    for half in range(2):
        locals_w.append(
            pltpu.make_async_copy(
                w_ref.at[:, :, w_columns(chip, half)],
                w_cat.at[pl.ds(0, heads), :, pl.ds(half * share, share)],
                local_sem.at[6 + half],
            )
        )
        locals_w[-1].start()

    span = n * size
    row_id = lax.broadcasted_iota(jnp.int32, (span, span), 0)
    col_id = lax.broadcasted_iota(jnp.int32, (span, span), 1)
    outer, inside = lax.div(row_id, size), lax.rem(row_id, size)
    goal = lax.div(inside, rows) * size + outer * rows + lax.rem(inside, rows)
    swap[...] = jnp.where(goal == col_id, 1.0, 0.0).astype(jnp.bfloat16)

    token_total = n * blocks * rows
    key_block = lax.rem(
        lax.div(lax.broadcasted_iota(jnp.int32, (1, token_total), 1), rows), blocks
    )
    rate = float(size ** (-0.5) * np.log2(np.e))

    def attend(qs, ks, vs, lane, head, slot):
        lanes = pl.ds(lane, size)
        keys = ks[:, :, :, lanes].reshape(token_total, size)
        values = vs[:, :, :, lanes].reshape(token_total, size)
        results = []
        for block in range(blocks):
            query = qs[:, block, :, lanes].reshape(n * rows, size)
            scores = lax.dot_general(
                query, keys, (((1,), (1,)), ((), ())), preferred_element_type=jnp.float32
            )
            bias = jnp.zeros((1, token_total), jnp.float32)
            for other in range(blocks):
                off = jnp.where(mask_ref[head, block, other] > 0, 0.0, -jnp.inf)
                bias = jnp.where(key_block == other, off, bias)
            scores = scores + bias
            largest = jnp.max(scores, axis=1, keepdims=True)
            weights = jnp.exp2((scores - largest) * rate)
            totals = jnp.sum(weights, axis=1, keepdims=True)
            blended = jnp.dot(
                weights.astype(jnp.bfloat16), values, preferred_element_type=jnp.float32
            )
            results.append((blended / totals).astype(jnp.bfloat16))
        o_buf[slot] = jnp.dot(
            jnp.concatenate(results, axis=1), swap[...], preferred_element_type=jnp.float32
        ).astype(jnp.bfloat16)

    def o_copy(slot, head, k):
        return pltpu.make_async_remote_copy(
            src_ref=o_buf.at[slot, :, pl.ds(pl.multiple_of(peers[k] * size, size), size)],
            dst_ref=feat.at[head],
            send_sem=o_send.at[slot, k],
            recv_sem=o_recv.at[slot, k],
            device_id={"seq": peers[k]},
            device_id_type=MESH,
        )

    def x_copy(head):
        return pltpu.make_async_remote_copy(
            src_ref=feat.at[head],
            dst_ref=feat.at[heads + head],
            send_sem=x_send.at[head],
            recv_sem=x_recv.at[head],
            device_id={"tp": chip_mate},
            device_id_type=MESH,
        )

    def emit(slot, head):
        for k in order:
            o_copy(slot, head, k).start()
        feat[head] = o_buf[slot, :, pl.ds(pl.multiple_of(me * size, size), size)]
        x_copy(head).start()

    for i in range(3):
        locals_main[i].wait()
        for k in order:
            mains[i, k].wait_recv()
    for j in range(base):
        attend(q_buf, k_buf, v_buf, j * size, me * base + j, j)
        emit(j, me * base + j)

    my_extra = n * base + extra_rank(me)

    @pl.when(has_extra)
    def _():
        for i in range(3):
            local_ext(i).wait()
            for k in order:
                ext_recv_wait(i, k)
        attend(q_ext, k_ext, v_ext, 0, my_extra, base)
        emit(base, my_extra)

    for k in sorted(range(1, n), key=lambda k: min(k, n - k)):
        origin = lax.rem(me + n - k, n)
        for j in range(base):
            o_copy(j, me * base + j, k).wait_recv()
            x_copy(origin * base + j).start()
    for j in range(extra):
        owner = lax.rem(shift + j, n)

        @pl.when(owner != me)
        def _():
            gap = lax.rem(me - owner + n, n)
            pltpu.make_async_remote_copy(
                src_ref=feat.at[n * base + j],
                dst_ref=feat.at[n * base + j],
                send_sem=o_send.at[base, gap],
                recv_sem=o_recv.at[base, gap],
                device_id={"seq": owner},
                device_id_type=MESH,
            ).wait_recv()
            x_copy(n * base + j).start()

    for half in range(2):
        locals_w[half].wait()
        w_copies[half].wait_recv()
    for head in range(heads):
        x_copy(head).wait_recv()
    groups = 2 * heads // n
    for g in range(groups):
        joined = jnp.concatenate([feat[g * n + a] for a in range(n)], axis=1)
        mixed[:, g * span : (g + 1) * span] = jnp.dot(
            joined, swap[...], preferred_element_type=jnp.float32
        ).astype(jnp.bfloat16)

    def core_copy(k):
        return pltpu.make_async_remote_copy(
            src_ref=core_out.at[k],
            dst_ref=core_in.at[k],
            send_sem=core_send.at[k],
            recv_sem=core_recv.at[k],
            device_id={"tp": core_mate},
            device_id_type=MESH,
        )

    def z_copy(k):
        return pltpu.make_async_remote_copy(
            src_ref=z_out.at[k],
            dst_ref=z_in.at[k],
            send_sem=z_send.at[k],
            recv_sem=z_recv.at[k],
            device_id={"seq": peers[k]},
            device_id_type=MESH,
        )

    def finish_core(k):
        core_copy(k).wait_recv()
        joint = own_sum[k] + core_in[k].astype(jnp.float32)
        if k == 0:
            own_sum[0] = joint
        else:
            z_out[k] = joint.astype(jnp.bfloat16)
            z_copy(k).start()

    depth = 2 * heads * rows
    tokens = blocks * rows
    steps = order + [0]
    for place, k in enumerate(steps):
        row = pl.ds(pl.multiple_of(peers[k] * rows, rows), rows)
        taken = jnp.concatenate(
            [
                jnp.concatenate(
                    [
                        mixed[row, g * span + b * size : g * span + (b + 1) * size]
                        for g in range(groups)
                    ],
                    axis=1,
                )
                for b in range(blocks)
            ],
            axis=0,
        )
        core_out[k] = jnp.dot(
            taken,
            w_cat[:, :, share:].reshape(depth, share),
            preferred_element_type=jnp.float32,
        ).astype(jnp.bfloat16)
        core_copy(k).start()
        own_sum[k] = jnp.dot(
            taken,
            w_cat[:, :, :share].reshape(depth, share),
            preferred_element_type=jnp.float32,
        )
        if place >= 1:
            finish_core(steps[place - 1])
    finish_core(0)
    result = own_sum[0]
    for k in sorted(range(1, n), key=lambda k: min(k, n - k)):
        z_copy(k).wait_recv()
        result = result + z_in[k].astype(jnp.float32)
    out_ref[...] = result.astype(jnp.bfloat16).reshape(blocks, rows, share)

    for k in order:
        for i in range(3):
            mains[i, k].wait_send()

            @pl.when(extra_rank(peers[k]) < extra)
            def _():
                ext_copy(i, k).wait_send()

        for j in range(base):
            o_copy(j, me * base + j, k).wait_send()

        @pl.when(has_extra)
        def _():
            o_copy(base, my_extra, k).wait_send()

        z_copy(k).wait_send()
    for half in range(2):
        w_copies[half].wait_send()
    for head in range(heads):
        x_copy(head).wait_send()
    for k in range(n):
        core_copy(k).wait_send()


def fused_body(queries, key_vectors, value_vectors, block_mask, out_weight):
    n = lax.axis_size("seq")
    blocks, rows, _ = queries.shape
    heads = block_mask.shape[0]
    size = n * rows
    base = heads // n
    share = out_weight.shape[2] // lax.axis_size("tp")
    kind = jnp.bfloat16
    dma = pltpu.SemaphoreType.DMA
    whole = pl.BlockSpec(memory_space=pl.ANY)
    return pl.pallas_call(
        functools.partial(fused_kernel, n),
        out_shape=jax.ShapeDtypeStruct((blocks, rows, share), kind),
        in_specs=[whole, whole, whole, pl.BlockSpec(memory_space=pltpu.SMEM), whole],
        out_specs=pl.BlockSpec(memory_space=pltpu.VMEM),
        scratch_shapes=[pltpu.VMEM((n, blocks, rows, base * size), kind)] * 3
        + [pltpu.VMEM((n, blocks, rows, size), kind)] * 3
        + [
            pltpu.VMEM((n * size, n * size), kind),
            pltpu.VMEM((base + 1, size, n * size), kind),
            pltpu.VMEM((2 * heads, size, size), kind),
            pltpu.VMEM((2 * heads, rows, 2 * share), kind),
            pltpu.VMEM((size, 2 * heads * size), kind),
            pltpu.VMEM((n, blocks * rows, share), jnp.float32),
        ]
        + [pltpu.VMEM((n, blocks * rows, share), kind)] * 4
        + [dma((8,))]
        + [dma((3, n))] * 4
        + [dma((2,))] * 2
        + [dma((base + 1, n))] * 2
        + [dma((heads,))] * 2
        + [dma((n,))] * 4,
        compiler_params=pltpu.CompilerParams(
            collective_id=0, has_side_effects=True, vmem_limit_bytes=40 * 1024 * 1024
        ),
    )(queries, key_vectors, value_vectors, block_mask, out_weight)


def body(queries, key_vectors, value_vectors, block_mask, out_weight):
    n, tp = lax.axis_size("seq"), lax.axis_size("tp")
    blocks, rows, features = queries.shape
    heads = block_mask.shape[0]
    size = features // heads
    share = out_weight.shape[2] // tp
    fits = (
        n > 1
        and tp // 2 == 2
        and tp % 2 == 0
        and blocks == n
        and rows % 16 == 0
        and size == n * rows
        and size % 128 == 0
        and share % size == 0
        and heads // n > 0
        and 2 * heads % n == 0
    )
    if fits:
        return fused_body(queries, key_vectors, value_vectors, block_mask, out_weight)
    return plain_body(queries, key_vectors, value_vectors, block_mask, out_weight)


def solution(mesh):
    return jax.shard_map(
        body,
        mesh=mesh,
        in_specs=(
            P("groups", "seq", "tp"),
            P("groups", "seq", "tp"),
            P("groups", "seq", "tp"),
            P("tp", None, None),
            P("tp", "seq", None),
        ),
        out_specs=P("groups", "seq", "tp"),
        check_vma=False,
    )
```

```python
import functools

import jax
import jax.numpy as jnp
import numpy as np
from jax import lax
from jax.experimental import pallas as pl
from jax.experimental.pallas import tpu as pltpu
from jax.sharding import PartitionSpec as P

MESH = pl.DeviceIdType.MESH

KEYS = 28


def strip_tables(heads_local, blocks, slot_total):
    slot_ids = np.arange(slot_total)
    head_of = slot_ids * heads_local // slot_total
    per_head = np.bincount(head_of, minlength=heads_local)
    head_begin = np.cumsum(per_head) - per_head
    order_in_head = slot_ids - head_begin[head_of]
    head_share = per_head[head_of]
    first_block = order_in_head * blocks // head_share
    block_count = (order_in_head + 1) * blocks // head_share - first_block
    return (head_of, first_block, block_count)


def plain_body(queries, key_vectors, value_vectors, block_mask, out_weight):
    rank_count = lax.axis_size("seq")
    my_rank = lax.axis_index("seq")
    block_total, row_share, feature_width = queries.shape
    heads_local = block_mask.shape[0]
    head_size = feature_width // heads_local
    block_rows = row_share * rank_count
    per_rank = (heads_local + rank_count - 1) // rank_count
    slot_total = rank_count * per_rank
    least_share = slot_total // heads_local
    strip_cap = ((block_total + least_share - 1) // least_share + 1) // 2 * 2
    key_cap = min(KEYS, block_total)
    head_of, first_block, block_count = strip_tables(heads_local, block_total, slot_total)
    slot_grid = np.arange(slot_total).reshape(rank_count, per_rank).T
    paired = jnp.concatenate(
        [
            key_vectors.reshape(block_total, row_share, heads_local, head_size),
            value_vectors.reshape(block_total, row_share, heads_local, head_size),
        ],
        axis=3,
    )
    send_heads = jnp.asarray(head_of[slot_grid].reshape(-1), jnp.int32)
    chosen = jnp.take(paired, send_heads, axis=2)
    chosen = chosen.reshape(block_total, row_share, per_rank, rank_count, 2 * head_size)
    outgoing_pairs = chosen.transpose(2, 0, 3, 1, 4).reshape(
        per_rank, block_total, block_rows, 2 * head_size
    )
    flat_queries = queries.reshape(block_total, row_share, heads_local, head_size).transpose(
        0, 2, 1, 3
    )
    flat_queries = flat_queries.reshape(block_total * heads_local, row_share, head_size)
    positions = np.arange(strip_cap)
    unit_block = first_block[slot_grid][:, None, :] + positions[None, :, None]
    is_live = positions[None, :, None] < block_count[slot_grid][:, None, :]
    unit_index = np.where(is_live, unit_block * heads_local + head_of[slot_grid][:, None, :], 0)
    picked = jnp.take(flat_queries, jnp.asarray(unit_index.reshape(-1), jnp.int32), axis=0)
    picked = jnp.where(
        jnp.asarray(is_live.reshape(-1))[:, None, None], picked, jnp.zeros_like(picked)
    )
    outgoing_queries = picked.reshape(per_rank, strip_cap, block_rows, head_size)
    strip_queries, strip_pairs = (
        lax.all_to_all(outgoing_queries, "seq", split_axis=2, concat_axis=2, tiled=True),
        lax.all_to_all(outgoing_pairs, "seq", split_axis=2, concat_axis=2, tiled=True),
    )
    my_slots = my_rank * per_rank + jnp.arange(per_rank, dtype=jnp.int32)
    my_heads = jnp.asarray(head_of, jnp.int32)[my_slots]
    my_first = jnp.asarray(first_block, jnp.int32)[my_slots]
    query_blocks = jnp.minimum(
        my_first[:, None] + jnp.arange(strip_cap, dtype=jnp.int32)[None, :], block_total - 1
    )
    mask_rows = block_mask[my_heads[:, None], query_blocks]
    column_ids = jnp.arange(block_total, dtype=jnp.int32)
    ranking = (1 - mask_rows) * block_total + column_ids
    key_pick = jnp.argsort(ranking, axis=-1)[..., :key_cap]
    key_live = jnp.take_along_axis(mask_rows, key_pick, axis=-1)
    group_total = per_rank * strip_cap // 2
    query_groups = strip_queries.reshape(group_total, 2, block_rows, head_size)
    pick_groups = key_pick.reshape(group_total, 2, key_cap)
    live_groups = key_live.reshape(group_total, 2, key_cap)
    slot_of_group = jnp.arange(group_total, dtype=jnp.int32) // (strip_cap // 2)
    score_scale = head_size ** (-0.5)

    def attend_group(inputs):
        query_tile, pick_tile, live_tile, slot_index = inputs
        pairs_here = strip_pairs[slot_index]
        gathered = pairs_here[pick_tile]
        scores = (
            jnp.einsum(
                "qid,qkjd->qikj",
                query_tile,
                gathered[..., :head_size],
                preferred_element_type=jnp.float32,
            )
            * score_scale
        )
        allowed = (live_tile > 0)[:, None, :, None]
        scores = jnp.where(allowed, scores, -jnp.inf)
        largest = jnp.max(scores, axis=(2, 3), keepdims=True)
        weights = jnp.exp(scores - largest)
        totals = jnp.sum(weights, axis=(2, 3))
        blended = jnp.einsum(
            "qikj,qkjd->qid",
            weights.astype(jnp.bfloat16),
            gathered[..., head_size:],
            preferred_element_type=jnp.float32,
        )
        return (blended / totals[..., None]).astype(jnp.bfloat16)

    strip_out = lax.map(attend_group, (query_groups, pick_groups, live_groups, slot_of_group))
    outgoing_out = strip_out.reshape(per_rank, strip_cap, block_rows, head_size)
    returned = lax.all_to_all(outgoing_out, "seq", split_axis=2, concat_axis=2, tiled=True)
    slot_mesh, step_mesh = np.meshgrid(np.arange(slot_total), positions, indexing="ij")
    live_slot = step_mesh < block_count[slot_mesh]
    placement_index = np.zeros((block_total, heads_local), np.int64)
    source_index = (
        slot_mesh % per_rank * strip_cap + step_mesh
    ) * rank_count + slot_mesh // per_rank
    placement_index[
        first_block[slot_mesh][live_slot] + step_mesh[live_slot], head_of[slot_mesh][live_slot]
    ] = source_index[live_slot]
    flat_back = returned.reshape(per_rank * strip_cap * rank_count, row_share, head_size)
    own_out = jnp.take(flat_back, jnp.asarray(placement_index.reshape(-1), jnp.int32), axis=0)
    own_out = own_out.reshape(block_total, heads_local, row_share, head_size)
    token_total = block_total * row_share
    token_out = own_out.transpose(0, 2, 1, 3).reshape(token_total, heads_local, head_size)
    partial_sum = jnp.einsum(
        "thd,hdo->to",
        token_out,
        lax.all_gather(out_weight, "seq", axis=1, tiled=True),
        preferred_element_type=jnp.float32,
    )
    summed = lax.psum_scatter(
        partial_sum.astype(jnp.bfloat16), "tp", scatter_dimension=1, tiled=True
    ).astype(jnp.float32)
    return summed.astype(jnp.bfloat16).reshape(block_total, row_share, summed.shape[1])


def fused_kernel(
    n,
    q_ref,
    k_ref,
    v_ref,
    mask_ref,
    w_ref,
    out_ref,
    q_buf,
    k_buf,
    v_buf,
    q_ext,
    k_ext,
    v_ext,
    swap,
    o_buf,
    feat,
    w_cat,
    mixed,
    own_sum,
    core_out,
    core_in,
    z_out,
    z_in,
    local_sem,
    main_send,
    main_recv,
    ext_send,
    ext_recv,
    w_send,
    w_recv,
    o_send,
    o_recv,
    x_send,
    x_recv,
    core_send,
    core_recv,
    z_send,
    z_recv,
):
    me = lax.axis_index("seq")
    tp = lax.axis_index("tp")
    heads = w_ref.shape[0]
    blocks, rows, _ = q_ref.shape
    size = n * rows
    base, extra = heads // n, heads % n
    width = base * size
    share = out_ref.shape[2]
    core = lax.rem(tp, 2)
    chip = lax.div(tp, 2)
    core_mate = tp + 1 - 2 * core
    chip_mate = lax.rem(tp + 2, 4)
    shift = lax.rem(tp * extra, n)
    peers = [lax.rem(me + k, n) for k in range(n)]

    def extra_rank(rank):
        return lax.rem(rank - shift + n, n)

    barrier = pltpu.get_barrier_semaphore()
    for k in range(1, n):
        pl.semaphore_signal(
            barrier, inc=1, device_id={"seq": peers[k]}, device_id_type=MESH
        )
    for mate in (core_mate, chip_mate):
        pl.semaphore_signal(barrier, inc=1, device_id={"tp": mate}, device_id_type=MESH)
    pl.semaphore_wait(barrier, n + 1)

    triples = ((q_ref, q_buf, q_ext), (k_ref, k_buf, k_ext), (v_ref, v_buf, v_ext))

    def main_copy(i, k):
        source, buf, _ = triples[i]
        return pltpu.make_async_remote_copy(
            src_ref=source.at[:, :, pl.ds(pl.multiple_of(peers[k] * width, size), width)],
            dst_ref=buf.at[me],
            send_sem=main_send.at[i, k],
            recv_sem=main_recv.at[i, k],
            device_id={"seq": peers[k]},
            device_id_type=MESH,
        )

    def ext_column(rank):
        return pl.ds(pl.multiple_of((n * base + extra_rank(rank)) * size, size), size)

    def ext_copy(i, k):
        source, _, buf = triples[i]
        return pltpu.make_async_remote_copy(
            src_ref=source.at[:, :, ext_column(peers[k])],
            dst_ref=buf.at[me],
            send_sem=ext_send.at[i, k],
            recv_sem=ext_recv.at[i, k],
            device_id={"seq": peers[k]},
            device_id_type=MESH,
        )

    def ext_recv_wait(i, k):
        _, _, buf = triples[i]
        pltpu.make_async_remote_copy(
            src_ref=buf.at[me],
            dst_ref=buf.at[me],
            send_sem=ext_send.at[i, k],
            recv_sem=ext_recv.at[i, k],
            device_id={"seq": peers[k]},
            device_id_type=MESH,
        ).wait_recv()

    has_extra = extra_rank(me) < extra
    order = sorted(range(1, n), key=lambda k: -min(k, n - k))
    mains = {}
    for i in (1, 0, 2):
        for k in order:
            mains[i, k] = main_copy(i, k)
            mains[i, k].start()
    for i in (1, 0, 2):
        for k in order:

            @pl.when(extra_rank(peers[k]) < extra)
            def _():
                ext_copy(i, k).start()

    def w_columns(to_chip, half):
        which = core if half == 0 else 1 - core
        return pl.ds(pl.multiple_of((to_chip * 2 + which) * share, size), share)

    w_copies = []
    for half in range(2):
        columns = pl.ds(half * share, share)
        w_copies.append(
            pltpu.make_async_remote_copy(
                src_ref=w_ref.at[:, :, w_columns(1 - chip, half)],
                dst_ref=w_cat.at[pl.ds(heads, heads), :, columns],
                send_sem=w_send.at[half],
                recv_sem=w_recv.at[half],
                device_id={"tp": chip_mate},
                device_id_type=MESH,
            )
        )
        w_copies[-1].start()
    locals_main, locals_w = [], []
    for i in range(3):
        source, buf, _ = triples[i]
        locals_main.append(
            pltpu.make_async_copy(
                source.at[:, :, pl.ds(pl.multiple_of(me * width, size), width)],
                buf.at[me],
                local_sem.at[i],
            )
        )
        locals_main[-1].start()

    def local_ext(i):
        source, _, buf = triples[i]
        return pltpu.make_async_copy(
            source.at[:, :, ext_column(me)], buf.at[me], local_sem.at[3 + i]
        )

    @pl.when(has_extra)
    def _():
        for i in range(3):
            local_ext(i).start()

    for half in range(2):
        locals_w.append(
            pltpu.make_async_copy(
                w_ref.at[:, :, w_columns(chip, half)],
                w_cat.at[pl.ds(0, heads), :, pl.ds(half * share, share)],
                local_sem.at[6 + half],
            )
        )
        locals_w[-1].start()

    span = n * size
    row_id = lax.broadcasted_iota(jnp.int32, (span, span), 0)
    col_id = lax.broadcasted_iota(jnp.int32, (span, span), 1)
    outer, inside = lax.div(row_id, size), lax.rem(row_id, size)
    goal = lax.div(inside, rows) * size + outer * rows + lax.rem(inside, rows)
    swap[...] = jnp.where(goal == col_id, 1.0, 0.0).astype(jnp.bfloat16)

    token_total = n * blocks * rows
    key_block = lax.rem(
        lax.div(lax.broadcasted_iota(jnp.int32, (1, token_total), 1), rows), blocks
    )
    rate = float(size ** (-0.5) * np.log2(np.e))

    def attend(qs, ks, vs, lane, head, slot):
        lanes = pl.ds(lane, size)
        keys = ks[:, :, :, lanes].reshape(token_total, size)
        values = vs[:, :, :, lanes].reshape(token_total, size)
        results = []
        is_head = lax.broadcasted_iota(jnp.int32, mask_ref.shape, 2) == head
        live = jnp.where(is_head, mask_ref[...], 0).astype(jnp.float32)
        live = jnp.sum(live, axis=2, keepdims=True)
        allowed = jnp.zeros((blocks, token_total), jnp.float32)
        for other in range(blocks):
            allowed = jnp.where(key_block == other, live[:, other, :], allowed)
        bias = jnp.where(allowed > 0.5, 0.0, -jnp.inf)
        for block in range(blocks):
            query = qs[:, block, :, lanes].reshape(n * rows, size)
            scores = lax.dot_general(
                query, keys, (((1,), (1,)), ((), ())), preferred_element_type=jnp.float32
            )
            scores = scores + bias[block : block + 1, :]
            largest = jnp.max(scores, axis=1, keepdims=True)
            weights = jnp.exp2((scores - largest) * rate)
            totals = jnp.sum(weights, axis=1, keepdims=True)
            blended = jnp.dot(
                weights.astype(jnp.bfloat16), values, preferred_element_type=jnp.float32
            )
            results.append((blended / totals).astype(jnp.bfloat16))
        o_buf[slot] = jnp.dot(
            jnp.concatenate(results, axis=1), swap[...], preferred_element_type=jnp.float32
        ).astype(jnp.bfloat16)

    def o_copy(slot, head, k):
        return pltpu.make_async_remote_copy(
            src_ref=o_buf.at[slot, :, pl.ds(pl.multiple_of(peers[k] * size, size), size)],
            dst_ref=feat.at[head],
            send_sem=o_send.at[slot, k],
            recv_sem=o_recv.at[slot, k],
            device_id={"seq": peers[k]},
            device_id_type=MESH,
        )

    def x_copy(head):
        return pltpu.make_async_remote_copy(
            src_ref=feat.at[head],
            dst_ref=feat.at[heads + head],
            send_sem=x_send.at[head],
            recv_sem=x_recv.at[head],
            device_id={"tp": chip_mate},
            device_id_type=MESH,
        )

    def emit(slot, head):
        for k in order:
            o_copy(slot, head, k).start()
        feat[head] = o_buf[slot, :, pl.ds(pl.multiple_of(me * size, size), size)]
        x_copy(head).start()

    for i in range(3):
        locals_main[i].wait()
        for k in order:
            mains[i, k].wait_recv()
    for j in range(base):
        attend(q_buf, k_buf, v_buf, j * size, me * base + j, j)
        emit(j, me * base + j)

    my_extra = n * base + extra_rank(me)

    @pl.when(has_extra)
    def _():
        for i in range(3):
            local_ext(i).wait()
            for k in order:
                ext_recv_wait(i, k)
        attend(q_ext, k_ext, v_ext, 0, my_extra, base)
        emit(base, my_extra)

    for k in sorted(range(1, n), key=lambda k: min(k, n - k)):
        origin = lax.rem(me + n - k, n)
        for j in range(base):
            o_copy(j, me * base + j, k).wait_recv()
            x_copy(origin * base + j).start()
    for j in range(extra):
        owner = lax.rem(shift + j, n)

        @pl.when(owner != me)
        def _():
            gap = lax.rem(me - owner + n, n)
            pltpu.make_async_remote_copy(
                src_ref=feat.at[n * base + j],
                dst_ref=feat.at[n * base + j],
                send_sem=o_send.at[base, gap],
                recv_sem=o_recv.at[base, gap],
                device_id={"seq": owner},
                device_id_type=MESH,
            ).wait_recv()
            x_copy(n * base + j).start()

    for half in range(2):
        locals_w[half].wait()
        w_copies[half].wait_recv()
    for head in range(heads):
        x_copy(head).wait_recv()
    groups = 2 * heads // n
    for g in range(groups):
        joined = jnp.concatenate([feat[g * n + a] for a in range(n)], axis=1)
        mixed[:, g * span : (g + 1) * span] = jnp.dot(
            joined, swap[...], preferred_element_type=jnp.float32
        ).astype(jnp.bfloat16)

    def core_copy(k):
        return pltpu.make_async_remote_copy(
            src_ref=core_out.at[k],
            dst_ref=core_in.at[k],
            send_sem=core_send.at[k],
            recv_sem=core_recv.at[k],
            device_id={"tp": core_mate},
            device_id_type=MESH,
        )

    def z_copy(k):
        return pltpu.make_async_remote_copy(
            src_ref=z_out.at[k],
            dst_ref=z_in.at[k],
            send_sem=z_send.at[k],
            recv_sem=z_recv.at[k],
            device_id={"seq": peers[k]},
            device_id_type=MESH,
        )

    def finish_core(k):
        core_copy(k).wait_recv()
        joint = own_sum[k] + core_in[k].astype(jnp.float32)
        if k == 0:
            own_sum[0] = joint
        else:
            z_out[k] = joint.astype(jnp.bfloat16)
            z_copy(k).start()

    depth = 2 * heads * rows
    tokens = blocks * rows
    steps = order + [0]
    for place, k in enumerate(steps):
        row = pl.ds(pl.multiple_of(peers[k] * rows, rows), rows)
        taken = jnp.concatenate(
            [
                jnp.concatenate(
                    [
                        mixed[row, g * span + b * size : g * span + (b + 1) * size]
                        for g in range(groups)
                    ],
                    axis=1,
                )
                for b in range(blocks)
            ],
            axis=0,
        )
        core_out[k] = jnp.dot(
            taken,
            w_cat[:, :, share:].reshape(depth, share),
            preferred_element_type=jnp.float32,
        ).astype(jnp.bfloat16)
        core_copy(k).start()
        own_sum[k] = jnp.dot(
            taken,
            w_cat[:, :, :share].reshape(depth, share),
            preferred_element_type=jnp.float32,
        )
        if place >= 1:
            finish_core(steps[place - 1])
    finish_core(0)
    result = own_sum[0]
    for k in sorted(range(1, n), key=lambda k: min(k, n - k)):
        z_copy(k).wait_recv()
        result = result + z_in[k].astype(jnp.float32)
    out_ref[...] = result.astype(jnp.bfloat16).reshape(blocks, rows, share)

    for k in order:
        for i in range(3):
            mains[i, k].wait_send()

            @pl.when(extra_rank(peers[k]) < extra)
            def _():
                ext_copy(i, k).wait_send()

        for j in range(base):
            o_copy(j, me * base + j, k).wait_send()

        @pl.when(has_extra)
        def _():
            o_copy(base, my_extra, k).wait_send()

        z_copy(k).wait_send()
    for half in range(2):
        w_copies[half].wait_send()
    for head in range(heads):
        x_copy(head).wait_send()
    for k in range(n):
        core_copy(k).wait_send()


def fused_body(queries, key_vectors, value_vectors, block_mask, out_weight):
    n = lax.axis_size("seq")
    blocks, rows, _ = queries.shape
    heads = block_mask.shape[0]
    size = n * rows
    base = heads // n
    share = out_weight.shape[2] // lax.axis_size("tp")
    kind = jnp.bfloat16
    dma = pltpu.SemaphoreType.DMA
    whole = pl.BlockSpec(memory_space=pl.ANY)
    return pl.pallas_call(
        functools.partial(fused_kernel, n),
        out_shape=jax.ShapeDtypeStruct((blocks, rows, share), kind),
        in_specs=[whole, whole, whole, pl.BlockSpec(memory_space=pltpu.VMEM), whole],
        out_specs=pl.BlockSpec(memory_space=pltpu.VMEM),
        scratch_shapes=[pltpu.VMEM((n, blocks, rows, base * size), kind)] * 3
        + [pltpu.VMEM((n, blocks, rows, size), kind)] * 3
        + [
            pltpu.VMEM((n * size, n * size), kind),
            pltpu.VMEM((base + 1, size, n * size), kind),
            pltpu.VMEM((2 * heads, size, size), kind),
            pltpu.VMEM((2 * heads, rows, 2 * share), kind),
            pltpu.VMEM((size, 2 * heads * size), kind),
            pltpu.VMEM((n, blocks * rows, share), jnp.float32),
        ]
        + [pltpu.VMEM((n, blocks * rows, share), kind)] * 4
        + [dma((8,))]
        + [dma((3, n))] * 4
        + [dma((2,))] * 2
        + [dma((base + 1, n))] * 2
        + [dma((heads,))] * 2
        + [dma((n,))] * 4,
        compiler_params=pltpu.CompilerParams(
            collective_id=0, has_side_effects=True, vmem_limit_bytes=60 * 1024 * 1024
        ),
    )(queries, key_vectors, value_vectors, block_mask.transpose(1, 2, 0), out_weight)


def body(queries, key_vectors, value_vectors, block_mask, out_weight):
    n, tp = lax.axis_size("seq"), lax.axis_size("tp")
    blocks, rows, features = queries.shape
    heads = block_mask.shape[0]
    size = features // heads
    share = out_weight.shape[2] // tp
    fits = (
        n > 1
        and tp // 2 == 2
        and tp % 2 == 0
        and blocks == n
        and rows % 16 == 0
        and size == n * rows
        and size % 128 == 0
        and share % size == 0
        and heads // n > 0
        and 2 * heads % n == 0
    )
    if fits:
        return fused_body(queries, key_vectors, value_vectors, block_mask, out_weight)
    return plain_body(queries, key_vectors, value_vectors, block_mask, out_weight)


def solution(mesh):
    return jax.shard_map(
        body,
        mesh=mesh,
        in_specs=(
            P("groups", "seq", "tp"),
            P("groups", "seq", "tp"),
            P("groups", "seq", "tp"),
            P("tp", None, None),
            P("tp", "seq", None),
        ),
        out_specs=P("groups", "seq", "tp"),
        check_vma=False,
    )
```

```python
import functools

import jax
import jax.numpy as jnp
import numpy as np
from jax import lax
from jax.experimental import pallas as pl
from jax.experimental.pallas import tpu as pltpu
from jax.sharding import PartitionSpec as P

MESH = pl.DeviceIdType.MESH

KEYS = 28


def strip_tables(heads_local, blocks, slot_total):
    slot_ids = np.arange(slot_total)
    head_of = slot_ids * heads_local // slot_total
    per_head = np.bincount(head_of, minlength=heads_local)
    head_begin = np.cumsum(per_head) - per_head
    order_in_head = slot_ids - head_begin[head_of]
    head_share = per_head[head_of]
    first_block = order_in_head * blocks // head_share
    block_count = (order_in_head + 1) * blocks // head_share - first_block
    return (head_of, first_block, block_count)


def plain_body(queries, key_vectors, value_vectors, block_mask, out_weight):
    rank_count = lax.axis_size("seq")
    my_rank = lax.axis_index("seq")
    block_total, row_share, feature_width = queries.shape
    heads_local = block_mask.shape[0]
    head_size = feature_width // heads_local
    block_rows = row_share * rank_count
    per_rank = (heads_local + rank_count - 1) // rank_count
    slot_total = rank_count * per_rank
    least_share = slot_total // heads_local
    strip_cap = ((block_total + least_share - 1) // least_share + 1) // 2 * 2
    key_cap = min(KEYS, block_total)
    head_of, first_block, block_count = strip_tables(heads_local, block_total, slot_total)
    slot_grid = np.arange(slot_total).reshape(rank_count, per_rank).T
    paired = jnp.concatenate(
        [
            key_vectors.reshape(block_total, row_share, heads_local, head_size),
            value_vectors.reshape(block_total, row_share, heads_local, head_size),
        ],
        axis=3,
    )
    send_heads = jnp.asarray(head_of[slot_grid].reshape(-1), jnp.int32)
    chosen = jnp.take(paired, send_heads, axis=2)
    chosen = chosen.reshape(block_total, row_share, per_rank, rank_count, 2 * head_size)
    outgoing_pairs = chosen.transpose(2, 0, 3, 1, 4).reshape(
        per_rank, block_total, block_rows, 2 * head_size
    )
    flat_queries = queries.reshape(block_total, row_share, heads_local, head_size).transpose(
        0, 2, 1, 3
    )
    flat_queries = flat_queries.reshape(block_total * heads_local, row_share, head_size)
    positions = np.arange(strip_cap)
    unit_block = first_block[slot_grid][:, None, :] + positions[None, :, None]
    is_live = positions[None, :, None] < block_count[slot_grid][:, None, :]
    unit_index = np.where(is_live, unit_block * heads_local + head_of[slot_grid][:, None, :], 0)
    picked = jnp.take(flat_queries, jnp.asarray(unit_index.reshape(-1), jnp.int32), axis=0)
    picked = jnp.where(
        jnp.asarray(is_live.reshape(-1))[:, None, None], picked, jnp.zeros_like(picked)
    )
    outgoing_queries = picked.reshape(per_rank, strip_cap, block_rows, head_size)
    strip_queries, strip_pairs = (
        lax.all_to_all(outgoing_queries, "seq", split_axis=2, concat_axis=2, tiled=True),
        lax.all_to_all(outgoing_pairs, "seq", split_axis=2, concat_axis=2, tiled=True),
    )
    my_slots = my_rank * per_rank + jnp.arange(per_rank, dtype=jnp.int32)
    my_heads = jnp.asarray(head_of, jnp.int32)[my_slots]
    my_first = jnp.asarray(first_block, jnp.int32)[my_slots]
    query_blocks = jnp.minimum(
        my_first[:, None] + jnp.arange(strip_cap, dtype=jnp.int32)[None, :], block_total - 1
    )
    mask_rows = block_mask[my_heads[:, None], query_blocks]
    column_ids = jnp.arange(block_total, dtype=jnp.int32)
    ranking = (1 - mask_rows) * block_total + column_ids
    key_pick = jnp.argsort(ranking, axis=-1)[..., :key_cap]
    key_live = jnp.take_along_axis(mask_rows, key_pick, axis=-1)
    group_total = per_rank * strip_cap // 2
    query_groups = strip_queries.reshape(group_total, 2, block_rows, head_size)
    pick_groups = key_pick.reshape(group_total, 2, key_cap)
    live_groups = key_live.reshape(group_total, 2, key_cap)
    slot_of_group = jnp.arange(group_total, dtype=jnp.int32) // (strip_cap // 2)
    score_scale = head_size ** (-0.5)

    def attend_group(inputs):
        query_tile, pick_tile, live_tile, slot_index = inputs
        pairs_here = strip_pairs[slot_index]
        gathered = pairs_here[pick_tile]
        scores = (
            jnp.einsum(
                "qid,qkjd->qikj",
                query_tile,
                gathered[..., :head_size],
                preferred_element_type=jnp.float32,
            )
            * score_scale
        )
        allowed = (live_tile > 0)[:, None, :, None]
        scores = jnp.where(allowed, scores, -jnp.inf)
        largest = jnp.max(scores, axis=(2, 3), keepdims=True)
        weights = jnp.exp(scores - largest)
        totals = jnp.sum(weights, axis=(2, 3))
        blended = jnp.einsum(
            "qikj,qkjd->qid",
            weights.astype(jnp.bfloat16),
            gathered[..., head_size:],
            preferred_element_type=jnp.float32,
        )
        return (blended / totals[..., None]).astype(jnp.bfloat16)

    strip_out = lax.map(attend_group, (query_groups, pick_groups, live_groups, slot_of_group))
    outgoing_out = strip_out.reshape(per_rank, strip_cap, block_rows, head_size)
    returned = lax.all_to_all(outgoing_out, "seq", split_axis=2, concat_axis=2, tiled=True)
    slot_mesh, step_mesh = np.meshgrid(np.arange(slot_total), positions, indexing="ij")
    live_slot = step_mesh < block_count[slot_mesh]
    placement_index = np.zeros((block_total, heads_local), np.int64)
    source_index = (
        slot_mesh % per_rank * strip_cap + step_mesh
    ) * rank_count + slot_mesh // per_rank
    placement_index[
        first_block[slot_mesh][live_slot] + step_mesh[live_slot], head_of[slot_mesh][live_slot]
    ] = source_index[live_slot]
    flat_back = returned.reshape(per_rank * strip_cap * rank_count, row_share, head_size)
    own_out = jnp.take(flat_back, jnp.asarray(placement_index.reshape(-1), jnp.int32), axis=0)
    own_out = own_out.reshape(block_total, heads_local, row_share, head_size)
    token_total = block_total * row_share
    token_out = own_out.transpose(0, 2, 1, 3).reshape(token_total, heads_local, head_size)
    partial_sum = jnp.einsum(
        "thd,hdo->to",
        token_out,
        lax.all_gather(out_weight, "seq", axis=1, tiled=True),
        preferred_element_type=jnp.float32,
    )
    summed = lax.psum_scatter(
        partial_sum.astype(jnp.bfloat16), "tp", scatter_dimension=1, tiled=True
    ).astype(jnp.float32)
    return summed.astype(jnp.bfloat16).reshape(block_total, row_share, summed.shape[1])


def fused_kernel(
    n,
    q_ref,
    k_ref,
    v_ref,
    mask_ref,
    w_ref,
    out_ref,
    q_buf,
    k_buf,
    v_buf,
    q_ext,
    k_ext,
    v_ext,
    swap,
    o_buf,
    o_ext,
    feat,
    w_cat,
    mixed,
    own_sum,
    total,
    core_out,
    core_in,
    z_out,
    z_in,
    local_sem,
    main_send,
    main_recv,
    ext_send,
    ext_recv,
    w_send,
    w_recv,
    o_send,
    o_recv,
    oe_send,
    oe_recv,
    x_send,
    x_recv,
    xe_send,
    xe_recv,
    core_send,
    core_recv,
    z_send,
    z_recv,
):
    me = lax.axis_index("seq")
    tp = lax.axis_index("tp")
    heads = w_ref.shape[0]
    blocks, rows, _ = q_ref.shape
    size = n * rows
    base, extra = heads // n, heads % n
    width = base * size
    share = out_ref.shape[2]
    core = lax.rem(tp, 2)
    chip = lax.div(tp, 2)
    core_mate = tp + 1 - 2 * core
    chip_mate = lax.rem(tp + 2, 4)
    shift = lax.rem(tp * extra, n)
    peers = [lax.rem(me + k, n) for k in range(n)]

    def extra_rank(rank):
        return lax.rem(rank - shift + n, n)

    barrier = pltpu.get_barrier_semaphore()
    for k in range(1, n):
        pl.semaphore_signal(
            barrier, inc=1, device_id={"seq": peers[k]}, device_id_type=MESH
        )
    for mate in (core_mate, chip_mate):
        pl.semaphore_signal(barrier, inc=1, device_id={"tp": mate}, device_id_type=MESH)
    pl.semaphore_wait(barrier, n + 1)

    triples = ((q_ref, q_buf, q_ext), (k_ref, k_buf, k_ext), (v_ref, v_buf, v_ext))

    def main_copy(i, k):
        source, buf, _ = triples[i]
        return pltpu.make_async_remote_copy(
            src_ref=source.at[:, :, pl.ds(pl.multiple_of(peers[k] * width, size), width)],
            dst_ref=buf.at[me],
            send_sem=main_send.at[i, k],
            recv_sem=main_recv.at[i, k],
            device_id={"seq": peers[k]},
            device_id_type=MESH,
        )

    def ext_column(rank):
        return pl.ds(pl.multiple_of((n * base + extra_rank(rank)) * size, size), size)

    def ext_copy(i, k):
        source, _, buf = triples[i]
        return pltpu.make_async_remote_copy(
            src_ref=source.at[:, :, ext_column(peers[k])],
            dst_ref=buf.at[me],
            send_sem=ext_send.at[i, k],
            recv_sem=ext_recv.at[i, k],
            device_id={"seq": peers[k]},
            device_id_type=MESH,
        )

    def ext_recv_wait(i, k):
        _, _, buf = triples[i]
        pltpu.make_async_remote_copy(
            src_ref=buf.at[me],
            dst_ref=buf.at[me],
            send_sem=ext_send.at[i, k],
            recv_sem=ext_recv.at[i, k],
            device_id={"seq": peers[k]},
            device_id_type=MESH,
        ).wait_recv()

    has_extra = extra_rank(me) < extra
    order = sorted(range(1, n), key=lambda k: -min(k, n - k))
    mains = {}
    for i in (1, 0, 2):
        for k in order:
            mains[i, k] = main_copy(i, k)
            mains[i, k].start()
    for i in (1, 0, 2):
        for k in order:

            @pl.when(extra_rank(peers[k]) < extra)
            def _():
                ext_copy(i, k).start()

    def w_columns(to_chip, half):
        which = core if half == 0 else 1 - core
        return pl.ds(pl.multiple_of((to_chip * 2 + which) * share, size), share)

    full = n * base
    spots = [(0, full, 0, full)]
    if extra:
        spots.append((full, extra, 2 * full, 2 * full + extra))
    w_copies = []
    for part, (first, count, _, there) in enumerate(spots):
        for half in range(2):
            w_copies.append(
                pltpu.make_async_remote_copy(
                    src_ref=w_ref.at[pl.ds(first, count), :, w_columns(1 - chip, half)],
                    dst_ref=w_cat.at[pl.ds(there, count), :, pl.ds(half * share, share)],
                    send_sem=w_send.at[part, half],
                    recv_sem=w_recv.at[part, half],
                    device_id={"tp": chip_mate},
                    device_id_type=MESH,
                )
            )
            w_copies[-1].start()
    locals_main, locals_w = [], []
    for i in range(3):
        source, buf, _ = triples[i]
        locals_main.append(
            pltpu.make_async_copy(
                source.at[:, :, pl.ds(pl.multiple_of(me * width, size), width)],
                buf.at[me],
                local_sem.at[i],
            )
        )
        locals_main[-1].start()

    def local_ext(i):
        source, _, buf = triples[i]
        return pltpu.make_async_copy(
            source.at[:, :, ext_column(me)], buf.at[me], local_sem.at[3 + i]
        )

    @pl.when(has_extra)
    def _():
        for i in range(3):
            local_ext(i).start()

    for part, (first, count, here, _) in enumerate(spots):
        for half in range(2):
            locals_w.append(
                pltpu.make_async_copy(
                    w_ref.at[pl.ds(first, count), :, w_columns(chip, half)],
                    w_cat.at[pl.ds(here, count), :, pl.ds(half * share, share)],
                    local_sem.at[6 + 2 * part + half],
                )
            )
            locals_w[-1].start()

    span = n * size
    row_id = lax.broadcasted_iota(jnp.int32, (span, span), 0)
    col_id = lax.broadcasted_iota(jnp.int32, (span, span), 1)
    outer, inside = lax.div(row_id, size), lax.rem(row_id, size)
    goal = lax.div(inside, rows) * size + outer * rows + lax.rem(inside, rows)
    swap[...] = jnp.where(goal == col_id, 1.0, 0.0).astype(jnp.bfloat16)

    token_total = n * blocks * rows
    key_block = lax.rem(
        lax.div(lax.broadcasted_iota(jnp.int32, (1, token_total), 1), rows), blocks
    )
    rate = float(size ** (-0.5) * np.log2(np.e))

    def head_bias(head):
        is_head = lax.broadcasted_iota(jnp.int32, mask_ref.shape, 2) == head
        live = jnp.where(is_head, mask_ref[...], 0).astype(jnp.float32)
        live = jnp.sum(live, axis=2, keepdims=True)
        allowed = jnp.zeros((blocks, token_total), jnp.float32)
        for other in range(blocks):
            allowed = jnp.where(key_block == other, live[:, other, :], allowed)
        return jnp.where(allowed > 0.5, 0.0, -jnp.inf)

    def blend(query, keys, values, bias):
        scores = lax.dot_general(
            query, keys, (((1,), (1,)), ((), ())), preferred_element_type=jnp.float32
        )
        if bias.shape[0] > 1:
            tall = scores.reshape(blocks, rows, token_total) + bias[:, None, :]
            scores = tall.reshape(blocks * rows, token_total)
        else:
            scores = scores + bias
        largest = jnp.max(scores, axis=1, keepdims=True)
        weights = jnp.exp2((scores - largest) * rate)
        totals = jnp.sum(weights, axis=1, keepdims=True)
        blended = jnp.dot(
            weights.astype(jnp.bfloat16), values, preferred_element_type=jnp.float32
        )
        return (blended / totals).astype(jnp.bfloat16)

    def swapped(pieces):
        return jnp.dot(
            jnp.concatenate(pieces, axis=1), swap[...], preferred_element_type=jnp.float32
        ).astype(jnp.bfloat16)

    my_columns = pl.ds(pl.multiple_of(me * size, size), size)

    def peer_columns(k):
        return pl.ds(pl.multiple_of(peers[k] * size, size), size)

    def o_copy(j, k):
        return pltpu.make_async_remote_copy(
            src_ref=o_buf.at[j, :, peer_columns(k)],
            dst_ref=feat.at[me * base + j],
            send_sem=o_send.at[j, k],
            recv_sem=o_recv.at[j, k],
            device_id={"seq": peers[k]},
            device_id_type=MESH,
        )

    def x_copy(head):
        return pltpu.make_async_remote_copy(
            src_ref=feat.at[head],
            dst_ref=feat.at[full + head],
            send_sem=x_send.at[head],
            recv_sem=x_recv.at[head],
            device_id={"tp": chip_mate},
            device_id_type=MESH,
        )

    def strip_rows(strip):
        return pl.ds(strip * rows, rows)

    my_extra = extra_rank(me)

    def oe_copy(strip, k):
        return pltpu.make_async_remote_copy(
            src_ref=o_ext.at[strip, :, peer_columns(k)],
            dst_ref=feat.at[2 * full + my_extra, strip_rows(strip)],
            send_sem=oe_send.at[strip, k],
            recv_sem=oe_recv.at[strip, k],
            device_id={"seq": peers[k]},
            device_id_type=MESH,
        )

    def xe_copy(strip, j):
        return pltpu.make_async_remote_copy(
            src_ref=feat.at[2 * full + j, strip_rows(strip)],
            dst_ref=feat.at[2 * full + extra + j, strip_rows(strip)],
            send_sem=xe_send.at[strip, j],
            recv_sem=xe_recv.at[strip, j],
            device_id={"tp": chip_mate},
            device_id_type=MESH,
        )

    strips = sorted(range(n), key=lambda r: min(r, n - 1 - r))
    near = sorted(range(1, n), key=lambda k: min(k, n - k))

    for i in range(3):
        locals_main[i].wait()
        for k in order:
            mains[i, k].wait_recv()
    for j in range(base):
        lanes = pl.ds(j * size, size)
        keys = k_buf[:, :, :, lanes].reshape(token_total, size)
        values = v_buf[:, :, :, lanes].reshape(token_total, size)
        bias = head_bias(me * base + j)
        o_buf[j] = swapped(
            [
                blend(
                    q_buf[:, block, :, lanes].reshape(n * rows, size),
                    keys,
                    values,
                    bias[block : block + 1, :],
                )
                for block in range(blocks)
            ]
        )
        for k in order:
            o_copy(j, k).start()
        feat[me * base + j] = o_buf[j, :, my_columns]
        x_copy(me * base + j).start()

    for j in range(base):
        for k in near:
            o_copy(j, k).wait_recv()
            x_copy(lax.rem(me + n - k, n) * base + j).start()

    def forward_extra(strip):
        for j in range(extra):
            owner = lax.rem(shift + j, n)

            @pl.when(owner != me)
            def _():
                gap = lax.rem(me - owner + n, n)
                there = feat.at[2 * full + j, strip_rows(strip)]
                pltpu.make_async_remote_copy(
                    src_ref=there,
                    dst_ref=there,
                    send_sem=oe_send.at[strip, gap],
                    recv_sem=oe_recv.at[strip, gap],
                    device_id={"seq": owner},
                    device_id_type=MESH,
                ).wait_recv()
                xe_copy(strip, j).start()

    if extra:

        @pl.when(has_extra)
        def _():
            for i in range(3):
                local_ext(i).wait()
                for k in order:
                    ext_recv_wait(i, k)

        for place, strip in enumerate(strips):

            @pl.when(has_extra)
            def _():
                keys = k_ext[...].reshape(token_total, size)
                values = v_ext[...].reshape(token_total, size)
                query = q_ext[strip].reshape(blocks * rows, size)
                found = blend(query, keys, values, head_bias(full + my_extra))
                o_ext[strip] = swapped(
                    [found[b * rows : (b + 1) * rows] for b in range(blocks)]
                )
                for k in order:
                    oe_copy(strip, k).start()
                feat[2 * full + my_extra, strip_rows(strip)] = o_ext[strip, :, my_columns]
                xe_copy(strip, my_extra).start()

            if place >= 1:
                forward_extra(strips[place - 1])
        forward_extra(strips[-1])

    for head in range(full):
        x_copy(head).wait_recv()
    groups = 2 * base
    for g in range(groups):
        mixed[g] = swapped([feat[g * n + a] for a in range(n)])
    for copy in locals_w:
        copy.wait()
    for copy in w_copies:
        copy.wait_recv()

    def core_copy(k):
        return pltpu.make_async_remote_copy(
            src_ref=core_out.at[k],
            dst_ref=core_in.at[k],
            send_sem=core_send.at[k],
            recv_sem=core_recv.at[k],
            device_id={"tp": core_mate},
            device_id_type=MESH,
        )

    def z_copy(strip):
        slot = lax.rem(me - strip + n, n)
        return pltpu.make_async_remote_copy(
            src_ref=z_out.at[strip],
            dst_ref=z_in.at[slot],
            send_sem=z_send.at[slot],
            recv_sem=z_recv.at[slot],
            device_id={"seq": strip},
            device_id_type=MESH,
        )

    def finish_core(strip):
        core_copy(strip).wait_recv()
        joint = own_sum[strip] + core_in[strip].astype(jnp.float32)

        @pl.when(me == strip)
        def _():
            total[...] = joint

        @pl.when(me != strip)
        def _():
            z_out[strip] = joint.astype(jnp.bfloat16)
            z_copy(strip).start()

    depth = 2 * heads * rows
    tokens = blocks * rows
    for place, strip in enumerate(strips):
        row = strip_rows(strip)
        parts = [[mixed[g, row, b * size : (b + 1) * size] for g in range(groups)] for b in range(blocks)]
        if extra:
            for j in range(extra):
                xe_copy(strip, j).wait_recv()
            last = swapped([feat[2 * full + a, row] for a in range(2 * extra)])
            for b in range(blocks):
                parts[b].append(last[:, b * size : (b + 1) * size])
        taken = jnp.concatenate([jnp.concatenate(p, axis=1) for p in parts], axis=0)
        core_out[strip] = jnp.dot(
            taken,
            w_cat[:, :, share:].reshape(depth, share),
            preferred_element_type=jnp.float32,
        ).astype(jnp.bfloat16)
        core_copy(strip).start()
        own_sum[strip] = jnp.dot(
            taken,
            w_cat[:, :, :share].reshape(depth, share),
            preferred_element_type=jnp.float32,
        )
        if place >= 1:
            finish_core(strips[place - 1])
    finish_core(strips[-1])
    result = total[...]
    for k in near:
        pltpu.make_async_remote_copy(
            src_ref=z_out.at[0],
            dst_ref=z_in.at[k],
            send_sem=z_send.at[k],
            recv_sem=z_recv.at[k],
            device_id={"seq": peers[k]},
            device_id_type=MESH,
        ).wait_recv()
        result = result + z_in[k].astype(jnp.float32)
    out_ref[...] = result.astype(jnp.bfloat16).reshape(blocks, rows, share)

    for k in order:
        for i in range(3):
            mains[i, k].wait_send()

            @pl.when(extra_rank(peers[k]) < extra)
            def _():
                ext_copy(i, k).wait_send()

        for j in range(base):
            o_copy(j, k).wait_send()

        @pl.when(has_extra)
        def _():
            for strip in strips:
                oe_copy(strip, k).wait_send()

    for copy in w_copies:
        copy.wait_send()
    for head in range(full):
        x_copy(head).wait_send()
    for strip in strips:
        for j in range(extra):
            xe_copy(strip, j).wait_send()
        core_copy(strip).wait_send()

        @pl.when(me != strip)
        def _():
            z_copy(strip).wait_send()


def fused_body(queries, key_vectors, value_vectors, block_mask, out_weight):
    n = lax.axis_size("seq")
    blocks, rows, _ = queries.shape
    heads = block_mask.shape[0]
    size = n * rows
    base, extra = heads // n, heads % n
    share = out_weight.shape[2] // lax.axis_size("tp")
    kind = jnp.bfloat16
    dma = pltpu.SemaphoreType.DMA
    whole = pl.BlockSpec(memory_space=pl.ANY)
    return pl.pallas_call(
        functools.partial(fused_kernel, n),
        out_shape=jax.ShapeDtypeStruct((blocks, rows, share), kind),
        in_specs=[whole, whole, whole, pl.BlockSpec(memory_space=pltpu.VMEM), whole],
        out_specs=pl.BlockSpec(memory_space=pltpu.VMEM),
        scratch_shapes=[pltpu.VMEM((n, blocks, rows, base * size), kind)] * 3
        + [pltpu.VMEM((n, blocks, rows, size), kind)] * 3
        + [
            pltpu.VMEM((n * size, n * size), kind),
            pltpu.VMEM((base, size, n * size), kind),
            pltpu.VMEM((n, rows, n * size), kind),
            pltpu.VMEM((2 * heads, size, size), kind),
            pltpu.VMEM((2 * heads, rows, 2 * share), kind),
            pltpu.VMEM((2 * base, size, n * size), kind),
            pltpu.VMEM((n, blocks * rows, share), jnp.float32),
            pltpu.VMEM((blocks * rows, share), jnp.float32),
        ]
        + [pltpu.VMEM((n, blocks * rows, share), kind)] * 4
        + [dma((10,))]
        + [dma((3, n))] * 4
        + [dma((2, 2))] * 2
        + [dma((base, n))] * 2
        + [dma((n, n))] * 2
        + [dma((n * base,))] * 2
        + [dma((n, extra + 1))] * 2
        + [dma((n,))] * 4,
        compiler_params=pltpu.CompilerParams(
            collective_id=0, has_side_effects=True, vmem_limit_bytes=60 * 1024 * 1024
        ),
    )(queries, key_vectors, value_vectors, block_mask.transpose(1, 2, 0), out_weight)


def body(queries, key_vectors, value_vectors, block_mask, out_weight):
    n, tp = lax.axis_size("seq"), lax.axis_size("tp")
    blocks, rows, features = queries.shape
    heads = block_mask.shape[0]
    size = features // heads
    share = out_weight.shape[2] // tp
    fits = (
        n > 1
        and tp // 2 == 2
        and tp % 2 == 0
        and blocks == n
        and rows % 16 == 0
        and size == n * rows
        and size % 128 == 0
        and share % size == 0
        and heads // n > 0
        and 2 * (heads % n) in (0, n)
    )
    if fits:
        return fused_body(queries, key_vectors, value_vectors, block_mask, out_weight)
    return plain_body(queries, key_vectors, value_vectors, block_mask, out_weight)


def solution(mesh):
    return jax.shard_map(
        body,
        mesh=mesh,
        in_specs=(
            P("groups", "seq", "tp"),
            P("groups", "seq", "tp"),
            P("groups", "seq", "tp"),
            P("tp", None, None),
            P("tp", "seq", None),
        ),
        out_specs=P("groups", "seq", "tp"),
        check_vma=False,
    )
```

```python
import functools

import jax
import jax.numpy as jnp
import numpy as np
from jax import lax
from jax.experimental import pallas as pl
from jax.experimental.pallas import tpu as pltpu
from jax.sharding import PartitionSpec as P

MESH = pl.DeviceIdType.MESH

KEYS = 28


def strip_tables(heads_local, blocks, slot_total):
    slot_ids = np.arange(slot_total)
    head_of = slot_ids * heads_local // slot_total
    per_head = np.bincount(head_of, minlength=heads_local)
    head_begin = np.cumsum(per_head) - per_head
    order_in_head = slot_ids - head_begin[head_of]
    head_share = per_head[head_of]
    first_block = order_in_head * blocks // head_share
    block_count = (order_in_head + 1) * blocks // head_share - first_block
    return (head_of, first_block, block_count)


def plain_body(queries, key_vectors, value_vectors, block_mask, out_weight):
    rank_count = lax.axis_size("seq")
    my_rank = lax.axis_index("seq")
    block_total, row_share, feature_width = queries.shape
    heads_local = block_mask.shape[0]
    head_size = feature_width // heads_local
    block_rows = row_share * rank_count
    per_rank = (heads_local + rank_count - 1) // rank_count
    slot_total = rank_count * per_rank
    least_share = slot_total // heads_local
    strip_cap = ((block_total + least_share - 1) // least_share + 1) // 2 * 2
    key_cap = min(KEYS, block_total)
    head_of, first_block, block_count = strip_tables(heads_local, block_total, slot_total)
    slot_grid = np.arange(slot_total).reshape(rank_count, per_rank).T
    paired = jnp.concatenate(
        [
            key_vectors.reshape(block_total, row_share, heads_local, head_size),
            value_vectors.reshape(block_total, row_share, heads_local, head_size),
        ],
        axis=3,
    )
    send_heads = jnp.asarray(head_of[slot_grid].reshape(-1), jnp.int32)
    chosen = jnp.take(paired, send_heads, axis=2)
    chosen = chosen.reshape(block_total, row_share, per_rank, rank_count, 2 * head_size)
    outgoing_pairs = chosen.transpose(2, 0, 3, 1, 4).reshape(
        per_rank, block_total, block_rows, 2 * head_size
    )
    flat_queries = queries.reshape(block_total, row_share, heads_local, head_size).transpose(
        0, 2, 1, 3
    )
    flat_queries = flat_queries.reshape(block_total * heads_local, row_share, head_size)
    positions = np.arange(strip_cap)
    unit_block = first_block[slot_grid][:, None, :] + positions[None, :, None]
    is_live = positions[None, :, None] < block_count[slot_grid][:, None, :]
    unit_index = np.where(is_live, unit_block * heads_local + head_of[slot_grid][:, None, :], 0)
    picked = jnp.take(flat_queries, jnp.asarray(unit_index.reshape(-1), jnp.int32), axis=0)
    picked = jnp.where(
        jnp.asarray(is_live.reshape(-1))[:, None, None], picked, jnp.zeros_like(picked)
    )
    outgoing_queries = picked.reshape(per_rank, strip_cap, block_rows, head_size)
    strip_queries, strip_pairs = (
        lax.all_to_all(outgoing_queries, "seq", split_axis=2, concat_axis=2, tiled=True),
        lax.all_to_all(outgoing_pairs, "seq", split_axis=2, concat_axis=2, tiled=True),
    )
    my_slots = my_rank * per_rank + jnp.arange(per_rank, dtype=jnp.int32)
    my_heads = jnp.asarray(head_of, jnp.int32)[my_slots]
    my_first = jnp.asarray(first_block, jnp.int32)[my_slots]
    query_blocks = jnp.minimum(
        my_first[:, None] + jnp.arange(strip_cap, dtype=jnp.int32)[None, :], block_total - 1
    )
    mask_rows = block_mask[my_heads[:, None], query_blocks]
    column_ids = jnp.arange(block_total, dtype=jnp.int32)
    ranking = (1 - mask_rows) * block_total + column_ids
    key_pick = jnp.argsort(ranking, axis=-1)[..., :key_cap]
    key_live = jnp.take_along_axis(mask_rows, key_pick, axis=-1)
    group_total = per_rank * strip_cap // 2
    query_groups = strip_queries.reshape(group_total, 2, block_rows, head_size)
    pick_groups = key_pick.reshape(group_total, 2, key_cap)
    live_groups = key_live.reshape(group_total, 2, key_cap)
    slot_of_group = jnp.arange(group_total, dtype=jnp.int32) // (strip_cap // 2)
    score_scale = head_size ** (-0.5)

    def attend_group(inputs):
        query_tile, pick_tile, live_tile, slot_index = inputs
        pairs_here = strip_pairs[slot_index]
        gathered = pairs_here[pick_tile]
        scores = (
            jnp.einsum(
                "qid,qkjd->qikj",
                query_tile,
                gathered[..., :head_size],
                preferred_element_type=jnp.float32,
            )
            * score_scale
        )
        allowed = (live_tile > 0)[:, None, :, None]
        scores = jnp.where(allowed, scores, -jnp.inf)
        largest = jnp.max(scores, axis=(2, 3), keepdims=True)
        weights = jnp.exp(scores - largest)
        totals = jnp.sum(weights, axis=(2, 3))
        blended = jnp.einsum(
            "qikj,qkjd->qid",
            weights.astype(jnp.bfloat16),
            gathered[..., head_size:],
            preferred_element_type=jnp.float32,
        )
        return (blended / totals[..., None]).astype(jnp.bfloat16)

    strip_out = lax.map(attend_group, (query_groups, pick_groups, live_groups, slot_of_group))
    outgoing_out = strip_out.reshape(per_rank, strip_cap, block_rows, head_size)
    returned = lax.all_to_all(outgoing_out, "seq", split_axis=2, concat_axis=2, tiled=True)
    slot_mesh, step_mesh = np.meshgrid(np.arange(slot_total), positions, indexing="ij")
    live_slot = step_mesh < block_count[slot_mesh]
    placement_index = np.zeros((block_total, heads_local), np.int64)
    source_index = (
        slot_mesh % per_rank * strip_cap + step_mesh
    ) * rank_count + slot_mesh // per_rank
    placement_index[
        first_block[slot_mesh][live_slot] + step_mesh[live_slot], head_of[slot_mesh][live_slot]
    ] = source_index[live_slot]
    flat_back = returned.reshape(per_rank * strip_cap * rank_count, row_share, head_size)
    own_out = jnp.take(flat_back, jnp.asarray(placement_index.reshape(-1), jnp.int32), axis=0)
    own_out = own_out.reshape(block_total, heads_local, row_share, head_size)
    token_total = block_total * row_share
    token_out = own_out.transpose(0, 2, 1, 3).reshape(token_total, heads_local, head_size)
    partial_sum = jnp.einsum(
        "thd,hdo->to",
        token_out,
        lax.all_gather(out_weight, "seq", axis=1, tiled=True),
        preferred_element_type=jnp.float32,
    )
    summed = lax.psum_scatter(
        partial_sum.astype(jnp.bfloat16), "tp", scatter_dimension=1, tiled=True
    ).astype(jnp.float32)
    return summed.astype(jnp.bfloat16).reshape(block_total, row_share, summed.shape[1])


def fused_kernel(
    n,
    q_ref,
    k_ref,
    v_ref,
    mask_ref,
    w_ref,
    out_ref,
    q_buf,
    k_buf,
    v_buf,
    swap,
    o_buf,
    feat,
    w_cat,
    main_sum,
    late,
    own_sum,
    core_out,
    core_in,
    z_out,
    z_in,
    local_sem,
    local_w_sem,
    main_send,
    main_recv,
    w_send,
    w_recv,
    o_send,
    o_recv,
    x_send,
    x_recv,
    xe_send,
    xe_recv,
    core_send,
    core_recv,
    z_send,
    z_recv,
):
    me = lax.axis_index("seq")
    tp = lax.axis_index("tp")
    heads = w_ref.shape[0]
    blocks, rows, _ = q_ref.shape
    size = n * rows
    base, extra = heads // n, heads % n
    share = out_ref.shape[2]
    core = lax.rem(tp, 2)
    chip = lax.div(tp, 2)
    core_mate = tp + 1 - 2 * core
    chip_mate = lax.rem(tp + 2, 4)
    shift = lax.rem(tp * extra, n)
    peers = [lax.rem(me + k, n) for k in range(n)]

    def extra_rank(rank):
        return lax.rem(rank - shift + n, n)

    barrier = pltpu.get_barrier_semaphore()
    for k in range(1, n):
        pl.semaphore_signal(
            barrier, inc=1, device_id={"seq": peers[k]}, device_id_type=MESH
        )
    for mate in (core_mate, chip_mate):
        pl.semaphore_signal(barrier, inc=1, device_id={"tp": mate}, device_id_type=MESH)
    pl.semaphore_wait(barrier, n + 1)

    pairs = ((k_ref, k_buf), (q_ref, q_buf), (v_ref, v_buf))

    def column(rank, slot):
        head = rank * base + slot if slot < base else n * base + extra_rank(rank)
        return pl.ds(pl.multiple_of(head * size, size), size)

    def qkv_copy(item, k):
        slot, i = item
        source, buf = pairs[i]
        return pltpu.make_async_remote_copy(
            src_ref=source.at[:, :, column(peers[k], slot)],
            dst_ref=buf.at[slot, me],
            send_sem=main_send.at[slot, i, k],
            recv_sem=main_recv.at[slot, i, k],
            device_id={"seq": peers[k]},
            device_id_type=MESH,
        )

    def qkv_start(item, k):
        if item[0] < base:
            qkv_copy(item, k).start()
        else:

            @pl.when(extra_rank(peers[k]) < extra)
            def _():
                qkv_copy(item, k).start()

    def qkv_wait_send(item, k):
        if item[0] < base:
            qkv_copy(item, k).wait_send()
        else:

            @pl.when(extra_rank(peers[k]) < extra)
            def _():
                qkv_copy(item, k).wait_send()

    def qkv_wait_recv(slot):
        for i in range(3):
            local_copy(slot, i).wait()
            for k in near:
                there = pairs[i][1].at[slot, me]
                pltpu.make_async_remote_copy(
                    src_ref=there,
                    dst_ref=there,
                    send_sem=main_send.at[slot, i, k],
                    recv_sem=main_recv.at[slot, i, k],
                    device_id={"seq": peers[k]},
                    device_id_type=MESH,
                ).wait_recv()

    def local_copy(slot, i):
        source, buf = pairs[i]
        return pltpu.make_async_copy(
            source.at[:, :, column(me, slot)], buf.at[slot, me], local_sem.at[slot, i]
        )

    has_extra = extra_rank(me) < extra
    order = sorted(range(1, n), key=lambda k: -min(k, n - k))
    near = order[::-1]
    slots = base + 1 if extra else base
    items = [(slot, i) for slot in range(slots) for i in range(3)]
    window = 4
    sent = [0]

    def advance(count):
        for _ in range(count):
            old = sent[0]
            sent[0] += 1
            for k in near:
                qkv_wait_send(items[old], k)
                if old + window < len(items):
                    qkv_start(items[old + window], k)

    for item in items[:window]:
        for k in order:
            qkv_start(item, k)

    def w_columns(to_chip, half):
        which = core if half == 0 else 1 - core
        return pl.ds(pl.multiple_of((to_chip * 2 + which) * share, size), share)

    full = n * base
    spots = [(0, full, 0, full)]
    if extra:
        spots.append((full, extra, 2 * full, 2 * full + extra))
    w_copies = []
    for part, (first, count, _, there) in enumerate(spots):
        for half in range(2):
            w_copies.append(
                pltpu.make_async_remote_copy(
                    src_ref=w_ref.at[pl.ds(first, count), :, w_columns(1 - chip, half)],
                    dst_ref=w_cat.at[pl.ds(there, count), :, pl.ds(half * share, share)],
                    send_sem=w_send.at[part, half],
                    recv_sem=w_recv.at[part, half],
                    device_id={"tp": chip_mate},
                    device_id_type=MESH,
                )
            )
            w_copies[-1].start()
    locals_w = []
    for slot in range(base):
        for i in range(3):
            local_copy(slot, i).start()

    if extra:

        @pl.when(has_extra)
        def _():
            for i in range(3):
                local_copy(base, i).start()

    for part, (first, count, here, _) in enumerate(spots):
        for half in range(2):
            locals_w.append(
                pltpu.make_async_copy(
                    w_ref.at[pl.ds(first, count), :, w_columns(chip, half)],
                    w_cat.at[pl.ds(here, count), :, pl.ds(half * share, share)],
                    local_w_sem.at[part, half],
                )
            )
            locals_w[-1].start()

    span = n * size
    row_id = lax.broadcasted_iota(jnp.int32, (span, span), 0)
    col_id = lax.broadcasted_iota(jnp.int32, (span, span), 1)
    outer, inside = lax.div(row_id, size), lax.rem(row_id, size)
    goal = lax.div(inside, rows) * size + outer * rows + lax.rem(inside, rows)
    swap[...] = jnp.where(goal == col_id, 1.0, 0.0).astype(jnp.bfloat16)

    token_total = n * blocks * rows
    key_block = lax.rem(
        lax.div(lax.broadcasted_iota(jnp.int32, (1, token_total), 1), rows), blocks
    )
    rate = float(size ** (-0.5) * np.log2(np.e))

    def head_bias(head):
        is_head = lax.broadcasted_iota(jnp.int32, mask_ref.shape, 2) == head
        live = jnp.where(is_head, mask_ref[...], 0).astype(jnp.float32)
        live = jnp.sum(live, axis=2, keepdims=True)
        allowed = jnp.zeros((blocks, token_total), jnp.float32)
        for other in range(blocks):
            allowed = jnp.where(key_block == other, live[:, other, :], allowed)
        return jnp.where(allowed > 0.5, 0.0, -jnp.inf)

    def blend(query, keys, values, bias):
        scores = lax.dot_general(
            query, keys, (((1,), (1,)), ((), ())), preferred_element_type=jnp.float32
        )
        scores = scores + bias
        largest = jnp.max(scores, axis=1, keepdims=True)
        weights = jnp.exp2((scores - largest) * rate)
        totals = jnp.sum(weights, axis=1, keepdims=True)
        blended = jnp.dot(
            weights.astype(jnp.bfloat16), values, preferred_element_type=jnp.float32
        )
        return (blended / totals).astype(jnp.bfloat16)

    def swapped(pieces):
        return jnp.dot(
            jnp.concatenate(pieces, axis=1), swap[...], preferred_element_type=jnp.float32
        ).astype(jnp.bfloat16)

    my_columns = pl.ds(pl.multiple_of(me * size, size), size)

    def peer_columns(k):
        return pl.ds(pl.multiple_of(peers[k] * size, size), size)

    my_extra = extra_rank(me)

    def place_of(slot):
        return me * base + slot if slot < base else 2 * full + my_extra

    def o_copy(slot, k):
        return pltpu.make_async_remote_copy(
            src_ref=o_buf.at[slot, :, peer_columns(k)],
            dst_ref=feat.at[place_of(slot)],
            send_sem=o_send.at[slot, k],
            recv_sem=o_recv.at[slot, k],
            device_id={"seq": peers[k]},
            device_id_type=MESH,
        )

    def x_copy(head):
        return pltpu.make_async_remote_copy(
            src_ref=feat.at[head],
            dst_ref=feat.at[full + head],
            send_sem=x_send.at[head],
            recv_sem=x_recv.at[head],
            device_id={"tp": chip_mate},
            device_id_type=MESH,
        )

    def xe_copy(j):
        return pltpu.make_async_remote_copy(
            src_ref=feat.at[2 * full + j],
            dst_ref=feat.at[2 * full + extra + j],
            send_sem=xe_send.at[j],
            recv_sem=xe_recv.at[j],
            device_id={"tp": chip_mate},
            device_id_type=MESH,
        )

    def attend(slot, head):
        keys = k_buf[slot].reshape(token_total, size)
        values = v_buf[slot].reshape(token_total, size)
        bias = head_bias(head)
        o_buf[slot] = swapped(
            [
                blend(
                    q_buf[slot, :, block].reshape(n * rows, size),
                    keys,
                    values,
                    bias[block : block + 1, :],
                )
                for block in range(blocks)
            ]
        )
        for k in order:
            o_copy(slot, k).start()
        feat[place_of(slot)] = o_buf[slot, :, my_columns]

    def forward(j):
        for k in near:
            o_copy(j, k).wait_recv()
            x_copy(lax.rem(me + n - k, n) * base + j).start()

    for j in range(base):
        advance(3 if j == 0 else min(2, len(items) - window - 3))
        qkv_wait_recv(j)
        attend(j, me * base + j)
        x_copy(me * base + j).start()
        if j >= 1:
            forward(j - 1)
    if extra:

        @pl.when(has_extra)
        def _():
            qkv_wait_recv(base)
            attend(base, full + my_extra)
            xe_copy(my_extra).start()

    forward(base - 1)
    for j in range(extra):
        owner = lax.rem(shift + j, n)

        @pl.when(owner != me)
        def _():
            gap = lax.rem(me - owner + n, n)
            there = feat.at[2 * full + j]
            pltpu.make_async_remote_copy(
                src_ref=there,
                dst_ref=there,
                send_sem=o_send.at[base, gap],
                recv_sem=o_recv.at[base, gap],
                device_id={"seq": owner},
                device_id_type=MESH,
            ).wait_recv()
            xe_copy(j).start()

    for head in range(full):
        x_copy(head).wait_recv()
    for copy in locals_w:
        copy.wait()
    for copy in w_copies:
        copy.wait_recv()
    groups = 2 * base
    tokens = blocks * rows

    def strip_order(pieces):
        wide = [jnp.concatenate(p, axis=1) for p in pieces]
        return jnp.concatenate(
            [wide[b][r * rows : (r + 1) * rows] for r in range(n) for b in range(blocks)],
            axis=0,
        )

    def cut_blocks(mixes):
        return [[m[:, b * size : (b + 1) * size] for m in mixes] for b in range(blocks)]

    taken = strip_order(
        cut_blocks([swapped([feat[g * n + a] for a in range(n)]) for g in range(groups)])
    )
    deep = 2 * full * rows
    for half in range(2):
        main_sum[half] = jnp.dot(
            taken,
            w_cat[: 2 * full, :, half * share : (half + 1) * share].reshape(deep, share),
            preferred_element_type=jnp.float32,
        ).reshape(n, tokens, share)
    if extra:
        for j in range(extra):
            xe_copy(j).wait_recv()
        late[...] = strip_order(
            cut_blocks([swapped([feat[2 * full + a] for a in range(2 * extra)])])
        ).reshape(n, tokens, size)

    def core_copy(k):
        return pltpu.make_async_remote_copy(
            src_ref=core_out.at[k],
            dst_ref=core_in.at[k],
            send_sem=core_send.at[k],
            recv_sem=core_recv.at[k],
            device_id={"tp": core_mate},
            device_id_type=MESH,
        )

    def z_copy(k):
        return pltpu.make_async_remote_copy(
            src_ref=z_out.at[k],
            dst_ref=z_in.at[k],
            send_sem=z_send.at[k],
            recv_sem=z_recv.at[k],
            device_id={"seq": peers[k]},
            device_id_type=MESH,
        )

    def strip_sum(k, half):
        found = main_sum[half, peers[k]]
        if extra:
            found = found + jnp.dot(
                late[peers[k]],
                w_cat[2 * full :, :, half * share : (half + 1) * share].reshape(
                    2 * extra * rows, share
                ),
                preferred_element_type=jnp.float32,
            )
        return found

    def finish_core(k):
        core_copy(k).wait_recv()
        joint = own_sum[k] + core_in[k].astype(jnp.float32)
        if k == 0:
            own_sum[0] = joint
        else:
            z_out[k] = joint.astype(jnp.bfloat16)
            z_copy(k).start()

    steps = order + [0]
    for place, k in enumerate(steps):
        core_out[k] = strip_sum(k, 1).astype(jnp.bfloat16)
        core_copy(k).start()
        own_sum[k] = strip_sum(k, 0)
        if place >= 1:
            finish_core(steps[place - 1])
    finish_core(0)
    result = own_sum[0]
    for k in near:
        z_copy(k).wait_recv()
        result = result + z_in[k].astype(jnp.float32)
    out_ref[...] = result.astype(jnp.bfloat16).reshape(blocks, rows, share)

    while sent[0] < len(items):
        advance(1)
    for k in order:
        for j in range(base):
            o_copy(j, k).wait_send()
        if extra:

            @pl.when(has_extra)
            def _():
                o_copy(base, k).wait_send()

        z_copy(k).wait_send()
    for copy in w_copies:
        copy.wait_send()
    for head in range(full):
        x_copy(head).wait_send()
    for j in range(extra):
        xe_copy(j).wait_send()
    for k in range(n):
        core_copy(k).wait_send()


def fused_body(queries, key_vectors, value_vectors, block_mask, out_weight):
    n = lax.axis_size("seq")
    blocks, rows, _ = queries.shape
    heads = block_mask.shape[0]
    size = n * rows
    base, extra = heads // n, heads % n
    share = out_weight.shape[2] // lax.axis_size("tp")
    kind = jnp.bfloat16
    dma = pltpu.SemaphoreType.DMA
    whole = pl.BlockSpec(memory_space=pl.ANY)
    return pl.pallas_call(
        functools.partial(fused_kernel, n),
        out_shape=jax.ShapeDtypeStruct((blocks, rows, share), kind),
        in_specs=[whole, whole, whole, pl.BlockSpec(memory_space=pltpu.VMEM), whole],
        out_specs=pl.BlockSpec(memory_space=pltpu.VMEM),
        scratch_shapes=[pltpu.VMEM((base + 1, n, blocks, rows, size), kind)] * 3
        + [
            pltpu.VMEM((n * size, n * size), kind),
            pltpu.VMEM((base + 1, size, n * size), kind),
            pltpu.VMEM((2 * heads, size, size), kind),
            pltpu.VMEM((2 * heads, rows, 2 * share), kind),
            pltpu.VMEM((2, n, blocks * rows, share), jnp.float32),
            pltpu.VMEM((n, blocks * rows, size), kind),
            pltpu.VMEM((n, blocks * rows, share), jnp.float32),
        ]
        + [pltpu.VMEM((n, blocks * rows, share), kind)] * 4
        + [dma((base + 1, 3))]
        + [dma((2, 2))]
        + [dma((base + 1, 3, n))] * 2
        + [dma((2, 2))] * 2
        + [dma((base + 1, n))] * 2
        + [dma((n * base,))] * 2
        + [dma((extra + 1,))] * 2
        + [dma((n,))] * 4,
        compiler_params=pltpu.CompilerParams(
            collective_id=0, has_side_effects=True, vmem_limit_bytes=60 * 1024 * 1024
        ),
    )(queries, key_vectors, value_vectors, block_mask.transpose(1, 2, 0), out_weight)


def body(queries, key_vectors, value_vectors, block_mask, out_weight):
    n, tp = lax.axis_size("seq"), lax.axis_size("tp")
    blocks, rows, features = queries.shape
    heads = block_mask.shape[0]
    size = features // heads
    share = out_weight.shape[2] // tp
    fits = (
        n > 1
        and tp // 2 == 2
        and tp % 2 == 0
        and blocks == n
        and rows % 16 == 0
        and size == n * rows
        and size % 128 == 0
        and share % size == 0
        and heads // n > 0
        and 2 * (heads % n) in (0, n)
    )
    if fits:
        return fused_body(queries, key_vectors, value_vectors, block_mask, out_weight)
    return plain_body(queries, key_vectors, value_vectors, block_mask, out_weight)


def solution(mesh):
    return jax.shard_map(
        body,
        mesh=mesh,
        in_specs=(
            P("groups", "seq", "tp"),
            P("groups", "seq", "tp"),
            P("groups", "seq", "tp"),
            P("tp", None, None),
            P("tp", "seq", None),
        ),
        out_specs=P("groups", "seq", "tp"),
        check_vma=False,
    )
```

```python
import functools

import jax
import jax.numpy as jnp
import numpy as np
from jax import lax
from jax.experimental import pallas as pl
from jax.experimental.pallas import tpu as pltpu
from jax.sharding import PartitionSpec as P

MESH = pl.DeviceIdType.MESH

KEYS = 28


def strip_tables(heads_local, blocks, slot_total):
    slot_ids = np.arange(slot_total)
    head_of = slot_ids * heads_local // slot_total
    per_head = np.bincount(head_of, minlength=heads_local)
    head_begin = np.cumsum(per_head) - per_head
    order_in_head = slot_ids - head_begin[head_of]
    head_share = per_head[head_of]
    first_block = order_in_head * blocks // head_share
    block_count = (order_in_head + 1) * blocks // head_share - first_block
    return (head_of, first_block, block_count)


def plain_body(queries, key_vectors, value_vectors, block_mask, out_weight):
    rank_count = lax.axis_size("seq")
    my_rank = lax.axis_index("seq")
    block_total, row_share, feature_width = queries.shape
    heads_local = block_mask.shape[0]
    head_size = feature_width // heads_local
    block_rows = row_share * rank_count
    per_rank = (heads_local + rank_count - 1) // rank_count
    slot_total = rank_count * per_rank
    least_share = slot_total // heads_local
    strip_cap = ((block_total + least_share - 1) // least_share + 1) // 2 * 2
    key_cap = min(KEYS, block_total)
    head_of, first_block, block_count = strip_tables(heads_local, block_total, slot_total)
    slot_grid = np.arange(slot_total).reshape(rank_count, per_rank).T
    paired = jnp.concatenate(
        [
            key_vectors.reshape(block_total, row_share, heads_local, head_size),
            value_vectors.reshape(block_total, row_share, heads_local, head_size),
        ],
        axis=3,
    )
    send_heads = jnp.asarray(head_of[slot_grid].reshape(-1), jnp.int32)
    chosen = jnp.take(paired, send_heads, axis=2)
    chosen = chosen.reshape(block_total, row_share, per_rank, rank_count, 2 * head_size)
    outgoing_pairs = chosen.transpose(2, 0, 3, 1, 4).reshape(
        per_rank, block_total, block_rows, 2 * head_size
    )
    flat_queries = queries.reshape(block_total, row_share, heads_local, head_size).transpose(
        0, 2, 1, 3
    )
    flat_queries = flat_queries.reshape(block_total * heads_local, row_share, head_size)
    positions = np.arange(strip_cap)
    unit_block = first_block[slot_grid][:, None, :] + positions[None, :, None]
    is_live = positions[None, :, None] < block_count[slot_grid][:, None, :]
    unit_index = np.where(is_live, unit_block * heads_local + head_of[slot_grid][:, None, :], 0)
    picked = jnp.take(flat_queries, jnp.asarray(unit_index.reshape(-1), jnp.int32), axis=0)
    picked = jnp.where(
        jnp.asarray(is_live.reshape(-1))[:, None, None], picked, jnp.zeros_like(picked)
    )
    outgoing_queries = picked.reshape(per_rank, strip_cap, block_rows, head_size)
    strip_queries, strip_pairs = (
        lax.all_to_all(outgoing_queries, "seq", split_axis=2, concat_axis=2, tiled=True),
        lax.all_to_all(outgoing_pairs, "seq", split_axis=2, concat_axis=2, tiled=True),
    )
    my_slots = my_rank * per_rank + jnp.arange(per_rank, dtype=jnp.int32)
    my_heads = jnp.asarray(head_of, jnp.int32)[my_slots]
    my_first = jnp.asarray(first_block, jnp.int32)[my_slots]
    query_blocks = jnp.minimum(
        my_first[:, None] + jnp.arange(strip_cap, dtype=jnp.int32)[None, :], block_total - 1
    )
    mask_rows = block_mask[my_heads[:, None], query_blocks]
    column_ids = jnp.arange(block_total, dtype=jnp.int32)
    ranking = (1 - mask_rows) * block_total + column_ids
    key_pick = jnp.argsort(ranking, axis=-1)[..., :key_cap]
    key_live = jnp.take_along_axis(mask_rows, key_pick, axis=-1)
    group_total = per_rank * strip_cap // 2
    query_groups = strip_queries.reshape(group_total, 2, block_rows, head_size)
    pick_groups = key_pick.reshape(group_total, 2, key_cap)
    live_groups = key_live.reshape(group_total, 2, key_cap)
    slot_of_group = jnp.arange(group_total, dtype=jnp.int32) // (strip_cap // 2)
    score_scale = head_size ** (-0.5)

    def attend_group(inputs):
        query_tile, pick_tile, live_tile, slot_index = inputs
        pairs_here = strip_pairs[slot_index]
        gathered = pairs_here[pick_tile]
        scores = (
            jnp.einsum(
                "qid,qkjd->qikj",
                query_tile,
                gathered[..., :head_size],
                preferred_element_type=jnp.float32,
            )
            * score_scale
        )
        allowed = (live_tile > 0)[:, None, :, None]
        scores = jnp.where(allowed, scores, -jnp.inf)
        largest = jnp.max(scores, axis=(2, 3), keepdims=True)
        weights = jnp.exp(scores - largest)
        totals = jnp.sum(weights, axis=(2, 3))
        blended = jnp.einsum(
            "qikj,qkjd->qid",
            weights.astype(jnp.bfloat16),
            gathered[..., head_size:],
            preferred_element_type=jnp.float32,
        )
        return (blended / totals[..., None]).astype(jnp.bfloat16)

    strip_out = lax.map(attend_group, (query_groups, pick_groups, live_groups, slot_of_group))
    outgoing_out = strip_out.reshape(per_rank, strip_cap, block_rows, head_size)
    returned = lax.all_to_all(outgoing_out, "seq", split_axis=2, concat_axis=2, tiled=True)
    slot_mesh, step_mesh = np.meshgrid(np.arange(slot_total), positions, indexing="ij")
    live_slot = step_mesh < block_count[slot_mesh]
    placement_index = np.zeros((block_total, heads_local), np.int64)
    source_index = (
        slot_mesh % per_rank * strip_cap + step_mesh
    ) * rank_count + slot_mesh // per_rank
    placement_index[
        first_block[slot_mesh][live_slot] + step_mesh[live_slot], head_of[slot_mesh][live_slot]
    ] = source_index[live_slot]
    flat_back = returned.reshape(per_rank * strip_cap * rank_count, row_share, head_size)
    own_out = jnp.take(flat_back, jnp.asarray(placement_index.reshape(-1), jnp.int32), axis=0)
    own_out = own_out.reshape(block_total, heads_local, row_share, head_size)
    token_total = block_total * row_share
    token_out = own_out.transpose(0, 2, 1, 3).reshape(token_total, heads_local, head_size)
    partial_sum = jnp.einsum(
        "thd,hdo->to",
        token_out,
        lax.all_gather(out_weight, "seq", axis=1, tiled=True),
        preferred_element_type=jnp.float32,
    )
    summed = lax.psum_scatter(
        partial_sum.astype(jnp.bfloat16), "tp", scatter_dimension=1, tiled=True
    ).astype(jnp.float32)
    return summed.astype(jnp.bfloat16).reshape(block_total, row_share, summed.shape[1])


def fused_kernel(
    n,
    q_ref,
    k_ref,
    v_ref,
    mask_ref,
    w_ref,
    out_ref,
    q_buf,
    k_buf,
    v_buf,
    swap,
    o_buf,
    feat,
    w_cat,
    main_sum,
    late,
    own_sum,
    core_out,
    core_in,
    z_out,
    z_in,
    relay,
    local_sem,
    local_w_sem,
    main_send,
    main_recv,
    w_send,
    w_recv,
    o_send,
    o_recv,
    x_send,
    x_recv,
    xe_send,
    xe_recv,
    core_send,
    core_recv,
    z_send,
    z_recv,
    relay_recv,
):
    me = lax.axis_index("seq")
    tp = lax.axis_index("tp")
    heads = w_ref.shape[0]
    blocks, rows, _ = q_ref.shape
    size = n * rows
    base, extra = heads // n, heads % n
    share = out_ref.shape[2]
    core = lax.rem(tp, 2)
    chip = lax.div(tp, 2)
    core_mate = tp + 1 - 2 * core
    chip_mate = lax.rem(tp + 2, 4)
    shift = lax.rem(tp * extra, n)
    peers = [lax.rem(me + k, n) for k in range(n)]

    def extra_rank(rank):
        return lax.rem(rank - shift + n, n)

    barrier = pltpu.get_barrier_semaphore()
    for k in range(1, n):
        pl.semaphore_signal(
            barrier, inc=1, device_id={"seq": peers[k]}, device_id_type=MESH
        )
    for mate in (core_mate, chip_mate):
        pl.semaphore_signal(barrier, inc=1, device_id={"tp": mate}, device_id_type=MESH)
    pl.semaphore_wait(barrier, n + 1)

    pairs = ((k_ref, k_buf), (q_ref, q_buf), (v_ref, v_buf))

    def column(rank, slot):
        head = rank * base + slot if slot < base else n * base + extra_rank(rank)
        return pl.ds(pl.multiple_of(head * size, size), size)

    def qkv_copy(item, k):
        slot, i = item
        source, buf = pairs[i]
        return pltpu.make_async_remote_copy(
            src_ref=source.at[:, :, column(peers[k], slot)],
            dst_ref=buf.at[slot, me],
            send_sem=main_send.at[slot, i, k],
            recv_sem=main_recv.at[slot, i, k],
            device_id={"seq": peers[k]},
            device_id_type=MESH,
        )

    def qkv_start(item, k):
        if item[0] < base:
            qkv_copy(item, k).start()
        else:

            @pl.when(extra_rank(peers[k]) < extra)
            def _():
                qkv_copy(item, k).start()

    def qkv_wait_send(item, k):
        if item[0] < base:
            qkv_copy(item, k).wait_send()
        else:

            @pl.when(extra_rank(peers[k]) < extra)
            def _():
                qkv_copy(item, k).wait_send()

    def qkv_wait_recv(slot):
        for i in range(3):
            local_copy(slot, i).wait()
            for k in near:
                there = pairs[i][1].at[slot, me]
                pltpu.make_async_remote_copy(
                    src_ref=there,
                    dst_ref=there,
                    send_sem=main_send.at[slot, i, k],
                    recv_sem=main_recv.at[slot, i, k],
                    device_id={"seq": peers[k]},
                    device_id_type=MESH,
                ).wait_recv()

    def local_copy(slot, i):
        source, buf = pairs[i]
        return pltpu.make_async_copy(
            source.at[:, :, column(me, slot)], buf.at[slot, me], local_sem.at[slot, i]
        )

    has_extra = extra_rank(me) < extra
    order = sorted(range(1, n), key=lambda k: -min(k, n - k))
    near = order[::-1]
    slots = base + 1 if extra else base
    items = [(slot, i) for slot in range(slots) for i in range(3)]
    window = 4
    sent = [0]

    def advance(count):
        for _ in range(count):
            old = sent[0]
            sent[0] += 1
            for k in near:
                qkv_wait_send(items[old], k)
                if old + window < len(items):
                    qkv_start(items[old + window], k)

    for item in items[:window]:
        for k in order:
            qkv_start(item, k)

    def w_columns(to_chip, half):
        which = core if half == 0 else 1 - core
        return pl.ds(pl.multiple_of((to_chip * 2 + which) * share, size), share)

    full = n * base
    spots = [(0, full, 0, full)]
    if extra:
        spots.append((full, extra, 2 * full, 2 * full + extra))
    w_copies = []
    for part, (first, count, _, there) in enumerate(spots):
        for half in range(2):
            w_copies.append(
                pltpu.make_async_remote_copy(
                    src_ref=w_ref.at[pl.ds(first, count), :, w_columns(1 - chip, half)],
                    dst_ref=w_cat.at[pl.ds(there, count), :, pl.ds(half * share, share)],
                    send_sem=w_send.at[part, half],
                    recv_sem=w_recv.at[part, half],
                    device_id={"tp": chip_mate},
                    device_id_type=MESH,
                )
            )
            w_copies[-1].start()
    locals_w = []
    for slot in range(base):
        for i in range(3):
            local_copy(slot, i).start()

    if extra:

        @pl.when(has_extra)
        def _():
            for i in range(3):
                local_copy(base, i).start()

    for part, (first, count, here, _) in enumerate(spots):
        for half in range(2):
            locals_w.append(
                pltpu.make_async_copy(
                    w_ref.at[pl.ds(first, count), :, w_columns(chip, half)],
                    w_cat.at[pl.ds(here, count), :, pl.ds(half * share, share)],
                    local_w_sem.at[part, half],
                )
            )
            locals_w[-1].start()

    span = n * size
    row_id = lax.broadcasted_iota(jnp.int32, (span, span), 0)
    col_id = lax.broadcasted_iota(jnp.int32, (span, span), 1)
    outer, inside = lax.div(row_id, size), lax.rem(row_id, size)
    goal = lax.div(inside, rows) * size + outer * rows + lax.rem(inside, rows)
    swap[...] = jnp.where(goal == col_id, 1.0, 0.0).astype(jnp.bfloat16)

    token_total = n * blocks * rows
    key_block = lax.rem(
        lax.div(lax.broadcasted_iota(jnp.int32, (1, token_total), 1), rows), blocks
    )
    rate = float(size ** (-0.5) * np.log2(np.e))

    def head_bias(head):
        is_head = lax.broadcasted_iota(jnp.int32, mask_ref.shape, 2) == head
        live = jnp.where(is_head, mask_ref[...], 0).astype(jnp.float32)
        live = jnp.sum(live, axis=2, keepdims=True)
        allowed = jnp.zeros((blocks, token_total), jnp.float32)
        for other in range(blocks):
            allowed = jnp.where(key_block == other, live[:, other, :], allowed)
        return jnp.where(allowed > 0.5, 0.0, -jnp.inf)

    def blend(query, keys, values, bias):
        scores = lax.dot_general(
            query, keys, (((1,), (1,)), ((), ())), preferred_element_type=jnp.float32
        )
        scores = scores + bias
        largest = jnp.max(scores, axis=1, keepdims=True)
        weights = jnp.exp2((scores - largest) * rate)
        totals = jnp.sum(weights, axis=1, keepdims=True)
        blended = jnp.dot(
            weights.astype(jnp.bfloat16), values, preferred_element_type=jnp.float32
        )
        return (blended / totals).astype(jnp.bfloat16)

    def swapped(pieces):
        return jnp.dot(
            jnp.concatenate(pieces, axis=1), swap[...], preferred_element_type=jnp.float32
        ).astype(jnp.bfloat16)

    my_columns = pl.ds(pl.multiple_of(me * size, size), size)

    def peer_columns(k):
        return pl.ds(pl.multiple_of(peers[k] * size, size), size)

    my_extra = extra_rank(me)

    def place_of(slot):
        return me * base + slot if slot < base else 2 * full + my_extra

    def o_copy(slot, k):
        return pltpu.make_async_remote_copy(
            src_ref=o_buf.at[slot, :, peer_columns(k)],
            dst_ref=feat.at[place_of(slot)],
            send_sem=o_send.at[slot, k],
            recv_sem=o_recv.at[slot, k],
            device_id={"seq": peers[k]},
            device_id_type=MESH,
        )

    def x_copy(head):
        return pltpu.make_async_remote_copy(
            src_ref=feat.at[head],
            dst_ref=feat.at[full + head],
            send_sem=x_send.at[head],
            recv_sem=x_recv.at[head],
            device_id={"tp": chip_mate},
            device_id_type=MESH,
        )

    def xe_copy(j):
        return pltpu.make_async_remote_copy(
            src_ref=feat.at[2 * full + j],
            dst_ref=feat.at[2 * full + extra + j],
            send_sem=xe_send.at[j],
            recv_sem=xe_recv.at[j],
            device_id={"tp": chip_mate},
            device_id_type=MESH,
        )

    def attend(slot, head):
        keys = k_buf[slot].reshape(token_total, size)
        values = v_buf[slot].reshape(token_total, size)
        bias = head_bias(head)
        o_buf[slot] = swapped(
            [
                blend(
                    q_buf[slot, :, block].reshape(n * rows, size),
                    keys,
                    values,
                    bias[block : block + 1, :],
                )
                for block in range(blocks)
            ]
        )
        for k in order:
            o_copy(slot, k).start()
        feat[place_of(slot)] = o_buf[slot, :, my_columns]

    def forward(j):
        for k in near:
            o_copy(j, k).wait_recv()
            x_copy(lax.rem(me + n - k, n) * base + j).start()

    for j in range(base):
        advance(3 if j == 0 else min(2, len(items) - window - 3))
        qkv_wait_recv(j)
        attend(j, me * base + j)
        x_copy(me * base + j).start()
        if j >= 1:
            forward(j - 1)
    if extra:

        @pl.when(has_extra)
        def _():
            qkv_wait_recv(base)
            attend(base, full + my_extra)
            xe_copy(my_extra).start()

    forward(base - 1)
    for j in range(extra):
        owner = lax.rem(shift + j, n)

        @pl.when(owner != me)
        def _():
            gap = lax.rem(me - owner + n, n)
            there = feat.at[2 * full + j]
            pltpu.make_async_remote_copy(
                src_ref=there,
                dst_ref=there,
                send_sem=o_send.at[base, gap],
                recv_sem=o_recv.at[base, gap],
                device_id={"seq": owner},
                device_id_type=MESH,
            ).wait_recv()
            xe_copy(j).start()

    for head in range(full):
        x_copy(head).wait_recv()
    for copy in locals_w:
        copy.wait()
    for copy in w_copies:
        copy.wait_recv()
    groups = 2 * base
    tokens = blocks * rows

    def strip_order(pieces):
        wide = [jnp.concatenate(p, axis=1) for p in pieces]
        return jnp.concatenate(
            [wide[b][r * rows : (r + 1) * rows] for r in range(n) for b in range(blocks)],
            axis=0,
        )

    def cut_blocks(mixes):
        return [[m[:, b * size : (b + 1) * size] for m in mixes] for b in range(blocks)]

    taken = strip_order(
        cut_blocks([swapped([feat[g * n + a] for a in range(n)]) for g in range(groups)])
    )
    deep = 2 * full * rows
    for half in range(2):
        main_sum[half] = jnp.dot(
            taken,
            w_cat[: 2 * full, :, half * share : (half + 1) * share].reshape(deep, share),
            preferred_element_type=jnp.float32,
        ).reshape(n, tokens, share)
    if extra:
        for j in range(extra):
            xe_copy(j).wait_recv()
        late[...] = strip_order(
            cut_blocks([swapped([feat[2 * full + a] for a in range(2 * extra)])])
        ).reshape(n, tokens, size)

    def core_copy(k):
        return pltpu.make_async_remote_copy(
            src_ref=core_out.at[k],
            dst_ref=core_in.at[k],
            send_sem=core_send.at[k],
            recv_sem=core_recv.at[k],
            device_id={"tp": core_mate},
            device_id_type=MESH,
        )

    half_n = n // 2
    left = me < half_n
    half_mate = me + 1 - 2 * lax.rem(me, 2)
    at_end = jnp.logical_or(me == 0, me == n - 1)
    far = [jnp.where(left, n - 1 - t, t) for t in range(half_n)]
    steps = far + [half_mate, me]
    piece = tokens // 2

    def part_of(p):
        return pl.ds(p * piece, piece)

    def relay_copy(t, p):
        return pltpu.make_async_remote_copy(
            src_ref=z_out.at[t, part_of(p)],
            dst_ref=relay.at[t, part_of(p)],
            send_sem=z_send.at[t, p],
            recv_sem=relay_recv.at[t, p],
            device_id={"seq": half_mate},
            device_id_type=MESH,
        )

    def far_copy(t, p):
        return pltpu.make_async_remote_copy(
            src_ref=z_out.at[t, part_of(p)],
            dst_ref=z_in.at[0, part_of(p)],
            send_sem=z_send.at[t, p],
            recv_sem=z_recv.at[0, p],
            device_id={"seq": far[t]},
            device_id_type=MESH,
        )

    def near_copy():
        return pltpu.make_async_remote_copy(
            src_ref=z_out.at[half_n],
            dst_ref=z_in.at[1],
            send_sem=z_send.at[half_n, 0],
            recv_sem=z_recv.at[1, 0],
            device_id={"seq": half_mate},
            device_id_type=MESH,
        )

    def strip_sum(strip, half):
        found = main_sum[half, strip]
        if extra:
            found = found + jnp.dot(
                late[strip],
                w_cat[2 * full :, :, half * share : (half + 1) * share].reshape(
                    2 * extra * rows, share
                ),
                preferred_element_type=jnp.float32,
            )
        return found

    def finish_core(t):
        core_copy(t).wait_recv()
        joint = own_sum[t] + core_in[t].astype(jnp.float32)
        if t == half_n + 1:
            own_sum[t] = joint
        elif t == half_n:
            z_out[t] = joint.astype(jnp.bfloat16)
            near_copy().start()
        else:
            own_sum[t] = joint

            @pl.when(at_end)
            def _():
                z_out[t] = joint.astype(jnp.bfloat16)
                for p in range(2):
                    relay_copy(t, p).start()

    for t, strip in enumerate(steps):
        core_out[t] = strip_sum(strip, 1).astype(jnp.bfloat16)
        core_copy(t).start()
        own_sum[t] = strip_sum(strip, 0)
        if t >= 1:
            finish_core(t - 1)
    finish_core(half_n + 1)

    @pl.when(jnp.logical_not(at_end))
    def _():
        for t in range(half_n):
            for p in range(2):
                relay_copy(t, p).wait_recv()
                z_out[t, part_of(p)] = (
                    own_sum[t, part_of(p)] + relay[t, part_of(p)].astype(jnp.float32)
                ).astype(jnp.bfloat16)
                far_copy(t, p).start()

    near_copy().wait_recv()
    for p in range(2):
        far_copy(0, p).wait_recv()
    result = own_sum[half_n + 1] + z_in[1].astype(jnp.float32) + z_in[0].astype(jnp.float32)
    out_ref[...] = result.astype(jnp.bfloat16).reshape(blocks, rows, share)
    near_copy().wait_send()
    for t in range(half_n):
        for p in range(2):
            relay_copy(t, p).wait_send()

    while sent[0] < len(items):
        advance(1)
    for k in order:
        for j in range(base):
            o_copy(j, k).wait_send()
        if extra:

            @pl.when(has_extra)
            def _():
                o_copy(base, k).wait_send()

    for copy in w_copies:
        copy.wait_send()
    for head in range(full):
        x_copy(head).wait_send()
    for j in range(extra):
        xe_copy(j).wait_send()
    for k in range(n):
        core_copy(k).wait_send()


def fused_body(queries, key_vectors, value_vectors, block_mask, out_weight):
    n = lax.axis_size("seq")
    blocks, rows, _ = queries.shape
    heads = block_mask.shape[0]
    size = n * rows
    base, extra = heads // n, heads % n
    share = out_weight.shape[2] // lax.axis_size("tp")
    kind = jnp.bfloat16
    dma = pltpu.SemaphoreType.DMA
    whole = pl.BlockSpec(memory_space=pl.ANY)
    return pl.pallas_call(
        functools.partial(fused_kernel, n),
        out_shape=jax.ShapeDtypeStruct((blocks, rows, share), kind),
        in_specs=[whole, whole, whole, pl.BlockSpec(memory_space=pltpu.VMEM), whole],
        out_specs=pl.BlockSpec(memory_space=pltpu.VMEM),
        scratch_shapes=[pltpu.VMEM((base + 1, n, blocks, rows, size), kind)] * 3
        + [
            pltpu.VMEM((n * size, n * size), kind),
            pltpu.VMEM((base + 1, size, n * size), kind),
            pltpu.VMEM((2 * heads, size, size), kind),
            pltpu.VMEM((2 * heads, rows, 2 * share), kind),
            pltpu.VMEM((2, n, blocks * rows, share), jnp.float32),
            pltpu.VMEM((n, blocks * rows, size), kind),
            pltpu.VMEM((n, blocks * rows, share), jnp.float32),
        ]
        + [pltpu.VMEM((n, blocks * rows, share), kind)] * 5
        + [dma((base + 1, 3))]
        + [dma((2, 2))]
        + [dma((base + 1, 3, n))] * 2
        + [dma((2, 2))] * 2
        + [dma((base + 1, n))] * 2
        + [dma((n * base,))] * 2
        + [dma((extra + 1,))] * 2
        + [dma((n,))] * 2
        + [dma((n, 2))] * 3,
        compiler_params=pltpu.CompilerParams(
            collective_id=0, has_side_effects=True, vmem_limit_bytes=60 * 1024 * 1024
        ),
    )(queries, key_vectors, value_vectors, block_mask.transpose(1, 2, 0), out_weight)


def body(queries, key_vectors, value_vectors, block_mask, out_weight):
    n, tp = lax.axis_size("seq"), lax.axis_size("tp")
    blocks, rows, features = queries.shape
    heads = block_mask.shape[0]
    size = features // heads
    share = out_weight.shape[2] // tp
    fits = (
        n // 2 == 2
        and n % 2 == 0
        and tp // 2 == 2
        and tp % 2 == 0
        and blocks == n
        and rows % 16 == 0
        and size == n * rows
        and size % 128 == 0
        and share % size == 0
        and heads // n > 0
        and 2 * (heads % n) in (0, n)
    )
    if fits:
        return fused_body(queries, key_vectors, value_vectors, block_mask, out_weight)
    return plain_body(queries, key_vectors, value_vectors, block_mask, out_weight)


def solution(mesh):
    return jax.shard_map(
        body,
        mesh=mesh,
        in_specs=(
            P("groups", "seq", "tp"),
            P("groups", "seq", "tp"),
            P("groups", "seq", "tp"),
            P("tp", None, None),
            P("tp", "seq", None),
        ),
        out_specs=P("groups", "seq", "tp"),
        check_vma=False,
    )
```

```python
import functools

import jax
import jax.numpy as jnp
import numpy as np
from jax import lax
from jax.experimental import pallas as pl
from jax.experimental.pallas import tpu as pltpu
from jax.sharding import PartitionSpec as P

MESH = pl.DeviceIdType.MESH

KEYS = 28


def strip_tables(heads_local, blocks, slot_total):
    slot_ids = np.arange(slot_total)
    head_of = slot_ids * heads_local // slot_total
    per_head = np.bincount(head_of, minlength=heads_local)
    head_begin = np.cumsum(per_head) - per_head
    order_in_head = slot_ids - head_begin[head_of]
    head_share = per_head[head_of]
    first_block = order_in_head * blocks // head_share
    block_count = (order_in_head + 1) * blocks // head_share - first_block
    return (head_of, first_block, block_count)


def plain_body(queries, key_vectors, value_vectors, block_mask, out_weight):
    rank_count = lax.axis_size("seq")
    my_rank = lax.axis_index("seq")
    block_total, row_share, feature_width = queries.shape
    heads_local = block_mask.shape[0]
    head_size = feature_width // heads_local
    block_rows = row_share * rank_count
    per_rank = (heads_local + rank_count - 1) // rank_count
    slot_total = rank_count * per_rank
    least_share = slot_total // heads_local
    strip_cap = ((block_total + least_share - 1) // least_share + 1) // 2 * 2
    key_cap = min(KEYS, block_total)
    head_of, first_block, block_count = strip_tables(heads_local, block_total, slot_total)
    slot_grid = np.arange(slot_total).reshape(rank_count, per_rank).T
    paired = jnp.concatenate(
        [
            key_vectors.reshape(block_total, row_share, heads_local, head_size),
            value_vectors.reshape(block_total, row_share, heads_local, head_size),
        ],
        axis=3,
    )
    send_heads = jnp.asarray(head_of[slot_grid].reshape(-1), jnp.int32)
    chosen = jnp.take(paired, send_heads, axis=2)
    chosen = chosen.reshape(block_total, row_share, per_rank, rank_count, 2 * head_size)
    outgoing_pairs = chosen.transpose(2, 0, 3, 1, 4).reshape(
        per_rank, block_total, block_rows, 2 * head_size
    )
    flat_queries = queries.reshape(block_total, row_share, heads_local, head_size).transpose(
        0, 2, 1, 3
    )
    flat_queries = flat_queries.reshape(block_total * heads_local, row_share, head_size)
    positions = np.arange(strip_cap)
    unit_block = first_block[slot_grid][:, None, :] + positions[None, :, None]
    is_live = positions[None, :, None] < block_count[slot_grid][:, None, :]
    unit_index = np.where(is_live, unit_block * heads_local + head_of[slot_grid][:, None, :], 0)
    picked = jnp.take(flat_queries, jnp.asarray(unit_index.reshape(-1), jnp.int32), axis=0)
    picked = jnp.where(
        jnp.asarray(is_live.reshape(-1))[:, None, None], picked, jnp.zeros_like(picked)
    )
    outgoing_queries = picked.reshape(per_rank, strip_cap, block_rows, head_size)
    strip_queries, strip_pairs = (
        lax.all_to_all(outgoing_queries, "seq", split_axis=2, concat_axis=2, tiled=True),
        lax.all_to_all(outgoing_pairs, "seq", split_axis=2, concat_axis=2, tiled=True),
    )
    my_slots = my_rank * per_rank + jnp.arange(per_rank, dtype=jnp.int32)
    my_heads = jnp.asarray(head_of, jnp.int32)[my_slots]
    my_first = jnp.asarray(first_block, jnp.int32)[my_slots]
    query_blocks = jnp.minimum(
        my_first[:, None] + jnp.arange(strip_cap, dtype=jnp.int32)[None, :], block_total - 1
    )
    mask_rows = block_mask[my_heads[:, None], query_blocks]
    column_ids = jnp.arange(block_total, dtype=jnp.int32)
    ranking = (1 - mask_rows) * block_total + column_ids
    key_pick = jnp.argsort(ranking, axis=-1)[..., :key_cap]
    key_live = jnp.take_along_axis(mask_rows, key_pick, axis=-1)
    group_total = per_rank * strip_cap // 2
    query_groups = strip_queries.reshape(group_total, 2, block_rows, head_size)
    pick_groups = key_pick.reshape(group_total, 2, key_cap)
    live_groups = key_live.reshape(group_total, 2, key_cap)
    slot_of_group = jnp.arange(group_total, dtype=jnp.int32) // (strip_cap // 2)
    score_scale = head_size ** (-0.5)

    def attend_group(inputs):
        query_tile, pick_tile, live_tile, slot_index = inputs
        pairs_here = strip_pairs[slot_index]
        gathered = pairs_here[pick_tile]
        scores = (
            jnp.einsum(
                "qid,qkjd->qikj",
                query_tile,
                gathered[..., :head_size],
                preferred_element_type=jnp.float32,
            )
            * score_scale
        )
        allowed = (live_tile > 0)[:, None, :, None]
        scores = jnp.where(allowed, scores, -jnp.inf)
        largest = jnp.max(scores, axis=(2, 3), keepdims=True)
        weights = jnp.exp(scores - largest)
        totals = jnp.sum(weights, axis=(2, 3))
        blended = jnp.einsum(
            "qikj,qkjd->qid",
            weights.astype(jnp.bfloat16),
            gathered[..., head_size:],
            preferred_element_type=jnp.float32,
        )
        return (blended / totals[..., None]).astype(jnp.bfloat16)

    strip_out = lax.map(attend_group, (query_groups, pick_groups, live_groups, slot_of_group))
    outgoing_out = strip_out.reshape(per_rank, strip_cap, block_rows, head_size)
    returned = lax.all_to_all(outgoing_out, "seq", split_axis=2, concat_axis=2, tiled=True)
    slot_mesh, step_mesh = np.meshgrid(np.arange(slot_total), positions, indexing="ij")
    live_slot = step_mesh < block_count[slot_mesh]
    placement_index = np.zeros((block_total, heads_local), np.int64)
    source_index = (
        slot_mesh % per_rank * strip_cap + step_mesh
    ) * rank_count + slot_mesh // per_rank
    placement_index[
        first_block[slot_mesh][live_slot] + step_mesh[live_slot], head_of[slot_mesh][live_slot]
    ] = source_index[live_slot]
    flat_back = returned.reshape(per_rank * strip_cap * rank_count, row_share, head_size)
    own_out = jnp.take(flat_back, jnp.asarray(placement_index.reshape(-1), jnp.int32), axis=0)
    own_out = own_out.reshape(block_total, heads_local, row_share, head_size)
    token_total = block_total * row_share
    token_out = own_out.transpose(0, 2, 1, 3).reshape(token_total, heads_local, head_size)
    partial_sum = jnp.einsum(
        "thd,hdo->to",
        token_out,
        lax.all_gather(out_weight, "seq", axis=1, tiled=True),
        preferred_element_type=jnp.float32,
    )
    summed = lax.psum_scatter(
        partial_sum.astype(jnp.bfloat16), "tp", scatter_dimension=1, tiled=True
    ).astype(jnp.float32)
    return summed.astype(jnp.bfloat16).reshape(block_total, row_share, summed.shape[1])


def fused_kernel(
    n,
    q_ref,
    k_ref,
    v_ref,
    mask_ref,
    w_ref,
    out_ref,
    q_buf,
    k_buf,
    v_buf,
    swap,
    o_buf,
    o_ext,
    feat,
    feat_ext,
    w_cat,
    main_sum,
    late,
    own_sum,
    core_out,
    core_in,
    z_out,
    z_in,
    relay,
    local_sem,
    local_w_sem,
    main_send,
    main_recv,
    w_send,
    w_recv,
    o_send,
    o_recv,
    oe_send,
    oe_recv,
    x_send,
    x_recv,
    xe_send,
    xe_recv,
    core_send,
    core_recv,
    z_send,
    z_recv,
    relay_recv,
):
    me = lax.axis_index("seq")
    tp = lax.axis_index("tp")
    heads = w_ref.shape[0]
    blocks, rows, _ = q_ref.shape
    size = n * rows
    base, extra = heads // n, heads % n
    share = out_ref.shape[2]
    core = lax.rem(tp, 2)
    chip = lax.div(tp, 2)
    core_mate = tp + 1 - 2 * core
    chip_mate = lax.rem(tp + 2, 4)
    shift = lax.rem(tp * extra, n)
    peers = [lax.rem(me + k, n) for k in range(n)]

    def extra_rank(rank):
        return lax.rem(rank - shift + n, n)

    barrier = pltpu.get_barrier_semaphore()
    for k in range(1, n):
        pl.semaphore_signal(
            barrier, inc=1, device_id={"seq": peers[k]}, device_id_type=MESH
        )
    for mate in (core_mate, chip_mate):
        pl.semaphore_signal(barrier, inc=1, device_id={"tp": mate}, device_id_type=MESH)
    pl.semaphore_wait(barrier, n + 1)

    pairs = ((k_ref, k_buf), (q_ref, q_buf), (v_ref, v_buf))

    def column(rank, slot):
        head = rank * base + slot if slot < base else n * base + extra_rank(rank)
        return pl.ds(pl.multiple_of(head * size, size), size)

    def qkv_copy(item, k):
        slot, i = item
        source, buf = pairs[i]
        return pltpu.make_async_remote_copy(
            src_ref=source.at[:, :, column(peers[k], slot)],
            dst_ref=buf.at[slot, me],
            send_sem=main_send.at[slot, i, k],
            recv_sem=main_recv.at[slot, i, k],
            device_id={"seq": peers[k]},
            device_id_type=MESH,
        )

    def qkv_start(item, k):
        if item[0] < base:
            qkv_copy(item, k).start()
        else:

            @pl.when(extra_rank(peers[k]) < extra)
            def _():
                qkv_copy(item, k).start()

    def qkv_wait_send(item, k):
        if item[0] < base:
            qkv_copy(item, k).wait_send()
        else:

            @pl.when(extra_rank(peers[k]) < extra)
            def _():
                qkv_copy(item, k).wait_send()

    def qkv_wait_recv(slot):
        for i in range(3):
            local_copy(slot, i).wait()
            for k in near:
                there = pairs[i][1].at[slot, me]
                pltpu.make_async_remote_copy(
                    src_ref=there,
                    dst_ref=there,
                    send_sem=main_send.at[slot, i, k],
                    recv_sem=main_recv.at[slot, i, k],
                    device_id={"seq": peers[k]},
                    device_id_type=MESH,
                ).wait_recv()

    def local_copy(slot, i):
        source, buf = pairs[i]
        return pltpu.make_async_copy(
            source.at[:, :, column(me, slot)], buf.at[slot, me], local_sem.at[slot, i]
        )

    has_extra = extra_rank(me) < extra
    order = sorted(range(1, n), key=lambda k: -min(k, n - k))
    near = order[::-1]
    slots = base + 1 if extra else base
    items = [(slot, i) for slot in range(slots) for i in range(3)]
    window = 4
    sent = [0]

    def advance(count):
        for _ in range(count):
            old = sent[0]
            sent[0] += 1
            for k in near:
                qkv_wait_send(items[old], k)
                if old + window < len(items):
                    qkv_start(items[old + window], k)

    for item in items[:window]:
        for k in order:
            qkv_start(item, k)

    def w_columns(to_chip, half):
        which = core if half == 0 else 1 - core
        return pl.ds(pl.multiple_of((to_chip * 2 + which) * share, size), share)

    full = n * base
    spots = [(0, full, 0, full)]
    if extra:
        spots.append((full, extra, 2 * full, 2 * full + extra))
    w_copies = []
    for part, (first, count, _, there) in enumerate(spots):
        for half in range(2):
            w_copies.append(
                pltpu.make_async_remote_copy(
                    src_ref=w_ref.at[pl.ds(first, count), :, w_columns(1 - chip, half)],
                    dst_ref=w_cat.at[pl.ds(there, count), :, pl.ds(half * share, share)],
                    send_sem=w_send.at[part, half],
                    recv_sem=w_recv.at[part, half],
                    device_id={"tp": chip_mate},
                    device_id_type=MESH,
                )
            )
            w_copies[-1].start()
    locals_w = []
    for slot in range(base):
        for i in range(3):
            local_copy(slot, i).start()

    if extra:

        @pl.when(has_extra)
        def _():
            for i in range(3):
                local_copy(base, i).start()

    for part, (first, count, here, _) in enumerate(spots):
        for half in range(2):
            locals_w.append(
                pltpu.make_async_copy(
                    w_ref.at[pl.ds(first, count), :, w_columns(chip, half)],
                    w_cat.at[pl.ds(here, count), :, pl.ds(half * share, share)],
                    local_w_sem.at[part, half],
                )
            )
            locals_w[-1].start()

    span = n * size
    row_id = lax.broadcasted_iota(jnp.int32, (span, span), 0)
    col_id = lax.broadcasted_iota(jnp.int32, (span, span), 1)
    outer, inside = lax.div(row_id, size), lax.rem(row_id, size)
    goal = lax.div(inside, rows) * size + outer * rows + lax.rem(inside, rows)
    swap[...] = jnp.where(goal == col_id, 1.0, 0.0).astype(jnp.bfloat16)

    token_total = n * blocks * rows
    key_block = lax.rem(
        lax.div(lax.broadcasted_iota(jnp.int32, (1, token_total), 1), rows), blocks
    )
    rate = float(size ** (-0.5) * np.log2(np.e))

    def head_bias(head):
        is_head = lax.broadcasted_iota(jnp.int32, mask_ref.shape, 2) == head
        live = jnp.where(is_head, mask_ref[...], 0).astype(jnp.float32)
        live = jnp.sum(live, axis=2, keepdims=True)
        allowed = jnp.zeros((blocks, token_total), jnp.float32)
        for other in range(blocks):
            allowed = jnp.where(key_block == other, live[:, other, :], allowed)
        return jnp.where(allowed > 0.5, 0.0, -jnp.inf)

    def blend(query, keys, values, bias):
        scores = lax.dot_general(
            query, keys, (((1,), (1,)), ((), ())), preferred_element_type=jnp.float32
        )
        scores = scores + bias
        largest = jnp.max(scores, axis=1, keepdims=True)
        weights = jnp.exp2((scores - largest) * rate)
        totals = jnp.sum(weights, axis=1, keepdims=True)
        blended = jnp.dot(
            weights.astype(jnp.bfloat16), values, preferred_element_type=jnp.float32
        )
        return (blended / totals).astype(jnp.bfloat16)

    def swapped(pieces):
        return jnp.dot(
            jnp.concatenate(pieces, axis=1), swap[...], preferred_element_type=jnp.float32
        ).astype(jnp.bfloat16)

    my_columns = pl.ds(pl.multiple_of(me * size, size), size)

    def peer_columns(k):
        return pl.ds(pl.multiple_of(peers[k] * size, size), size)

    my_extra = extra_rank(me)

    halves = 2
    short = rows // halves
    wide_rows = n * short

    def o_copy(slot, k):
        return pltpu.make_async_remote_copy(
            src_ref=o_buf.at[slot, :, peer_columns(k)],
            dst_ref=feat.at[me * base + slot],
            send_sem=o_send.at[slot, k],
            recv_sem=o_recv.at[slot, k],
            device_id={"seq": peers[k]},
            device_id_type=MESH,
        )

    def oe_copy(a, k):
        return pltpu.make_async_remote_copy(
            src_ref=o_ext.at[a, :, peer_columns(k)],
            dst_ref=feat_ext.at[a, my_extra],
            send_sem=oe_send.at[a, k],
            recv_sem=oe_recv.at[a, k],
            device_id={"seq": peers[k]},
            device_id_type=MESH,
        )

    def x_copy(head):
        return pltpu.make_async_remote_copy(
            src_ref=feat.at[head],
            dst_ref=feat.at[full + head],
            send_sem=x_send.at[head],
            recv_sem=x_recv.at[head],
            device_id={"tp": chip_mate},
            device_id_type=MESH,
        )

    def xe_copy(a, j):
        return pltpu.make_async_remote_copy(
            src_ref=feat_ext.at[a, j],
            dst_ref=feat_ext.at[a, extra + j],
            send_sem=xe_send.at[a, j],
            recv_sem=xe_recv.at[a, j],
            device_id={"tp": chip_mate},
            device_id_type=MESH,
        )

    def attend(slot, head):
        keys = k_buf[slot].reshape(token_total, size)
        values = v_buf[slot].reshape(token_total, size)
        bias = head_bias(head)
        o_buf[slot] = swapped(
            [
                blend(
                    q_buf[slot, :, block].reshape(n * rows, size),
                    keys,
                    values,
                    bias[block : block + 1, :],
                )
                for block in range(blocks)
            ]
        )
        for k in order:
            o_copy(slot, k).start()
        feat[me * base + slot] = o_buf[slot, :, my_columns]

    def attend_extra():
        keys = k_buf[base].reshape(token_total, size)
        values = v_buf[base].reshape(token_total, size)
        bias = head_bias(full + my_extra)
        for a in range(halves):
            o_ext[a] = swapped(
                [
                    blend(
                        q_buf[base, :, block, a * short : (a + 1) * short].reshape(
                            wide_rows, size
                        ),
                        keys,
                        values,
                        bias[block : block + 1, :],
                    )
                    for block in range(blocks)
                ]
            )
            for k in order:
                oe_copy(a, k).start()
            feat_ext[a, my_extra] = o_ext[a, :, my_columns]
            xe_copy(a, my_extra).start()

    def forward_extra(a):
        for j in range(extra):
            owner = lax.rem(shift + j, n)

            @pl.when(owner != me)
            def _():
                gap = lax.rem(me - owner + n, n)
                there = feat_ext.at[a, j]
                pltpu.make_async_remote_copy(
                    src_ref=there,
                    dst_ref=there,
                    send_sem=oe_send.at[a, gap],
                    recv_sem=oe_recv.at[a, gap],
                    device_id={"seq": owner},
                    device_id_type=MESH,
                ).wait_recv()
                xe_copy(a, j).start()

    def forward(j):
        for k in near:
            o_copy(j, k).wait_recv()
            x_copy(lax.rem(me + n - k, n) * base + j).start()

    for j in range(base):
        advance(3 if j == 0 else min(2, len(items) - window - 3))
        qkv_wait_recv(j)
        attend(j, me * base + j)
        x_copy(me * base + j).start()
        if j >= 1:
            forward(j - 1)
    forward(base - 1)
    if extra:

        @pl.when(has_extra)
        def _():
            qkv_wait_recv(base)
            attend_extra()

    forward_extra(0)
    for head in range(full):
        x_copy(head).wait_recv()
    for copy in locals_w:
        copy.wait()
    for copy in w_copies:
        copy.wait_recv()
    groups = 2 * base
    tokens = blocks * rows

    def strip_order(pieces):
        wide = [jnp.concatenate(p, axis=1) for p in pieces]
        return jnp.concatenate(
            [wide[b][r * rows : (r + 1) * rows] for r in range(n) for b in range(blocks)],
            axis=0,
        )

    def cut_blocks(mixes):
        return [[m[:, b * size : (b + 1) * size] for m in mixes] for b in range(blocks)]

    taken = strip_order(
        cut_blocks([swapped([feat[g * n + a] for a in range(n)]) for g in range(groups)])
    )
    deep = 2 * full * rows
    for half in range(2):
        main_sum[half] = jnp.dot(
            taken,
            w_cat[: 2 * full, :, half * share : (half + 1) * share].reshape(deep, share),
            preferred_element_type=jnp.float32,
        ).reshape(n, blocks, rows, share)
    for a in range(1, halves):
        forward_extra(a)

    def core_copy(a, t):
        return pltpu.make_async_remote_copy(
            src_ref=core_out.at[a, t],
            dst_ref=core_in.at[a, t],
            send_sem=core_send.at[a, t],
            recv_sem=core_recv.at[a, t],
            device_id={"tp": core_mate},
            device_id_type=MESH,
        )

    half_n = n // 2
    left = me < half_n
    half_mate = me + 1 - 2 * lax.rem(me, 2)
    at_end = jnp.logical_or(me == 0, me == n - 1)
    far = [jnp.where(left, n - 1 - t, t) for t in range(half_n)]
    steps = far + [half_mate, me]
    piece = tokens // halves

    def relay_copy(a, t):
        return pltpu.make_async_remote_copy(
            src_ref=z_out.at[a, t],
            dst_ref=relay.at[a, t],
            send_sem=z_send.at[a, t],
            recv_sem=relay_recv.at[a, t],
            device_id={"seq": half_mate},
            device_id_type=MESH,
        )

    def far_copy(a, t):
        return pltpu.make_async_remote_copy(
            src_ref=z_out.at[a, t],
            dst_ref=z_in.at[a, 0],
            send_sem=z_send.at[a, t],
            recv_sem=z_recv.at[a, 0],
            device_id={"seq": far[t]},
            device_id_type=MESH,
        )

    def near_copy(a):
        return pltpu.make_async_remote_copy(
            src_ref=z_out.at[a, half_n],
            dst_ref=z_in.at[a, 1],
            send_sem=z_send.at[a, half_n],
            recv_sem=z_recv.at[a, 1],
            device_id={"seq": half_mate},
            device_id_type=MESH,
        )

    def strip_sum(a, strip, half):
        found = main_sum[half, strip, :, a * short : (a + 1) * short, :].reshape(piece, share)
        if extra:
            found = found + jnp.dot(
                late[a, strip],
                w_cat[2 * full :, :, half * share : (half + 1) * share].reshape(
                    2 * extra * rows, share
                ),
                preferred_element_type=jnp.float32,
            )
        return found

    def finish_core(a, t):
        core_copy(a, t).wait_recv()
        joint = own_sum[a, t] + core_in[a, t].astype(jnp.float32)
        if t == half_n + 1:
            own_sum[a, t] = joint
        elif t == half_n:
            z_out[a, t] = joint.astype(jnp.bfloat16)
            near_copy(a).start()
        else:
            own_sum[a, t] = joint

            @pl.when(at_end)
            def _():
                z_out[a, t] = joint.astype(jnp.bfloat16)
                relay_copy(a, t).start()

    for a in range(halves):
        if extra:
            for j in range(extra):
                xe_copy(a, j).wait_recv()
            mix = swapped([feat_ext[a, e] for e in range(2 * extra)])
            for r in range(n):
                late[a, r] = jnp.concatenate(
                    [
                        mix[r * short : (r + 1) * short, b * size : (b + 1) * size]
                        for b in range(blocks)
                    ],
                    axis=0,
                )
        for t, strip in enumerate(steps):
            core_out[a, t] = strip_sum(a, strip, 1).astype(jnp.bfloat16)
            core_copy(a, t).start()
            own_sum[a, t] = strip_sum(a, strip, 0)
            if t >= 1:
                finish_core(a, t - 1)
        finish_core(a, half_n + 1)

    @pl.when(jnp.logical_not(at_end))
    def _():
        for a in range(halves):
            for t in range(half_n):
                relay_copy(a, t).wait_recv()
                z_out[a, t] = (own_sum[a, t] + relay[a, t].astype(jnp.float32)).astype(
                    jnp.bfloat16
                )
                far_copy(a, t).start()

    for a in range(halves):
        near_copy(a).wait_recv()
        far_copy(a, 0).wait_recv()
        result = own_sum[a, half_n + 1] + z_in[a, 1].astype(jnp.float32)
        result = result + z_in[a, 0].astype(jnp.float32)
        out_ref[:, a * short : (a + 1) * short, :] = result.astype(jnp.bfloat16).reshape(
            blocks, short, share
        )
        near_copy(a).wait_send()
        for t in range(half_n):
            relay_copy(a, t).wait_send()

    while sent[0] < len(items):
        advance(1)
    for k in order:
        for j in range(base):
            o_copy(j, k).wait_send()
        if extra:

            @pl.when(has_extra)
            def _():
                for a in range(halves):
                    oe_copy(a, k).wait_send()

    for copy in w_copies:
        copy.wait_send()
    for head in range(full):
        x_copy(head).wait_send()
    for a in range(halves):
        for j in range(extra):
            xe_copy(a, j).wait_send()
        for t in range(len(steps)):
            core_copy(a, t).wait_send()


def fused_body(queries, key_vectors, value_vectors, block_mask, out_weight):
    n = lax.axis_size("seq")
    blocks, rows, _ = queries.shape
    heads = block_mask.shape[0]
    size = n * rows
    base, extra = heads // n, heads % n
    share = out_weight.shape[2] // lax.axis_size("tp")
    kind = jnp.bfloat16
    dma = pltpu.SemaphoreType.DMA
    whole = pl.BlockSpec(memory_space=pl.ANY)
    return pl.pallas_call(
        functools.partial(fused_kernel, n),
        out_shape=jax.ShapeDtypeStruct((blocks, rows, share), kind),
        in_specs=[whole, whole, whole, pl.BlockSpec(memory_space=pltpu.VMEM), whole],
        out_specs=pl.BlockSpec(memory_space=pltpu.VMEM),
        scratch_shapes=[pltpu.VMEM((base + 1, n, blocks, rows, size), kind)] * 3
        + [
            pltpu.VMEM((n * size, n * size), kind),
            pltpu.VMEM((base, size, n * size), kind),
            pltpu.VMEM((2, size // 2, n * size), kind),
            pltpu.VMEM((2 * base * n, size, size), kind),
            pltpu.VMEM((2, 2 * extra + 1, size // 2, size), kind),
            pltpu.VMEM((2 * heads, rows, 2 * share), kind),
            pltpu.VMEM((2, n, blocks, rows, share), jnp.float32),
            pltpu.VMEM((2, n, blocks * rows // 2, size), kind),
            pltpu.VMEM((2, n, blocks * rows // 2, share), jnp.float32),
        ]
        + [pltpu.VMEM((2, n, blocks * rows // 2, share), kind)] * 5
        + [dma((base + 1, 3))]
        + [dma((2, 2))]
        + [dma((base + 1, 3, n))] * 2
        + [dma((2, 2))] * 2
        + [dma((base, n))] * 2
        + [dma((2, n))] * 2
        + [dma((n * base,))] * 2
        + [dma((2, extra + 1))] * 2
        + [dma((2, n))] * 5,
        compiler_params=pltpu.CompilerParams(
            collective_id=0, has_side_effects=True, vmem_limit_bytes=60 * 1024 * 1024
        ),
    )(queries, key_vectors, value_vectors, block_mask.transpose(1, 2, 0), out_weight)


def body(queries, key_vectors, value_vectors, block_mask, out_weight):
    n, tp = lax.axis_size("seq"), lax.axis_size("tp")
    blocks, rows, features = queries.shape
    heads = block_mask.shape[0]
    size = features // heads
    share = out_weight.shape[2] // tp
    fits = (
        n // 2 == 2
        and n % 2 == 0
        and tp // 2 == 2
        and tp % 2 == 0
        and blocks == n
        and rows % 32 == 0
        and size == n * rows
        and size % 128 == 0
        and share % size == 0
        and heads // n > 0
        and 2 * (heads % n) in (0, n)
    )
    if fits:
        return fused_body(queries, key_vectors, value_vectors, block_mask, out_weight)
    return plain_body(queries, key_vectors, value_vectors, block_mask, out_weight)


def solution(mesh):
    return jax.shard_map(
        body,
        mesh=mesh,
        in_specs=(
            P("groups", "seq", "tp"),
            P("groups", "seq", "tp"),
            P("groups", "seq", "tp"),
            P("tp", None, None),
            P("tp", "seq", None),
        ),
        out_specs=P("groups", "seq", "tp"),
        check_vma=False,
    )
```

```python
import functools

import jax
import jax.numpy as jnp
import numpy as np
from jax import lax
from jax.experimental import pallas as pl
from jax.experimental.pallas import tpu as pltpu
from jax.sharding import PartitionSpec as P

MESH = pl.DeviceIdType.MESH

KEYS = 28


def strip_tables(heads_local, blocks, slot_total):
    slot_ids = np.arange(slot_total)
    head_of = slot_ids * heads_local // slot_total
    per_head = np.bincount(head_of, minlength=heads_local)
    head_begin = np.cumsum(per_head) - per_head
    order_in_head = slot_ids - head_begin[head_of]
    head_share = per_head[head_of]
    first_block = order_in_head * blocks // head_share
    block_count = (order_in_head + 1) * blocks // head_share - first_block
    return (head_of, first_block, block_count)


def plain_body(queries, key_vectors, value_vectors, block_mask, out_weight):
    rank_count = lax.axis_size("seq")
    my_rank = lax.axis_index("seq")
    block_total, row_share, feature_width = queries.shape
    heads_local = block_mask.shape[0]
    head_size = feature_width // heads_local
    block_rows = row_share * rank_count
    per_rank = (heads_local + rank_count - 1) // rank_count
    slot_total = rank_count * per_rank
    least_share = slot_total // heads_local
    strip_cap = ((block_total + least_share - 1) // least_share + 1) // 2 * 2
    key_cap = min(KEYS, block_total)
    head_of, first_block, block_count = strip_tables(heads_local, block_total, slot_total)
    slot_grid = np.arange(slot_total).reshape(rank_count, per_rank).T
    paired = jnp.concatenate(
        [
            key_vectors.reshape(block_total, row_share, heads_local, head_size),
            value_vectors.reshape(block_total, row_share, heads_local, head_size),
        ],
        axis=3,
    )
    send_heads = jnp.asarray(head_of[slot_grid].reshape(-1), jnp.int32)
    chosen = jnp.take(paired, send_heads, axis=2)
    chosen = chosen.reshape(block_total, row_share, per_rank, rank_count, 2 * head_size)
    outgoing_pairs = chosen.transpose(2, 0, 3, 1, 4).reshape(
        per_rank, block_total, block_rows, 2 * head_size
    )
    flat_queries = queries.reshape(block_total, row_share, heads_local, head_size).transpose(
        0, 2, 1, 3
    )
    flat_queries = flat_queries.reshape(block_total * heads_local, row_share, head_size)
    positions = np.arange(strip_cap)
    unit_block = first_block[slot_grid][:, None, :] + positions[None, :, None]
    is_live = positions[None, :, None] < block_count[slot_grid][:, None, :]
    unit_index = np.where(is_live, unit_block * heads_local + head_of[slot_grid][:, None, :], 0)
    picked = jnp.take(flat_queries, jnp.asarray(unit_index.reshape(-1), jnp.int32), axis=0)
    picked = jnp.where(
        jnp.asarray(is_live.reshape(-1))[:, None, None], picked, jnp.zeros_like(picked)
    )
    outgoing_queries = picked.reshape(per_rank, strip_cap, block_rows, head_size)
    strip_queries, strip_pairs = (
        lax.all_to_all(outgoing_queries, "seq", split_axis=2, concat_axis=2, tiled=True),
        lax.all_to_all(outgoing_pairs, "seq", split_axis=2, concat_axis=2, tiled=True),
    )
    my_slots = my_rank * per_rank + jnp.arange(per_rank, dtype=jnp.int32)
    my_heads = jnp.asarray(head_of, jnp.int32)[my_slots]
    my_first = jnp.asarray(first_block, jnp.int32)[my_slots]
    query_blocks = jnp.minimum(
        my_first[:, None] + jnp.arange(strip_cap, dtype=jnp.int32)[None, :], block_total - 1
    )
    mask_rows = block_mask[my_heads[:, None], query_blocks]
    column_ids = jnp.arange(block_total, dtype=jnp.int32)
    ranking = (1 - mask_rows) * block_total + column_ids
    key_pick = jnp.argsort(ranking, axis=-1)[..., :key_cap]
    key_live = jnp.take_along_axis(mask_rows, key_pick, axis=-1)
    group_total = per_rank * strip_cap // 2
    query_groups = strip_queries.reshape(group_total, 2, block_rows, head_size)
    pick_groups = key_pick.reshape(group_total, 2, key_cap)
    live_groups = key_live.reshape(group_total, 2, key_cap)
    slot_of_group = jnp.arange(group_total, dtype=jnp.int32) // (strip_cap // 2)
    score_scale = head_size ** (-0.5)

    def attend_group(inputs):
        query_tile, pick_tile, live_tile, slot_index = inputs
        pairs_here = strip_pairs[slot_index]
        gathered = pairs_here[pick_tile]
        scores = (
            jnp.einsum(
                "qid,qkjd->qikj",
                query_tile,
                gathered[..., :head_size],
                preferred_element_type=jnp.float32,
            )
            * score_scale
        )
        allowed = (live_tile > 0)[:, None, :, None]
        scores = jnp.where(allowed, scores, -jnp.inf)
        largest = jnp.max(scores, axis=(2, 3), keepdims=True)
        weights = jnp.exp(scores - largest)
        totals = jnp.sum(weights, axis=(2, 3))
        blended = jnp.einsum(
            "qikj,qkjd->qid",
            weights.astype(jnp.bfloat16),
            gathered[..., head_size:],
            preferred_element_type=jnp.float32,
        )
        return (blended / totals[..., None]).astype(jnp.bfloat16)

    strip_out = lax.map(attend_group, (query_groups, pick_groups, live_groups, slot_of_group))
    outgoing_out = strip_out.reshape(per_rank, strip_cap, block_rows, head_size)
    returned = lax.all_to_all(outgoing_out, "seq", split_axis=2, concat_axis=2, tiled=True)
    slot_mesh, step_mesh = np.meshgrid(np.arange(slot_total), positions, indexing="ij")
    live_slot = step_mesh < block_count[slot_mesh]
    placement_index = np.zeros((block_total, heads_local), np.int64)
    source_index = (
        slot_mesh % per_rank * strip_cap + step_mesh
    ) * rank_count + slot_mesh // per_rank
    placement_index[
        first_block[slot_mesh][live_slot] + step_mesh[live_slot], head_of[slot_mesh][live_slot]
    ] = source_index[live_slot]
    flat_back = returned.reshape(per_rank * strip_cap * rank_count, row_share, head_size)
    own_out = jnp.take(flat_back, jnp.asarray(placement_index.reshape(-1), jnp.int32), axis=0)
    own_out = own_out.reshape(block_total, heads_local, row_share, head_size)
    token_total = block_total * row_share
    token_out = own_out.transpose(0, 2, 1, 3).reshape(token_total, heads_local, head_size)
    partial_sum = jnp.einsum(
        "thd,hdo->to",
        token_out,
        lax.all_gather(out_weight, "seq", axis=1, tiled=True),
        preferred_element_type=jnp.float32,
    )
    summed = lax.psum_scatter(
        partial_sum.astype(jnp.bfloat16), "tp", scatter_dimension=1, tiled=True
    ).astype(jnp.float32)
    return summed.astype(jnp.bfloat16).reshape(block_total, row_share, summed.shape[1])


def fused_kernel(
    n,
    q_ref,
    k_ref,
    v_ref,
    mask_ref,
    w_ref,
    out_ref,
    q_buf,
    k_buf,
    v_buf,
    swap,
    o_buf,
    feat,
    w_cat,
    main_sum,
    late,
    own_sum,
    core_out,
    core_in,
    z_out,
    z_in,
    relay,
    local_sem,
    local_w_sem,
    main_send,
    main_recv,
    w_send,
    w_recv,
    o_send,
    o_recv,
    x_send,
    x_recv,
    xe_send,
    xe_recv,
    core_send,
    core_recv,
    z_send,
    z_recv,
    relay_recv,
):
    me = lax.axis_index("seq")
    tp = lax.axis_index("tp")
    heads = w_ref.shape[0]
    blocks, rows, _ = q_ref.shape
    size = n * rows
    base, extra = heads // n, heads % n
    share = out_ref.shape[2]
    core = lax.rem(tp, 2)
    chip = lax.div(tp, 2)
    core_mate = tp + 1 - 2 * core
    chip_mate = lax.rem(tp + 2, 4)
    shift = lax.rem(tp * extra, n)
    peers = [lax.rem(me + k, n) for k in range(n)]

    def extra_rank(rank):
        return lax.rem(rank - shift + n, n)

    barrier = pltpu.get_barrier_semaphore()
    for k in range(1, n):
        pl.semaphore_signal(
            barrier, inc=1, device_id={"seq": peers[k]}, device_id_type=MESH
        )
    for mate in (core_mate, chip_mate):
        pl.semaphore_signal(barrier, inc=1, device_id={"tp": mate}, device_id_type=MESH)
    pl.semaphore_wait(barrier, n + 1)

    pairs = ((k_ref, k_buf), (q_ref, q_buf), (v_ref, v_buf))

    def column(rank, slot):
        head = rank * base + slot if slot < base else n * base + extra_rank(rank)
        return pl.ds(pl.multiple_of(head * size, size), size)

    def qkv_copy(item, k):
        slot, i = item
        source, buf = pairs[i]
        return pltpu.make_async_remote_copy(
            src_ref=source.at[:, :, column(peers[k], slot)],
            dst_ref=buf.at[slot, me],
            send_sem=main_send.at[slot, i, k],
            recv_sem=main_recv.at[slot, i, k],
            device_id={"seq": peers[k]},
            device_id_type=MESH,
        )

    def qkv_start(item, k):
        if item[0] < base:
            qkv_copy(item, k).start()
        else:

            @pl.when(extra_rank(peers[k]) < extra)
            def _():
                qkv_copy(item, k).start()

    def qkv_wait_send(item, k):
        if item[0] < base:
            qkv_copy(item, k).wait_send()
        else:

            @pl.when(extra_rank(peers[k]) < extra)
            def _():
                qkv_copy(item, k).wait_send()

    def qkv_wait_recv(slot):
        for i in range(3):
            local_copy(slot, i).wait()
            for k in near:
                there = pairs[i][1].at[slot, me]
                pltpu.make_async_remote_copy(
                    src_ref=there,
                    dst_ref=there,
                    send_sem=main_send.at[slot, i, k],
                    recv_sem=main_recv.at[slot, i, k],
                    device_id={"seq": peers[k]},
                    device_id_type=MESH,
                ).wait_recv()

    def local_copy(slot, i):
        source, buf = pairs[i]
        return pltpu.make_async_copy(
            source.at[:, :, column(me, slot)], buf.at[slot, me], local_sem.at[slot, i]
        )

    has_extra = extra_rank(me) < extra
    order = sorted(range(1, n), key=lambda k: -min(k, n - k))
    near = order[::-1]
    slots = base + 1 if extra else base
    items = [(slot, i) for slot in range(slots) for i in range(3)]
    window = 4
    sent = [0]

    def advance(count):
        for _ in range(count):
            old = sent[0]
            sent[0] += 1
            for k in near:
                qkv_wait_send(items[old], k)
                if old + window < len(items):
                    qkv_start(items[old + window], k)

    for item in items[:window]:
        for k in order:
            qkv_start(item, k)

    def w_columns(to_chip, half):
        which = core if half == 0 else 1 - core
        return pl.ds(pl.multiple_of((to_chip * 2 + which) * share, size), share)

    full = n * base
    spots = [(0, full, 0, full)]
    if extra:
        spots.append((full, extra, 2 * full, 2 * full + extra))
    w_copies = []
    for part, (first, count, _, there) in enumerate(spots):
        for half in range(2):
            w_copies.append(
                pltpu.make_async_remote_copy(
                    src_ref=w_ref.at[pl.ds(first, count), :, w_columns(1 - chip, half)],
                    dst_ref=w_cat.at[pl.ds(there, count), :, pl.ds(half * share, share)],
                    send_sem=w_send.at[part, half],
                    recv_sem=w_recv.at[part, half],
                    device_id={"tp": chip_mate},
                    device_id_type=MESH,
                )
            )
            w_copies[-1].start()
    locals_w = []
    for slot in range(base):
        for i in range(3):
            local_copy(slot, i).start()

    if extra:

        @pl.when(has_extra)
        def _():
            for i in range(3):
                local_copy(base, i).start()

    for part, (first, count, here, _) in enumerate(spots):
        for half in range(2):
            locals_w.append(
                pltpu.make_async_copy(
                    w_ref.at[pl.ds(first, count), :, w_columns(chip, half)],
                    w_cat.at[pl.ds(here, count), :, pl.ds(half * share, share)],
                    local_w_sem.at[part, half],
                )
            )
            locals_w[-1].start()

    span = n * size
    row_id = lax.broadcasted_iota(jnp.int32, (span, span), 0)
    col_id = lax.broadcasted_iota(jnp.int32, (span, span), 1)
    outer, inside = lax.div(row_id, size), lax.rem(row_id, size)
    goal = lax.div(inside, rows) * size + outer * rows + lax.rem(inside, rows)
    swap[...] = jnp.where(goal == col_id, 1.0, 0.0).astype(jnp.bfloat16)

    token_total = n * blocks * rows
    key_block = lax.rem(
        lax.div(lax.broadcasted_iota(jnp.int32, (1, token_total), 1), rows), blocks
    )
    rate = float(size ** (-0.5) * np.log2(np.e))

    def head_bias(head):
        is_head = lax.broadcasted_iota(jnp.int32, mask_ref.shape, 2) == head
        live = jnp.where(is_head, mask_ref[...], 0).astype(jnp.float32)
        live = jnp.sum(live, axis=2, keepdims=True)
        allowed = jnp.zeros((blocks, token_total), jnp.float32)
        for other in range(blocks):
            allowed = jnp.where(key_block == other, live[:, other, :], allowed)
        return jnp.where(allowed > 0.5, 0.0, -jnp.inf)

    def blend(query, keys, values, bias):
        scores = lax.dot_general(
            query, keys, (((1,), (1,)), ((), ())), preferred_element_type=jnp.float32
        )
        scores = scores + bias
        largest = jnp.max(scores, axis=1, keepdims=True)
        weights = jnp.exp2((scores - largest) * rate)
        totals = jnp.sum(weights, axis=1, keepdims=True)
        blended = jnp.dot(
            weights.astype(jnp.bfloat16), values, preferred_element_type=jnp.float32
        )
        return (blended / totals).astype(jnp.bfloat16)

    def swapped(pieces):
        return jnp.dot(
            jnp.concatenate(pieces, axis=1), swap[...], preferred_element_type=jnp.float32
        ).astype(jnp.bfloat16)

    my_columns = pl.ds(pl.multiple_of(me * size, size), size)

    def peer_columns(k):
        return pl.ds(pl.multiple_of(peers[k] * size, size), size)

    my_extra = extra_rank(me)

    def place_of(slot):
        return me * base + slot if slot < base else 2 * full + my_extra

    def o_copy(slot, k):
        return pltpu.make_async_remote_copy(
            src_ref=o_buf.at[slot, :, peer_columns(k)],
            dst_ref=feat.at[place_of(slot)],
            send_sem=o_send.at[slot, k],
            recv_sem=o_recv.at[slot, k],
            device_id={"seq": peers[k]},
            device_id_type=MESH,
        )

    def x_copy(head):
        return pltpu.make_async_remote_copy(
            src_ref=feat.at[head],
            dst_ref=feat.at[full + head],
            send_sem=x_send.at[head],
            recv_sem=x_recv.at[head],
            device_id={"tp": chip_mate},
            device_id_type=MESH,
        )

    def xe_copy(j):
        return pltpu.make_async_remote_copy(
            src_ref=feat.at[2 * full + j],
            dst_ref=feat.at[2 * full + extra + j],
            send_sem=xe_send.at[j],
            recv_sem=xe_recv.at[j],
            device_id={"tp": chip_mate},
            device_id_type=MESH,
        )

    def attend(slot, head):
        keys = k_buf[slot].reshape(token_total, size)
        values = v_buf[slot].reshape(token_total, size)
        bias = head_bias(head)
        o_buf[slot] = swapped(
            [
                blend(
                    q_buf[slot, :, block].reshape(n * rows, size),
                    keys,
                    values,
                    bias[block : block + 1, :],
                )
                for block in range(blocks)
            ]
        )
        for k in order:
            o_copy(slot, k).start()
        feat[place_of(slot)] = o_buf[slot, :, my_columns]

    def forward(j):
        for k in near:
            o_copy(j, k).wait_recv()
            x_copy(lax.rem(me + n - k, n) * base + j).start()

    for j in range(base):
        advance(3 if j == 0 else min(2, len(items) - window - 3))
        qkv_wait_recv(j)
        attend(j, me * base + j)
        x_copy(me * base + j).start()
        if j >= 1:
            forward(j - 1)
    if extra:

        @pl.when(has_extra)
        def _():
            qkv_wait_recv(base)
            attend(base, full + my_extra)
            xe_copy(my_extra).start()

    forward(base - 1)
    for j in range(extra):
        owner = lax.rem(shift + j, n)

        @pl.when(owner != me)
        def _():
            gap = lax.rem(me - owner + n, n)
            there = feat.at[2 * full + j]
            pltpu.make_async_remote_copy(
                src_ref=there,
                dst_ref=there,
                send_sem=o_send.at[base, gap],
                recv_sem=o_recv.at[base, gap],
                device_id={"seq": owner},
                device_id_type=MESH,
            ).wait_recv()
            xe_copy(j).start()

    for head in range(full):
        x_copy(head).wait_recv()
    for copy in locals_w:
        copy.wait()
    for copy in w_copies:
        copy.wait_recv()
    groups = 2 * base
    tokens = blocks * rows

    def strip_order(pieces):
        wide = [jnp.concatenate(p, axis=1) for p in pieces]
        return jnp.concatenate(
            [wide[b][r * rows : (r + 1) * rows] for r in range(n) for b in range(blocks)],
            axis=0,
        )

    def cut_blocks(mixes):
        return [[m[:, b * size : (b + 1) * size] for m in mixes] for b in range(blocks)]

    taken = strip_order(
        cut_blocks([swapped([feat[g * n + a] for a in range(n)]) for g in range(groups)])
    )
    deep = 2 * full * rows
    for half in range(2):
        main_sum[half] = jnp.dot(
            taken,
            w_cat[: 2 * full, :, half * share : (half + 1) * share].reshape(deep, share),
            preferred_element_type=jnp.float32,
        ).reshape(n, tokens, share)
    if extra:
        for j in range(extra):
            xe_copy(j).wait_recv()
        late[...] = strip_order(
            cut_blocks([swapped([feat[2 * full + a] for a in range(2 * extra)])])
        ).reshape(n, tokens, size)

    half_n = n // 2
    left = me < half_n
    firsts = [jnp.where(left, half_n, 0), jnp.where(left, 0, half_n)]

    def core_copy(batch):
        there = pl.ds(batch * half_n, half_n)
        return pltpu.make_async_remote_copy(
            src_ref=core_out.at[there],
            dst_ref=core_in.at[there],
            send_sem=core_send.at[batch],
            recv_sem=core_recv.at[batch],
            device_id={"tp": core_mate},
            device_id_type=MESH,
        )

    half_mate = me + 1 - 2 * lax.rem(me, 2)
    at_end = jnp.logical_or(me == 0, me == n - 1)
    far = [firsts[0] + t for t in range(half_n)]
    my_spot = half_n + lax.rem(me, half_n)
    mate_spot = half_n + lax.rem(half_mate, half_n)
    piece = tokens // 2

    def part_of(p):
        return pl.ds(p * piece, piece)

    def relay_copy(t, p):
        return pltpu.make_async_remote_copy(
            src_ref=z_out.at[t, part_of(p)],
            dst_ref=relay.at[t, part_of(p)],
            send_sem=z_send.at[t, p],
            recv_sem=relay_recv.at[t, p],
            device_id={"seq": half_mate},
            device_id_type=MESH,
        )

    def far_copy(t, p):
        return pltpu.make_async_remote_copy(
            src_ref=z_out.at[t, part_of(p)],
            dst_ref=z_in.at[0, part_of(p)],
            send_sem=z_send.at[t, p],
            recv_sem=z_recv.at[0, p],
            device_id={"seq": far[t]},
            device_id_type=MESH,
        )

    def near_copy():
        return pltpu.make_async_remote_copy(
            src_ref=z_out.at[half_n],
            dst_ref=z_in.at[1],
            send_sem=z_send.at[half_n, 0],
            recv_sem=z_recv.at[1, 0],
            device_id={"seq": half_mate},
            device_id_type=MESH,
        )

    def batch_sum(batch, half):
        chosen = pl.ds(firsts[batch], half_n)
        found = main_sum[half, chosen].reshape(half_n * tokens, share)
        if extra:
            found = found + jnp.dot(
                late[chosen].reshape(half_n * tokens, size),
                w_cat[2 * full :, :, half * share : (half + 1) * share].reshape(
                    2 * extra * rows, share
                ),
                preferred_element_type=jnp.float32,
            )
        return found.reshape(half_n, tokens, share)

    for batch in range(2):
        spot = slice(batch * half_n, (batch + 1) * half_n)
        core_out[spot] = batch_sum(batch, 1).astype(jnp.bfloat16)
        core_copy(batch).start()
    for batch in range(2):
        spot = slice(batch * half_n, (batch + 1) * half_n)
        own_sum[spot] = batch_sum(batch, 0)
    core_copy(0).wait_recv()

    @pl.when(at_end)
    def _():
        for t in range(half_n):
            z_out[t] = (own_sum[t] + core_in[t].astype(jnp.float32)).astype(jnp.bfloat16)
            for p in range(2):
                relay_copy(t, p).start()

    core_copy(1).wait_recv()
    z_out[half_n] = (
        own_sum[mate_spot] + core_in[mate_spot].astype(jnp.float32)
    ).astype(jnp.bfloat16)
    near_copy().start()

    @pl.when(jnp.logical_not(at_end))
    def _():
        for t in range(half_n):
            for p in range(2):
                relay_copy(t, p).wait_recv()
                joint = own_sum[t, part_of(p)] + core_in[t, part_of(p)].astype(jnp.float32)
                z_out[t, part_of(p)] = (
                    joint + relay[t, part_of(p)].astype(jnp.float32)
                ).astype(jnp.bfloat16)
                far_copy(t, p).start()

    mine = own_sum[my_spot] + core_in[my_spot].astype(jnp.float32)
    near_copy().wait_recv()
    for p in range(2):
        far_copy(0, p).wait_recv()
    result = mine + z_in[1].astype(jnp.float32) + z_in[0].astype(jnp.float32)
    out_ref[...] = result.astype(jnp.bfloat16).reshape(blocks, rows, share)
    near_copy().wait_send()
    for t in range(half_n):
        for p in range(2):
            relay_copy(t, p).wait_send()

    while sent[0] < len(items):
        advance(1)
    for k in order:
        for j in range(base):
            o_copy(j, k).wait_send()
        if extra:

            @pl.when(has_extra)
            def _():
                o_copy(base, k).wait_send()

    for copy in w_copies:
        copy.wait_send()
    for head in range(full):
        x_copy(head).wait_send()
    for j in range(extra):
        xe_copy(j).wait_send()
    for batch in range(2):
        core_copy(batch).wait_send()


def fused_body(queries, key_vectors, value_vectors, block_mask, out_weight):
    n = lax.axis_size("seq")
    blocks, rows, _ = queries.shape
    heads = block_mask.shape[0]
    size = n * rows
    base, extra = heads // n, heads % n
    share = out_weight.shape[2] // lax.axis_size("tp")
    kind = jnp.bfloat16
    dma = pltpu.SemaphoreType.DMA
    whole = pl.BlockSpec(memory_space=pl.ANY)
    return pl.pallas_call(
        functools.partial(fused_kernel, n),
        out_shape=jax.ShapeDtypeStruct((blocks, rows, share), kind),
        in_specs=[whole, whole, whole, pl.BlockSpec(memory_space=pltpu.VMEM), whole],
        out_specs=pl.BlockSpec(memory_space=pltpu.VMEM),
        scratch_shapes=[pltpu.VMEM((base + 1, n, blocks, rows, size), kind)] * 3
        + [
            pltpu.VMEM((n * size, n * size), kind),
            pltpu.VMEM((base + 1, size, n * size), kind),
            pltpu.VMEM((2 * heads, size, size), kind),
            pltpu.VMEM((2 * heads, rows, 2 * share), kind),
            pltpu.VMEM((2, n, blocks * rows, share), jnp.float32),
            pltpu.VMEM((n, blocks * rows, size), kind),
            pltpu.VMEM((n, blocks * rows, share), jnp.float32),
        ]
        + [pltpu.VMEM((n, blocks * rows, share), kind)] * 5
        + [dma((base + 1, 3))]
        + [dma((2, 2))]
        + [dma((base + 1, 3, n))] * 2
        + [dma((2, 2))] * 2
        + [dma((base + 1, n))] * 2
        + [dma((n * base,))] * 2
        + [dma((extra + 1,))] * 2
        + [dma((n,))] * 2
        + [dma((n, 2))] * 3,
        compiler_params=pltpu.CompilerParams(
            collective_id=0, has_side_effects=True, vmem_limit_bytes=60 * 1024 * 1024
        ),
    )(queries, key_vectors, value_vectors, block_mask.transpose(1, 2, 0), out_weight)


def body(queries, key_vectors, value_vectors, block_mask, out_weight):
    n, tp = lax.axis_size("seq"), lax.axis_size("tp")
    blocks, rows, features = queries.shape
    heads = block_mask.shape[0]
    size = features // heads
    share = out_weight.shape[2] // tp
    fits = (
        n // 2 == 2
        and n % 2 == 0
        and tp // 2 == 2
        and tp % 2 == 0
        and blocks == n
        and rows % 16 == 0
        and size == n * rows
        and size % 128 == 0
        and share % size == 0
        and heads // n > 0
        and 2 * (heads % n) in (0, n)
    )
    if fits:
        return fused_body(queries, key_vectors, value_vectors, block_mask, out_weight)
    return plain_body(queries, key_vectors, value_vectors, block_mask, out_weight)


def solution(mesh):
    return jax.shard_map(
        body,
        mesh=mesh,
        in_specs=(
            P("groups", "seq", "tp"),
            P("groups", "seq", "tp"),
            P("groups", "seq", "tp"),
            P("tp", None, None),
            P("tp", "seq", None),
        ),
        out_specs=P("groups", "seq", "tp"),
        check_vma=False,
    )
```

```python
import functools

import jax
import jax.numpy as jnp
import numpy as np
from jax import lax
from jax.experimental import pallas as pl
from jax.experimental.pallas import tpu as pltpu
from jax.sharding import PartitionSpec as P

MESH = pl.DeviceIdType.MESH

KEYS = 28


def strip_tables(heads_local, blocks, slot_total):
    slot_ids = np.arange(slot_total)
    head_of = slot_ids * heads_local // slot_total
    per_head = np.bincount(head_of, minlength=heads_local)
    head_begin = np.cumsum(per_head) - per_head
    order_in_head = slot_ids - head_begin[head_of]
    head_share = per_head[head_of]
    first_block = order_in_head * blocks // head_share
    block_count = (order_in_head + 1) * blocks // head_share - first_block
    return (head_of, first_block, block_count)


def plain_body(queries, key_vectors, value_vectors, block_mask, out_weight):
    rank_count = lax.axis_size("seq")
    my_rank = lax.axis_index("seq")
    block_total, row_share, feature_width = queries.shape
    heads_local = block_mask.shape[0]
    head_size = feature_width // heads_local
    block_rows = row_share * rank_count
    per_rank = (heads_local + rank_count - 1) // rank_count
    slot_total = rank_count * per_rank
    least_share = slot_total // heads_local
    strip_cap = ((block_total + least_share - 1) // least_share + 1) // 2 * 2
    key_cap = min(KEYS, block_total)
    head_of, first_block, block_count = strip_tables(heads_local, block_total, slot_total)
    slot_grid = np.arange(slot_total).reshape(rank_count, per_rank).T
    paired = jnp.concatenate(
        [
            key_vectors.reshape(block_total, row_share, heads_local, head_size),
            value_vectors.reshape(block_total, row_share, heads_local, head_size),
        ],
        axis=3,
    )
    send_heads = jnp.asarray(head_of[slot_grid].reshape(-1), jnp.int32)
    chosen = jnp.take(paired, send_heads, axis=2)
    chosen = chosen.reshape(block_total, row_share, per_rank, rank_count, 2 * head_size)
    outgoing_pairs = chosen.transpose(2, 0, 3, 1, 4).reshape(
        per_rank, block_total, block_rows, 2 * head_size
    )
    flat_queries = queries.reshape(block_total, row_share, heads_local, head_size).transpose(
        0, 2, 1, 3
    )
    flat_queries = flat_queries.reshape(block_total * heads_local, row_share, head_size)
    positions = np.arange(strip_cap)
    unit_block = first_block[slot_grid][:, None, :] + positions[None, :, None]
    is_live = positions[None, :, None] < block_count[slot_grid][:, None, :]
    unit_index = np.where(is_live, unit_block * heads_local + head_of[slot_grid][:, None, :], 0)
    picked = jnp.take(flat_queries, jnp.asarray(unit_index.reshape(-1), jnp.int32), axis=0)
    picked = jnp.where(
        jnp.asarray(is_live.reshape(-1))[:, None, None], picked, jnp.zeros_like(picked)
    )
    outgoing_queries = picked.reshape(per_rank, strip_cap, block_rows, head_size)
    strip_queries, strip_pairs = (
        lax.all_to_all(outgoing_queries, "seq", split_axis=2, concat_axis=2, tiled=True),
        lax.all_to_all(outgoing_pairs, "seq", split_axis=2, concat_axis=2, tiled=True),
    )
    my_slots = my_rank * per_rank + jnp.arange(per_rank, dtype=jnp.int32)
    my_heads = jnp.asarray(head_of, jnp.int32)[my_slots]
    my_first = jnp.asarray(first_block, jnp.int32)[my_slots]
    query_blocks = jnp.minimum(
        my_first[:, None] + jnp.arange(strip_cap, dtype=jnp.int32)[None, :], block_total - 1
    )
    mask_rows = block_mask[my_heads[:, None], query_blocks]
    column_ids = jnp.arange(block_total, dtype=jnp.int32)
    ranking = (1 - mask_rows) * block_total + column_ids
    key_pick = jnp.argsort(ranking, axis=-1)[..., :key_cap]
    key_live = jnp.take_along_axis(mask_rows, key_pick, axis=-1)
    group_total = per_rank * strip_cap // 2
    query_groups = strip_queries.reshape(group_total, 2, block_rows, head_size)
    pick_groups = key_pick.reshape(group_total, 2, key_cap)
    live_groups = key_live.reshape(group_total, 2, key_cap)
    slot_of_group = jnp.arange(group_total, dtype=jnp.int32) // (strip_cap // 2)
    score_scale = head_size ** (-0.5)

    def attend_group(inputs):
        query_tile, pick_tile, live_tile, slot_index = inputs
        pairs_here = strip_pairs[slot_index]
        gathered = pairs_here[pick_tile]
        scores = (
            jnp.einsum(
                "qid,qkjd->qikj",
                query_tile,
                gathered[..., :head_size],
                preferred_element_type=jnp.float32,
            )
            * score_scale
        )
        allowed = (live_tile > 0)[:, None, :, None]
        scores = jnp.where(allowed, scores, -jnp.inf)
        largest = jnp.max(scores, axis=(2, 3), keepdims=True)
        weights = jnp.exp(scores - largest)
        totals = jnp.sum(weights, axis=(2, 3))
        blended = jnp.einsum(
            "qikj,qkjd->qid",
            weights.astype(jnp.bfloat16),
            gathered[..., head_size:],
            preferred_element_type=jnp.float32,
        )
        return (blended / totals[..., None]).astype(jnp.bfloat16)

    strip_out = lax.map(attend_group, (query_groups, pick_groups, live_groups, slot_of_group))
    outgoing_out = strip_out.reshape(per_rank, strip_cap, block_rows, head_size)
    returned = lax.all_to_all(outgoing_out, "seq", split_axis=2, concat_axis=2, tiled=True)
    slot_mesh, step_mesh = np.meshgrid(np.arange(slot_total), positions, indexing="ij")
    live_slot = step_mesh < block_count[slot_mesh]
    placement_index = np.zeros((block_total, heads_local), np.int64)
    source_index = (
        slot_mesh % per_rank * strip_cap + step_mesh
    ) * rank_count + slot_mesh // per_rank
    placement_index[
        first_block[slot_mesh][live_slot] + step_mesh[live_slot], head_of[slot_mesh][live_slot]
    ] = source_index[live_slot]
    flat_back = returned.reshape(per_rank * strip_cap * rank_count, row_share, head_size)
    own_out = jnp.take(flat_back, jnp.asarray(placement_index.reshape(-1), jnp.int32), axis=0)
    own_out = own_out.reshape(block_total, heads_local, row_share, head_size)
    token_total = block_total * row_share
    token_out = own_out.transpose(0, 2, 1, 3).reshape(token_total, heads_local, head_size)
    partial_sum = jnp.einsum(
        "thd,hdo->to",
        token_out,
        lax.all_gather(out_weight, "seq", axis=1, tiled=True),
        preferred_element_type=jnp.float32,
    )
    summed = lax.psum_scatter(
        partial_sum.astype(jnp.bfloat16), "tp", scatter_dimension=1, tiled=True
    ).astype(jnp.float32)
    return summed.astype(jnp.bfloat16).reshape(block_total, row_share, summed.shape[1])


def fused_kernel(
    n,
    q_ref,
    k_ref,
    v_ref,
    mask_ref,
    w_ref,
    out_ref,
    q_buf,
    k_buf,
    v_buf,
    swap,
    o_buf,
    feat,
    w_cat,
    main_sum,
    late,
    own_sum,
    core_out,
    core_in,
    z_out,
    z_in,
    relay,
    local_sem,
    local_w_sem,
    main_send,
    main_recv,
    w_send,
    w_recv,
    o_send,
    o_recv,
    x_send,
    x_recv,
    xe_send,
    xe_recv,
    core_send,
    core_recv,
    z_send,
    z_recv,
    relay_recv,
):
    me = lax.axis_index("seq")
    tp = lax.axis_index("tp")
    heads = w_ref.shape[0]
    blocks, rows, _ = q_ref.shape
    size = n * rows
    base, extra = heads // n, heads % n
    share = out_ref.shape[2]
    core = lax.rem(tp, 2)
    chip = lax.div(tp, 2)
    core_mate = tp + 1 - 2 * core
    chip_mate = lax.rem(tp + 2, 4)
    shift = lax.rem(tp * extra, n)
    peers = [lax.rem(me + k, n) for k in range(n)]

    def extra_rank(rank):
        return lax.rem(rank - shift + n, n)

    barrier = pltpu.get_barrier_semaphore()
    for k in range(1, n):
        pl.semaphore_signal(
            barrier, inc=1, device_id={"seq": peers[k]}, device_id_type=MESH
        )
    for mate in (core_mate, chip_mate):
        pl.semaphore_signal(barrier, inc=1, device_id={"tp": mate}, device_id_type=MESH)
    pl.semaphore_wait(barrier, n + 1)

    pairs = ((k_ref, k_buf), (q_ref, q_buf), (v_ref, v_buf))

    def column(rank, slot):
        head = rank * base + slot if slot < base else n * base + extra_rank(rank)
        return pl.ds(pl.multiple_of(head * size, size), size)

    def qkv_copy(item, k):
        slot, i = item
        source, buf = pairs[i]
        return pltpu.make_async_remote_copy(
            src_ref=source.at[:, :, column(peers[k], slot)],
            dst_ref=buf.at[slot, me],
            send_sem=main_send.at[slot, i, k],
            recv_sem=main_recv.at[slot, i, k],
            device_id={"seq": peers[k]},
            device_id_type=MESH,
        )

    def qkv_start(item, k):
        if item[0] < base:
            qkv_copy(item, k).start()
        else:

            @pl.when(extra_rank(peers[k]) < extra)
            def _():
                qkv_copy(item, k).start()

    def qkv_wait_send(item, k):
        if item[0] < base:
            qkv_copy(item, k).wait_send()
        else:

            @pl.when(extra_rank(peers[k]) < extra)
            def _():
                qkv_copy(item, k).wait_send()

    def qkv_wait_recv(slot):
        for i in range(3):
            local_copy(slot, i).wait()
            for k in near:
                there = pairs[i][1].at[slot, me]
                pltpu.make_async_remote_copy(
                    src_ref=there,
                    dst_ref=there,
                    send_sem=main_send.at[slot, i, k],
                    recv_sem=main_recv.at[slot, i, k],
                    device_id={"seq": peers[k]},
                    device_id_type=MESH,
                ).wait_recv()

    def local_copy(slot, i):
        source, buf = pairs[i]
        return pltpu.make_async_copy(
            source.at[:, :, column(me, slot)], buf.at[slot, me], local_sem.at[slot, i]
        )

    has_extra = extra_rank(me) < extra
    order = sorted(range(1, n), key=lambda k: -min(k, n - k))
    near = order[::-1]
    slots = base + 1 if extra else base
    items = [(slot, i) for slot in range(slots) for i in range(3)]
    window = len(items)
    sent = [0]

    def advance(count):
        for _ in range(count):
            old = sent[0]
            sent[0] += 1
            for k in near:
                qkv_wait_send(items[old], k)
                if old + window < len(items):
                    qkv_start(items[old + window], k)

    for item in items[:window]:
        for k in order:
            qkv_start(item, k)

    def w_columns(to_chip, half):
        which = core if half == 0 else 1 - core
        return pl.ds(pl.multiple_of((to_chip * 2 + which) * share, size), share)

    full = n * base
    spots = [(0, full, 0, full)]
    if extra:
        spots.append((full, extra, 2 * full, 2 * full + extra))
    w_copies = []
    for part, (first, count, _, there) in enumerate(spots):
        for half in range(2):
            w_copies.append(
                pltpu.make_async_remote_copy(
                    src_ref=w_ref.at[pl.ds(first, count), :, w_columns(1 - chip, half)],
                    dst_ref=w_cat.at[pl.ds(there, count), :, pl.ds(half * share, share)],
                    send_sem=w_send.at[part, half],
                    recv_sem=w_recv.at[part, half],
                    device_id={"tp": chip_mate},
                    device_id_type=MESH,
                )
            )
            w_copies[-1].start()
    locals_w = []
    for slot in range(base):
        for i in range(3):
            local_copy(slot, i).start()

    if extra:

        @pl.when(has_extra)
        def _():
            for i in range(3):
                local_copy(base, i).start()

    for part, (first, count, here, _) in enumerate(spots):
        for half in range(2):
            locals_w.append(
                pltpu.make_async_copy(
                    w_ref.at[pl.ds(first, count), :, w_columns(chip, half)],
                    w_cat.at[pl.ds(here, count), :, pl.ds(half * share, share)],
                    local_w_sem.at[part, half],
                )
            )
            locals_w[-1].start()

    span = n * size
    row_id = lax.broadcasted_iota(jnp.int32, (span, span), 0)
    col_id = lax.broadcasted_iota(jnp.int32, (span, span), 1)
    outer, inside = lax.div(row_id, size), lax.rem(row_id, size)
    goal = lax.div(inside, rows) * size + outer * rows + lax.rem(inside, rows)
    swap[...] = jnp.where(goal == col_id, 1.0, 0.0).astype(jnp.bfloat16)

    token_total = n * blocks * rows
    key_block = lax.rem(
        lax.div(lax.broadcasted_iota(jnp.int32, (1, token_total), 1), rows), blocks
    )
    rate = float(size ** (-0.5) * np.log2(np.e))

    def head_bias(head):
        is_head = lax.broadcasted_iota(jnp.int32, mask_ref.shape, 2) == head
        live = jnp.where(is_head, mask_ref[...], 0).astype(jnp.float32)
        live = jnp.sum(live, axis=2, keepdims=True)
        allowed = jnp.zeros((blocks, token_total), jnp.float32)
        for other in range(blocks):
            allowed = jnp.where(key_block == other, live[:, other, :], allowed)
        return jnp.where(allowed > 0.5, 0.0, -jnp.inf)

    def blend(query, keys, values, bias):
        scores = lax.dot_general(
            query, keys, (((1,), (1,)), ((), ())), preferred_element_type=jnp.float32
        )
        scores = scores + bias
        largest = jnp.max(scores, axis=1, keepdims=True)
        weights = jnp.exp2((scores - largest) * rate)
        totals = jnp.sum(weights, axis=1, keepdims=True)
        blended = jnp.dot(
            weights.astype(jnp.bfloat16), values, preferred_element_type=jnp.float32
        )
        return (blended / totals).astype(jnp.bfloat16)

    def swapped(pieces):
        return jnp.dot(
            jnp.concatenate(pieces, axis=1), swap[...], preferred_element_type=jnp.float32
        ).astype(jnp.bfloat16)

    my_columns = pl.ds(pl.multiple_of(me * size, size), size)

    def peer_columns(k):
        return pl.ds(pl.multiple_of(peers[k] * size, size), size)

    my_extra = extra_rank(me)

    def place_of(slot):
        return me * base + slot if slot < base else 2 * full + my_extra

    def o_copy(slot, k):
        return pltpu.make_async_remote_copy(
            src_ref=o_buf.at[slot, :, peer_columns(k)],
            dst_ref=feat.at[place_of(slot)],
            send_sem=o_send.at[slot, k],
            recv_sem=o_recv.at[slot, k],
            device_id={"seq": peers[k]},
            device_id_type=MESH,
        )

    def x_copy(head):
        return pltpu.make_async_remote_copy(
            src_ref=feat.at[head],
            dst_ref=feat.at[full + head],
            send_sem=x_send.at[head],
            recv_sem=x_recv.at[head],
            device_id={"tp": chip_mate},
            device_id_type=MESH,
        )

    def xe_copy(j):
        return pltpu.make_async_remote_copy(
            src_ref=feat.at[2 * full + j],
            dst_ref=feat.at[2 * full + extra + j],
            send_sem=xe_send.at[j],
            recv_sem=xe_recv.at[j],
            device_id={"tp": chip_mate},
            device_id_type=MESH,
        )

    def attend(slot, head):
        keys = k_buf[slot].reshape(token_total, size)
        values = v_buf[slot].reshape(token_total, size)
        bias = head_bias(head)
        o_buf[slot] = swapped(
            [
                blend(
                    q_buf[slot, :, block].reshape(n * rows, size),
                    keys,
                    values,
                    bias[block : block + 1, :],
                )
                for block in range(blocks)
            ]
        )
        for k in order:
            o_copy(slot, k).start()
        feat[place_of(slot)] = o_buf[slot, :, my_columns]

    def forward(j):
        for k in near:
            o_copy(j, k).wait_recv()
            x_copy(lax.rem(me + n - k, n) * base + j).start()

    for j in range(base):
        advance(3 if j == 0 else min(2, len(items) - window - 3))
        qkv_wait_recv(j)
        attend(j, me * base + j)
        x_copy(me * base + j).start()
        if j >= 1:
            forward(j - 1)
    if extra:

        @pl.when(has_extra)
        def _():
            qkv_wait_recv(base)
            attend(base, full + my_extra)
            xe_copy(my_extra).start()

    forward(base - 1)
    for j in range(extra):
        owner = lax.rem(shift + j, n)

        @pl.when(owner != me)
        def _():
            gap = lax.rem(me - owner + n, n)
            there = feat.at[2 * full + j]
            pltpu.make_async_remote_copy(
                src_ref=there,
                dst_ref=there,
                send_sem=o_send.at[base, gap],
                recv_sem=o_recv.at[base, gap],
                device_id={"seq": owner},
                device_id_type=MESH,
            ).wait_recv()
            xe_copy(j).start()

    for head in range(full):
        x_copy(head).wait_recv()
    for copy in locals_w:
        copy.wait()
    for copy in w_copies:
        copy.wait_recv()
    groups = 2 * base
    tokens = blocks * rows

    def strip_order(pieces):
        wide = [jnp.concatenate(p, axis=1) for p in pieces]
        return jnp.concatenate(
            [wide[b][r * rows : (r + 1) * rows] for r in range(n) for b in range(blocks)],
            axis=0,
        )

    def cut_blocks(mixes):
        return [[m[:, b * size : (b + 1) * size] for m in mixes] for b in range(blocks)]

    taken = strip_order(
        cut_blocks([swapped([feat[g * n + a] for a in range(n)]) for g in range(groups)])
    )
    deep = 2 * full * rows
    for half in range(2):
        main_sum[half] = jnp.dot(
            taken,
            w_cat[: 2 * full, :, half * share : (half + 1) * share].reshape(deep, share),
            preferred_element_type=jnp.float32,
        ).reshape(n, tokens, share)
    if extra:
        for j in range(extra):
            xe_copy(j).wait_recv()
        late[...] = strip_order(
            cut_blocks([swapped([feat[2 * full + a] for a in range(2 * extra)])])
        ).reshape(n, tokens, size)

    half_n = n // 2
    left = me < half_n
    firsts = [jnp.where(left, half_n, 0), jnp.where(left, 0, half_n)]

    def core_copy(batch):
        there = pl.ds(batch * half_n, half_n)
        return pltpu.make_async_remote_copy(
            src_ref=core_out.at[there],
            dst_ref=core_in.at[there],
            send_sem=core_send.at[batch],
            recv_sem=core_recv.at[batch],
            device_id={"tp": core_mate},
            device_id_type=MESH,
        )

    half_mate = me + 1 - 2 * lax.rem(me, 2)
    at_end = jnp.logical_or(me == 0, me == n - 1)
    far = [firsts[0] + t for t in range(half_n)]
    my_spot = half_n + lax.rem(me, half_n)
    mate_spot = half_n + lax.rem(half_mate, half_n)
    piece = tokens // 2

    def part_of(p):
        return pl.ds(p * piece, piece)

    def relay_copy(t, p):
        return pltpu.make_async_remote_copy(
            src_ref=z_out.at[t, part_of(p)],
            dst_ref=relay.at[t, part_of(p)],
            send_sem=z_send.at[t, p],
            recv_sem=relay_recv.at[t, p],
            device_id={"seq": half_mate},
            device_id_type=MESH,
        )

    def far_copy(t, p):
        return pltpu.make_async_remote_copy(
            src_ref=z_out.at[t, part_of(p)],
            dst_ref=z_in.at[0, part_of(p)],
            send_sem=z_send.at[t, p],
            recv_sem=z_recv.at[0, p],
            device_id={"seq": far[t]},
            device_id_type=MESH,
        )

    def near_copy():
        return pltpu.make_async_remote_copy(
            src_ref=z_out.at[half_n],
            dst_ref=z_in.at[1],
            send_sem=z_send.at[half_n, 0],
            recv_sem=z_recv.at[1, 0],
            device_id={"seq": half_mate},
            device_id_type=MESH,
        )

    def batch_sum(batch, half):
        chosen = pl.ds(firsts[batch], half_n)
        found = main_sum[half, chosen].reshape(half_n * tokens, share)
        if extra:
            found = found + jnp.dot(
                late[chosen].reshape(half_n * tokens, size),
                w_cat[2 * full :, :, half * share : (half + 1) * share].reshape(
                    2 * extra * rows, share
                ),
                preferred_element_type=jnp.float32,
            )
        return found.reshape(half_n, tokens, share)

    for batch in range(2):
        spot = slice(batch * half_n, (batch + 1) * half_n)
        core_out[spot] = batch_sum(batch, 1).astype(jnp.bfloat16)
        core_copy(batch).start()
    for batch in range(2):
        spot = slice(batch * half_n, (batch + 1) * half_n)
        own_sum[spot] = batch_sum(batch, 0)
    core_copy(0).wait_recv()

    @pl.when(at_end)
    def _():
        for t in range(half_n):
            z_out[t] = (own_sum[t] + core_in[t].astype(jnp.float32)).astype(jnp.bfloat16)
            for p in range(2):
                relay_copy(t, p).start()

    core_copy(1).wait_recv()
    z_out[half_n] = (
        own_sum[mate_spot] + core_in[mate_spot].astype(jnp.float32)
    ).astype(jnp.bfloat16)
    near_copy().start()

    @pl.when(jnp.logical_not(at_end))
    def _():
        for t in range(half_n):
            for p in range(2):
                relay_copy(t, p).wait_recv()
                joint = own_sum[t, part_of(p)] + core_in[t, part_of(p)].astype(jnp.float32)
                z_out[t, part_of(p)] = (
                    joint + relay[t, part_of(p)].astype(jnp.float32)
                ).astype(jnp.bfloat16)
                far_copy(t, p).start()

    mine = own_sum[my_spot] + core_in[my_spot].astype(jnp.float32)
    near_copy().wait_recv()
    for p in range(2):
        far_copy(0, p).wait_recv()
    result = mine + z_in[1].astype(jnp.float32) + z_in[0].astype(jnp.float32)
    out_ref[...] = result.astype(jnp.bfloat16).reshape(blocks, rows, share)
    near_copy().wait_send()
    for t in range(half_n):
        for p in range(2):
            relay_copy(t, p).wait_send()

    while sent[0] < len(items):
        advance(1)
    for k in order:
        for j in range(base):
            o_copy(j, k).wait_send()
        if extra:

            @pl.when(has_extra)
            def _():
                o_copy(base, k).wait_send()

    for copy in w_copies:
        copy.wait_send()
    for head in range(full):
        x_copy(head).wait_send()
    for j in range(extra):
        xe_copy(j).wait_send()
    for batch in range(2):
        core_copy(batch).wait_send()


def fused_body(queries, key_vectors, value_vectors, block_mask, out_weight):
    n = lax.axis_size("seq")
    blocks, rows, _ = queries.shape
    heads = block_mask.shape[0]
    size = n * rows
    base, extra = heads // n, heads % n
    share = out_weight.shape[2] // lax.axis_size("tp")
    kind = jnp.bfloat16
    dma = pltpu.SemaphoreType.DMA
    whole = pl.BlockSpec(memory_space=pl.ANY)
    return pl.pallas_call(
        functools.partial(fused_kernel, n),
        out_shape=jax.ShapeDtypeStruct((blocks, rows, share), kind),
        in_specs=[whole, whole, whole, pl.BlockSpec(memory_space=pltpu.VMEM), whole],
        out_specs=pl.BlockSpec(memory_space=pltpu.VMEM),
        scratch_shapes=[pltpu.VMEM((base + 1, n, blocks, rows, size), kind)] * 3
        + [
            pltpu.VMEM((n * size, n * size), kind),
            pltpu.VMEM((base + 1, size, n * size), kind),
            pltpu.VMEM((2 * heads, size, size), kind),
            pltpu.VMEM((2 * heads, rows, 2 * share), kind),
            pltpu.VMEM((2, n, blocks * rows, share), jnp.float32),
            pltpu.VMEM((n, blocks * rows, size), kind),
            pltpu.VMEM((n, blocks * rows, share), jnp.float32),
        ]
        + [pltpu.VMEM((n, blocks * rows, share), kind)] * 5
        + [dma((base + 1, 3))]
        + [dma((2, 2))]
        + [dma((base + 1, 3, n))] * 2
        + [dma((2, 2))] * 2
        + [dma((base + 1, n))] * 2
        + [dma((n * base,))] * 2
        + [dma((extra + 1,))] * 2
        + [dma((n,))] * 2
        + [dma((n, 2))] * 3,
        compiler_params=pltpu.CompilerParams(
            collective_id=0, has_side_effects=True, vmem_limit_bytes=60 * 1024 * 1024
        ),
    )(queries, key_vectors, value_vectors, block_mask.transpose(1, 2, 0), out_weight)


def body(queries, key_vectors, value_vectors, block_mask, out_weight):
    n, tp = lax.axis_size("seq"), lax.axis_size("tp")
    blocks, rows, features = queries.shape
    heads = block_mask.shape[0]
    size = features // heads
    share = out_weight.shape[2] // tp
    fits = (
        n // 2 == 2
        and n % 2 == 0
        and tp // 2 == 2
        and tp % 2 == 0
        and blocks == n
        and rows % 16 == 0
        and size == n * rows
        and size % 128 == 0
        and share % size == 0
        and heads // n > 0
        and 2 * (heads % n) in (0, n)
    )
    if fits:
        return fused_body(queries, key_vectors, value_vectors, block_mask, out_weight)
    return plain_body(queries, key_vectors, value_vectors, block_mask, out_weight)


def solution(mesh):
    return jax.shard_map(
        body,
        mesh=mesh,
        in_specs=(
            P("groups", "seq", "tp"),
            P("groups", "seq", "tp"),
            P("groups", "seq", "tp"),
            P("tp", None, None),
            P("tp", "seq", None),
        ),
        out_specs=P("groups", "seq", "tp"),
        check_vma=False,
    )
```

```python
import functools

import jax
import jax.numpy as jnp
import numpy as np
from jax import lax
from jax.experimental import pallas as pl
from jax.experimental.pallas import tpu as pltpu
from jax.sharding import PartitionSpec as P

MESH = pl.DeviceIdType.MESH

KEYS = 28


def strip_tables(heads_local, blocks, slot_total):
    slot_ids = np.arange(slot_total)
    head_of = slot_ids * heads_local // slot_total
    per_head = np.bincount(head_of, minlength=heads_local)
    head_begin = np.cumsum(per_head) - per_head
    order_in_head = slot_ids - head_begin[head_of]
    head_share = per_head[head_of]
    first_block = order_in_head * blocks // head_share
    block_count = (order_in_head + 1) * blocks // head_share - first_block
    return (head_of, first_block, block_count)


def plain_body(queries, key_vectors, value_vectors, block_mask, out_weight):
    rank_count = lax.axis_size("seq")
    my_rank = lax.axis_index("seq")
    block_total, row_share, feature_width = queries.shape
    heads_local = block_mask.shape[0]
    head_size = feature_width // heads_local
    block_rows = row_share * rank_count
    per_rank = (heads_local + rank_count - 1) // rank_count
    slot_total = rank_count * per_rank
    least_share = slot_total // heads_local
    strip_cap = ((block_total + least_share - 1) // least_share + 1) // 2 * 2
    key_cap = min(KEYS, block_total)
    head_of, first_block, block_count = strip_tables(heads_local, block_total, slot_total)
    slot_grid = np.arange(slot_total).reshape(rank_count, per_rank).T
    paired = jnp.concatenate(
        [
            key_vectors.reshape(block_total, row_share, heads_local, head_size),
            value_vectors.reshape(block_total, row_share, heads_local, head_size),
        ],
        axis=3,
    )
    send_heads = jnp.asarray(head_of[slot_grid].reshape(-1), jnp.int32)
    chosen = jnp.take(paired, send_heads, axis=2)
    chosen = chosen.reshape(block_total, row_share, per_rank, rank_count, 2 * head_size)
    outgoing_pairs = chosen.transpose(2, 0, 3, 1, 4).reshape(
        per_rank, block_total, block_rows, 2 * head_size
    )
    flat_queries = queries.reshape(block_total, row_share, heads_local, head_size).transpose(
        0, 2, 1, 3
    )
    flat_queries = flat_queries.reshape(block_total * heads_local, row_share, head_size)
    positions = np.arange(strip_cap)
    unit_block = first_block[slot_grid][:, None, :] + positions[None, :, None]
    is_live = positions[None, :, None] < block_count[slot_grid][:, None, :]
    unit_index = np.where(is_live, unit_block * heads_local + head_of[slot_grid][:, None, :], 0)
    picked = jnp.take(flat_queries, jnp.asarray(unit_index.reshape(-1), jnp.int32), axis=0)
    picked = jnp.where(
        jnp.asarray(is_live.reshape(-1))[:, None, None], picked, jnp.zeros_like(picked)
    )
    outgoing_queries = picked.reshape(per_rank, strip_cap, block_rows, head_size)
    strip_queries, strip_pairs = (
        lax.all_to_all(outgoing_queries, "seq", split_axis=2, concat_axis=2, tiled=True),
        lax.all_to_all(outgoing_pairs, "seq", split_axis=2, concat_axis=2, tiled=True),
    )
    my_slots = my_rank * per_rank + jnp.arange(per_rank, dtype=jnp.int32)
    my_heads = jnp.asarray(head_of, jnp.int32)[my_slots]
    my_first = jnp.asarray(first_block, jnp.int32)[my_slots]
    query_blocks = jnp.minimum(
        my_first[:, None] + jnp.arange(strip_cap, dtype=jnp.int32)[None, :], block_total - 1
    )
    mask_rows = block_mask[my_heads[:, None], query_blocks]
    column_ids = jnp.arange(block_total, dtype=jnp.int32)
    ranking = (1 - mask_rows) * block_total + column_ids
    key_pick = jnp.argsort(ranking, axis=-1)[..., :key_cap]
    key_live = jnp.take_along_axis(mask_rows, key_pick, axis=-1)
    group_total = per_rank * strip_cap // 2
    query_groups = strip_queries.reshape(group_total, 2, block_rows, head_size)
    pick_groups = key_pick.reshape(group_total, 2, key_cap)
    live_groups = key_live.reshape(group_total, 2, key_cap)
    slot_of_group = jnp.arange(group_total, dtype=jnp.int32) // (strip_cap // 2)
    score_scale = head_size ** (-0.5)

    def attend_group(inputs):
        query_tile, pick_tile, live_tile, slot_index = inputs
        pairs_here = strip_pairs[slot_index]
        gathered = pairs_here[pick_tile]
        scores = (
            jnp.einsum(
                "qid,qkjd->qikj",
                query_tile,
                gathered[..., :head_size],
                preferred_element_type=jnp.float32,
            )
            * score_scale
        )
        allowed = (live_tile > 0)[:, None, :, None]
        scores = jnp.where(allowed, scores, -jnp.inf)
        largest = jnp.max(scores, axis=(2, 3), keepdims=True)
        weights = jnp.exp(scores - largest)
        totals = jnp.sum(weights, axis=(2, 3))
        blended = jnp.einsum(
            "qikj,qkjd->qid",
            weights.astype(jnp.bfloat16),
            gathered[..., head_size:],
            preferred_element_type=jnp.float32,
        )
        return (blended / totals[..., None]).astype(jnp.bfloat16)

    strip_out = lax.map(attend_group, (query_groups, pick_groups, live_groups, slot_of_group))
    outgoing_out = strip_out.reshape(per_rank, strip_cap, block_rows, head_size)
    returned = lax.all_to_all(outgoing_out, "seq", split_axis=2, concat_axis=2, tiled=True)
    slot_mesh, step_mesh = np.meshgrid(np.arange(slot_total), positions, indexing="ij")
    live_slot = step_mesh < block_count[slot_mesh]
    placement_index = np.zeros((block_total, heads_local), np.int64)
    source_index = (
        slot_mesh % per_rank * strip_cap + step_mesh
    ) * rank_count + slot_mesh // per_rank
    placement_index[
        first_block[slot_mesh][live_slot] + step_mesh[live_slot], head_of[slot_mesh][live_slot]
    ] = source_index[live_slot]
    flat_back = returned.reshape(per_rank * strip_cap * rank_count, row_share, head_size)
    own_out = jnp.take(flat_back, jnp.asarray(placement_index.reshape(-1), jnp.int32), axis=0)
    own_out = own_out.reshape(block_total, heads_local, row_share, head_size)
    token_total = block_total * row_share
    token_out = own_out.transpose(0, 2, 1, 3).reshape(token_total, heads_local, head_size)
    partial_sum = jnp.einsum(
        "thd,hdo->to",
        token_out,
        lax.all_gather(out_weight, "seq", axis=1, tiled=True),
        preferred_element_type=jnp.float32,
    )
    summed = lax.psum_scatter(
        partial_sum.astype(jnp.bfloat16), "tp", scatter_dimension=1, tiled=True
    ).astype(jnp.float32)
    return summed.astype(jnp.bfloat16).reshape(block_total, row_share, summed.shape[1])


def fused_kernel(
    n,
    q_ref,
    k_ref,
    v_ref,
    mask_ref,
    w_ref,
    out_ref,
    q_buf,
    k_buf,
    v_buf,
    swap,
    o_buf,
    feat,
    w_cat,
    main_sum,
    late,
    own_sum,
    core_out,
    core_in,
    z_out,
    z_in,
    relay,
    local_sem,
    local_w_sem,
    main_send,
    main_recv,
    w_send,
    w_recv,
    o_send,
    o_recv,
    x_send,
    x_recv,
    xe_send,
    xe_recv,
    core_send,
    core_recv,
    z_send,
    z_recv,
    relay_recv,
):
    me = lax.axis_index("seq")
    tp = lax.axis_index("tp")
    heads = w_ref.shape[0]
    blocks, rows, _ = q_ref.shape
    size = n * rows
    base, extra = heads // n, heads % n
    share = out_ref.shape[2]
    core = lax.rem(tp, 2)
    chip = lax.div(tp, 2)
    core_mate = tp + 1 - 2 * core
    chip_mate = lax.rem(tp + 2, 4)
    shift = lax.rem(tp * extra, n)
    peers = [lax.rem(me + k, n) for k in range(n)]

    def extra_rank(rank):
        return lax.rem(rank - shift + n, n)

    barrier = pltpu.get_barrier_semaphore()
    for k in range(1, n):
        pl.semaphore_signal(
            barrier, inc=1, device_id={"seq": peers[k]}, device_id_type=MESH
        )
    for mate in (core_mate, chip_mate):
        pl.semaphore_signal(barrier, inc=1, device_id={"tp": mate}, device_id_type=MESH)
    pl.semaphore_wait(barrier, n + 1)

    pairs = ((k_ref, k_buf), (q_ref, q_buf), (v_ref, v_buf))

    def column(rank, slot):
        head = rank * base + slot if slot < base else n * base + extra_rank(rank)
        return pl.ds(pl.multiple_of(head * size, size), size)

    def qkv_copy(item, k):
        slot, i = item
        source, buf = pairs[i]
        return pltpu.make_async_remote_copy(
            src_ref=source.at[:, :, column(peers[k], slot)],
            dst_ref=buf.at[slot, me],
            send_sem=main_send.at[slot, i, k],
            recv_sem=main_recv.at[slot, i, k],
            device_id={"seq": peers[k]},
            device_id_type=MESH,
        )

    def qkv_start(item, k):
        if item[0] < base:
            qkv_copy(item, k).start()
        else:

            @pl.when(extra_rank(peers[k]) < extra)
            def _():
                qkv_copy(item, k).start()

    def qkv_wait_send(item, k):
        if item[0] < base:
            qkv_copy(item, k).wait_send()
        else:

            @pl.when(extra_rank(peers[k]) < extra)
            def _():
                qkv_copy(item, k).wait_send()

    def qkv_wait_recv(slot):
        for i in range(3):
            local_copy(slot, i).wait()
            for k in near:
                there = pairs[i][1].at[slot, me]
                pltpu.make_async_remote_copy(
                    src_ref=there,
                    dst_ref=there,
                    send_sem=main_send.at[slot, i, k],
                    recv_sem=main_recv.at[slot, i, k],
                    device_id={"seq": peers[k]},
                    device_id_type=MESH,
                ).wait_recv()

    def local_copy(slot, i):
        source, buf = pairs[i]
        return pltpu.make_async_copy(
            source.at[:, :, column(me, slot)], buf.at[slot, me], local_sem.at[slot, i]
        )

    has_extra = extra_rank(me) < extra
    order = sorted(range(1, n), key=lambda k: -min(k, n - k))
    near = order[::-1]
    slots = base + 1 if extra else base
    items = [(slot, i) for slot in range(slots) for i in range(3)]
    window = len(items)
    sent = [0]

    def advance(count):
        for _ in range(count):
            old = sent[0]
            sent[0] += 1
            for k in near:
                qkv_wait_send(items[old], k)
                if old + window < len(items):
                    qkv_start(items[old + window], k)

    for item in items[:window]:
        for k in order:
            qkv_start(item, k)

    def w_columns(to_chip, half):
        which = core if half == 0 else 1 - core
        return pl.ds(pl.multiple_of((to_chip * 2 + which) * share, size), share)

    full = n * base
    spots = [(0, full, 0, full)]
    if extra:
        spots.append((full, extra, 2 * full, 2 * full + extra))
    w_copies = []
    for part, (first, count, _, there) in enumerate(spots):
        for half in range(2):
            w_copies.append(
                pltpu.make_async_remote_copy(
                    src_ref=w_ref.at[pl.ds(first, count), :, w_columns(1 - chip, half)],
                    dst_ref=w_cat.at[pl.ds(there, count), :, pl.ds(half * share, share)],
                    send_sem=w_send.at[part, half],
                    recv_sem=w_recv.at[part, half],
                    device_id={"tp": chip_mate},
                    device_id_type=MESH,
                )
            )
    locals_w = []
    for slot in range(base):
        for i in range(3):
            local_copy(slot, i).start()

    if extra:

        @pl.when(has_extra)
        def _():
            for i in range(3):
                local_copy(base, i).start()

    for part, (first, count, here, _) in enumerate(spots):
        for half in range(2):
            locals_w.append(
                pltpu.make_async_copy(
                    w_ref.at[pl.ds(first, count), :, w_columns(chip, half)],
                    w_cat.at[pl.ds(here, count), :, pl.ds(half * share, share)],
                    local_w_sem.at[part, half],
                )
            )
            locals_w[-1].start()

    span = n * size
    row_id = lax.broadcasted_iota(jnp.int32, (span, span), 0)
    col_id = lax.broadcasted_iota(jnp.int32, (span, span), 1)
    outer, inside = lax.div(row_id, size), lax.rem(row_id, size)
    goal = lax.div(inside, rows) * size + outer * rows + lax.rem(inside, rows)
    swap[...] = jnp.where(goal == col_id, 1.0, 0.0).astype(jnp.bfloat16)

    token_total = n * blocks * rows
    key_block = lax.rem(
        lax.div(lax.broadcasted_iota(jnp.int32, (1, token_total), 1), rows), blocks
    )
    rate = float(size ** (-0.5) * np.log2(np.e))

    def head_bias(head):
        is_head = lax.broadcasted_iota(jnp.int32, mask_ref.shape, 2) == head
        live = jnp.where(is_head, mask_ref[...], 0).astype(jnp.float32)
        live = jnp.sum(live, axis=2, keepdims=True)
        allowed = jnp.zeros((blocks, token_total), jnp.float32)
        for other in range(blocks):
            allowed = jnp.where(key_block == other, live[:, other, :], allowed)
        return jnp.where(allowed > 0.5, 0.0, -jnp.inf)

    def blend(query, keys, values, bias):
        scores = lax.dot_general(
            query, keys, (((1,), (1,)), ((), ())), preferred_element_type=jnp.float32
        )
        scores = scores + bias
        largest = jnp.max(scores, axis=1, keepdims=True)
        weights = jnp.exp2((scores - largest) * rate)
        totals = jnp.sum(weights, axis=1, keepdims=True)
        blended = jnp.dot(
            weights.astype(jnp.bfloat16), values, preferred_element_type=jnp.float32
        )
        return (blended / totals).astype(jnp.bfloat16)

    def swapped(pieces):
        return jnp.dot(
            jnp.concatenate(pieces, axis=1), swap[...], preferred_element_type=jnp.float32
        ).astype(jnp.bfloat16)

    my_columns = pl.ds(pl.multiple_of(me * size, size), size)

    def peer_columns(k):
        return pl.ds(pl.multiple_of(peers[k] * size, size), size)

    my_extra = extra_rank(me)

    def place_of(slot):
        return me * base + slot if slot < base else 2 * full + my_extra

    def o_copy(slot, k):
        return pltpu.make_async_remote_copy(
            src_ref=o_buf.at[slot, :, peer_columns(k)],
            dst_ref=feat.at[place_of(slot)],
            send_sem=o_send.at[slot, k],
            recv_sem=o_recv.at[slot, k],
            device_id={"seq": peers[k]},
            device_id_type=MESH,
        )

    def x_copy(head):
        return pltpu.make_async_remote_copy(
            src_ref=feat.at[head],
            dst_ref=feat.at[full + head],
            send_sem=x_send.at[head],
            recv_sem=x_recv.at[head],
            device_id={"tp": chip_mate},
            device_id_type=MESH,
        )

    def xe_copy(j):
        return pltpu.make_async_remote_copy(
            src_ref=feat.at[2 * full + j],
            dst_ref=feat.at[2 * full + extra + j],
            send_sem=xe_send.at[j],
            recv_sem=xe_recv.at[j],
            device_id={"tp": chip_mate},
            device_id_type=MESH,
        )

    def attend(slot, head):
        keys = k_buf[slot].reshape(token_total, size)
        values = v_buf[slot].reshape(token_total, size)
        bias = head_bias(head)
        o_buf[slot] = swapped(
            [
                blend(
                    q_buf[slot, :, block].reshape(n * rows, size),
                    keys,
                    values,
                    bias[block : block + 1, :],
                )
                for block in range(blocks)
            ]
        )
        for k in order:
            o_copy(slot, k).start()
        feat[place_of(slot)] = o_buf[slot, :, my_columns]

    def forward(j):
        for k in near:
            o_copy(j, k).wait_recv()
            x_copy(lax.rem(me + n - k, n) * base + j).start()

    for j in range(base):
        advance(3 if j == 0 else min(2, len(items) - window - 3))
        qkv_wait_recv(j)
        attend(j, me * base + j)
        if j == 0:
            for copy in w_copies:
                copy.start()
        x_copy(me * base + j).start()
        if j >= 1:
            forward(j - 1)
    if extra:

        @pl.when(has_extra)
        def _():
            qkv_wait_recv(base)
            attend(base, full + my_extra)
            xe_copy(my_extra).start()

    forward(base - 1)
    for j in range(extra):
        owner = lax.rem(shift + j, n)

        @pl.when(owner != me)
        def _():
            gap = lax.rem(me - owner + n, n)
            there = feat.at[2 * full + j]
            pltpu.make_async_remote_copy(
                src_ref=there,
                dst_ref=there,
                send_sem=o_send.at[base, gap],
                recv_sem=o_recv.at[base, gap],
                device_id={"seq": owner},
                device_id_type=MESH,
            ).wait_recv()
            xe_copy(j).start()

    for head in range(full):
        x_copy(head).wait_recv()
    for copy in locals_w:
        copy.wait()
    for copy in w_copies:
        copy.wait_recv()
    groups = 2 * base
    tokens = blocks * rows

    def strip_order(pieces):
        wide = [jnp.concatenate(p, axis=1) for p in pieces]
        return jnp.concatenate(
            [wide[b][r * rows : (r + 1) * rows] for r in range(n) for b in range(blocks)],
            axis=0,
        )

    def cut_blocks(mixes):
        return [[m[:, b * size : (b + 1) * size] for m in mixes] for b in range(blocks)]

    taken = strip_order(
        cut_blocks([swapped([feat[g * n + a] for a in range(n)]) for g in range(groups)])
    )
    deep = 2 * full * rows
    for half in range(2):
        main_sum[half] = jnp.dot(
            taken,
            w_cat[: 2 * full, :, half * share : (half + 1) * share].reshape(deep, share),
            preferred_element_type=jnp.float32,
        ).reshape(n, tokens, share)
    if extra:
        for j in range(extra):
            xe_copy(j).wait_recv()
        late[...] = strip_order(
            cut_blocks([swapped([feat[2 * full + a] for a in range(2 * extra)])])
        ).reshape(n, tokens, size)

    half_n = n // 2
    left = me < half_n
    firsts = [jnp.where(left, half_n, 0), jnp.where(left, 0, half_n)]

    def core_copy(batch):
        there = pl.ds(batch * half_n, half_n)
        return pltpu.make_async_remote_copy(
            src_ref=core_out.at[there],
            dst_ref=core_in.at[there],
            send_sem=core_send.at[batch],
            recv_sem=core_recv.at[batch],
            device_id={"tp": core_mate},
            device_id_type=MESH,
        )

    half_mate = me + 1 - 2 * lax.rem(me, 2)
    at_end = jnp.logical_or(me == 0, me == n - 1)
    far = [firsts[0] + t for t in range(half_n)]
    my_spot = half_n + lax.rem(me, half_n)
    mate_spot = half_n + lax.rem(half_mate, half_n)
    piece = tokens // 2

    def part_of(p):
        return pl.ds(p * piece, piece)

    def relay_copy(t, p):
        return pltpu.make_async_remote_copy(
            src_ref=z_out.at[t, part_of(p)],
            dst_ref=relay.at[t, part_of(p)],
            send_sem=z_send.at[t, p],
            recv_sem=relay_recv.at[t, p],
            device_id={"seq": half_mate},
            device_id_type=MESH,
        )

    def far_copy(t, p):
        return pltpu.make_async_remote_copy(
            src_ref=z_out.at[t, part_of(p)],
            dst_ref=z_in.at[0, part_of(p)],
            send_sem=z_send.at[t, p],
            recv_sem=z_recv.at[0, p],
            device_id={"seq": far[t]},
            device_id_type=MESH,
        )

    def near_copy():
        return pltpu.make_async_remote_copy(
            src_ref=z_out.at[half_n],
            dst_ref=z_in.at[1],
            send_sem=z_send.at[half_n, 0],
            recv_sem=z_recv.at[1, 0],
            device_id={"seq": half_mate},
            device_id_type=MESH,
        )

    def batch_sum(batch, half):
        chosen = pl.ds(firsts[batch], half_n)
        found = main_sum[half, chosen].reshape(half_n * tokens, share)
        if extra:
            found = found + jnp.dot(
                late[chosen].reshape(half_n * tokens, size),
                w_cat[2 * full :, :, half * share : (half + 1) * share].reshape(
                    2 * extra * rows, share
                ),
                preferred_element_type=jnp.float32,
            )
        return found.reshape(half_n, tokens, share)

    for batch in range(2):
        spot = slice(batch * half_n, (batch + 1) * half_n)
        core_out[spot] = batch_sum(batch, 1).astype(jnp.bfloat16)
        core_copy(batch).start()
    for batch in range(2):
        spot = slice(batch * half_n, (batch + 1) * half_n)
        own_sum[spot] = batch_sum(batch, 0)
    core_copy(0).wait_recv()

    @pl.when(at_end)
    def _():
        for t in range(half_n):
            z_out[t] = (own_sum[t] + core_in[t].astype(jnp.float32)).astype(jnp.bfloat16)
            for p in range(2):
                relay_copy(t, p).start()

    core_copy(1).wait_recv()
    z_out[half_n] = (
        own_sum[mate_spot] + core_in[mate_spot].astype(jnp.float32)
    ).astype(jnp.bfloat16)
    near_copy().start()

    @pl.when(jnp.logical_not(at_end))
    def _():
        for t in range(half_n):
            for p in range(2):
                relay_copy(t, p).wait_recv()
                joint = own_sum[t, part_of(p)] + core_in[t, part_of(p)].astype(jnp.float32)
                z_out[t, part_of(p)] = (
                    joint + relay[t, part_of(p)].astype(jnp.float32)
                ).astype(jnp.bfloat16)
                far_copy(t, p).start()

    mine = own_sum[my_spot] + core_in[my_spot].astype(jnp.float32)
    near_copy().wait_recv()
    for p in range(2):
        far_copy(0, p).wait_recv()
    result = mine + z_in[1].astype(jnp.float32) + z_in[0].astype(jnp.float32)
    out_ref[...] = result.astype(jnp.bfloat16).reshape(blocks, rows, share)
    near_copy().wait_send()
    for t in range(half_n):
        for p in range(2):
            relay_copy(t, p).wait_send()

    while sent[0] < len(items):
        advance(1)
    for k in order:
        for j in range(base):
            o_copy(j, k).wait_send()
        if extra:

            @pl.when(has_extra)
            def _():
                o_copy(base, k).wait_send()

    for copy in w_copies:
        copy.wait_send()
    for head in range(full):
        x_copy(head).wait_send()
    for j in range(extra):
        xe_copy(j).wait_send()
    for batch in range(2):
        core_copy(batch).wait_send()


def fused_body(queries, key_vectors, value_vectors, block_mask, out_weight):
    n = lax.axis_size("seq")
    blocks, rows, _ = queries.shape
    heads = block_mask.shape[0]
    size = n * rows
    base, extra = heads // n, heads % n
    share = out_weight.shape[2] // lax.axis_size("tp")
    kind = jnp.bfloat16
    dma = pltpu.SemaphoreType.DMA
    whole = pl.BlockSpec(memory_space=pl.ANY)
    return pl.pallas_call(
        functools.partial(fused_kernel, n),
        out_shape=jax.ShapeDtypeStruct((blocks, rows, share), kind),
        in_specs=[whole, whole, whole, pl.BlockSpec(memory_space=pltpu.VMEM), whole],
        out_specs=pl.BlockSpec(memory_space=pltpu.VMEM),
        scratch_shapes=[pltpu.VMEM((base + 1, n, blocks, rows, size), kind)] * 3
        + [
            pltpu.VMEM((n * size, n * size), kind),
            pltpu.VMEM((base + 1, size, n * size), kind),
            pltpu.VMEM((2 * heads, size, size), kind),
            pltpu.VMEM((2 * heads, rows, 2 * share), kind),
            pltpu.VMEM((2, n, blocks * rows, share), jnp.float32),
            pltpu.VMEM((n, blocks * rows, size), kind),
            pltpu.VMEM((n, blocks * rows, share), jnp.float32),
        ]
        + [pltpu.VMEM((n, blocks * rows, share), kind)] * 5
        + [dma((base + 1, 3))]
        + [dma((2, 2))]
        + [dma((base + 1, 3, n))] * 2
        + [dma((2, 2))] * 2
        + [dma((base + 1, n))] * 2
        + [dma((n * base,))] * 2
        + [dma((extra + 1,))] * 2
        + [dma((n,))] * 2
        + [dma((n, 2))] * 3,
        compiler_params=pltpu.CompilerParams(
            collective_id=0, has_side_effects=True, vmem_limit_bytes=60 * 1024 * 1024
        ),
    )(queries, key_vectors, value_vectors, block_mask.transpose(1, 2, 0), out_weight)


def body(queries, key_vectors, value_vectors, block_mask, out_weight):
    n, tp = lax.axis_size("seq"), lax.axis_size("tp")
    blocks, rows, features = queries.shape
    heads = block_mask.shape[0]
    size = features // heads
    share = out_weight.shape[2] // tp
    fits = (
        n // 2 == 2
        and n % 2 == 0
        and tp // 2 == 2
        and tp % 2 == 0
        and blocks == n
        and rows % 16 == 0
        and size == n * rows
        and size % 128 == 0
        and share % size == 0
        and heads // n > 0
        and 2 * (heads % n) in (0, n)
    )
    if fits:
        return fused_body(queries, key_vectors, value_vectors, block_mask, out_weight)
    return plain_body(queries, key_vectors, value_vectors, block_mask, out_weight)


def solution(mesh):
    return jax.shard_map(
        body,
        mesh=mesh,
        in_specs=(
            P("groups", "seq", "tp"),
            P("groups", "seq", "tp"),
            P("groups", "seq", "tp"),
            P("tp", None, None),
            P("tp", "seq", None),
        ),
        out_specs=P("groups", "seq", "tp"),
        check_vma=False,
    )
```

```python
import functools

import jax
import jax.numpy as jnp
import numpy as np
from jax import lax
from jax.experimental import pallas as pl
from jax.experimental.pallas import tpu as pltpu
from jax.sharding import PartitionSpec as P

MESH = pl.DeviceIdType.MESH

KEYS = 28


def strip_tables(heads_local, blocks, slot_total):
    slot_ids = np.arange(slot_total)
    head_of = slot_ids * heads_local // slot_total
    per_head = np.bincount(head_of, minlength=heads_local)
    head_begin = np.cumsum(per_head) - per_head
    order_in_head = slot_ids - head_begin[head_of]
    head_share = per_head[head_of]
    first_block = order_in_head * blocks // head_share
    block_count = (order_in_head + 1) * blocks // head_share - first_block
    return (head_of, first_block, block_count)


def plain_body(queries, key_vectors, value_vectors, block_mask, out_weight):
    rank_count = lax.axis_size("seq")
    my_rank = lax.axis_index("seq")
    block_total, row_share, feature_width = queries.shape
    heads_local = block_mask.shape[0]
    head_size = feature_width // heads_local
    block_rows = row_share * rank_count
    per_rank = (heads_local + rank_count - 1) // rank_count
    slot_total = rank_count * per_rank
    least_share = slot_total // heads_local
    strip_cap = ((block_total + least_share - 1) // least_share + 1) // 2 * 2
    key_cap = min(KEYS, block_total)
    head_of, first_block, block_count = strip_tables(heads_local, block_total, slot_total)
    slot_grid = np.arange(slot_total).reshape(rank_count, per_rank).T
    paired = jnp.concatenate(
        [
            key_vectors.reshape(block_total, row_share, heads_local, head_size),
            value_vectors.reshape(block_total, row_share, heads_local, head_size),
        ],
        axis=3,
    )
    send_heads = jnp.asarray(head_of[slot_grid].reshape(-1), jnp.int32)
    chosen = jnp.take(paired, send_heads, axis=2)
    chosen = chosen.reshape(block_total, row_share, per_rank, rank_count, 2 * head_size)
    outgoing_pairs = chosen.transpose(2, 0, 3, 1, 4).reshape(
        per_rank, block_total, block_rows, 2 * head_size
    )
    flat_queries = queries.reshape(block_total, row_share, heads_local, head_size).transpose(
        0, 2, 1, 3
    )
    flat_queries = flat_queries.reshape(block_total * heads_local, row_share, head_size)
    positions = np.arange(strip_cap)
    unit_block = first_block[slot_grid][:, None, :] + positions[None, :, None]
    is_live = positions[None, :, None] < block_count[slot_grid][:, None, :]
    unit_index = np.where(is_live, unit_block * heads_local + head_of[slot_grid][:, None, :], 0)
    picked = jnp.take(flat_queries, jnp.asarray(unit_index.reshape(-1), jnp.int32), axis=0)
    picked = jnp.where(
        jnp.asarray(is_live.reshape(-1))[:, None, None], picked, jnp.zeros_like(picked)
    )
    outgoing_queries = picked.reshape(per_rank, strip_cap, block_rows, head_size)
    strip_queries, strip_pairs = (
        lax.all_to_all(outgoing_queries, "seq", split_axis=2, concat_axis=2, tiled=True),
        lax.all_to_all(outgoing_pairs, "seq", split_axis=2, concat_axis=2, tiled=True),
    )
    my_slots = my_rank * per_rank + jnp.arange(per_rank, dtype=jnp.int32)
    my_heads = jnp.asarray(head_of, jnp.int32)[my_slots]
    my_first = jnp.asarray(first_block, jnp.int32)[my_slots]
    query_blocks = jnp.minimum(
        my_first[:, None] + jnp.arange(strip_cap, dtype=jnp.int32)[None, :], block_total - 1
    )
    mask_rows = block_mask[my_heads[:, None], query_blocks]
    column_ids = jnp.arange(block_total, dtype=jnp.int32)
    ranking = (1 - mask_rows) * block_total + column_ids
    key_pick = jnp.argsort(ranking, axis=-1)[..., :key_cap]
    key_live = jnp.take_along_axis(mask_rows, key_pick, axis=-1)
    group_total = per_rank * strip_cap // 2
    query_groups = strip_queries.reshape(group_total, 2, block_rows, head_size)
    pick_groups = key_pick.reshape(group_total, 2, key_cap)
    live_groups = key_live.reshape(group_total, 2, key_cap)
    slot_of_group = jnp.arange(group_total, dtype=jnp.int32) // (strip_cap // 2)
    score_scale = head_size ** (-0.5)

    def attend_group(inputs):
        query_tile, pick_tile, live_tile, slot_index = inputs
        pairs_here = strip_pairs[slot_index]
        gathered = pairs_here[pick_tile]
        scores = (
            jnp.einsum(
                "qid,qkjd->qikj",
                query_tile,
                gathered[..., :head_size],
                preferred_element_type=jnp.float32,
            )
            * score_scale
        )
        allowed = (live_tile > 0)[:, None, :, None]
        scores = jnp.where(allowed, scores, -jnp.inf)
        largest = jnp.max(scores, axis=(2, 3), keepdims=True)
        weights = jnp.exp(scores - largest)
        totals = jnp.sum(weights, axis=(2, 3))
        blended = jnp.einsum(
            "qikj,qkjd->qid",
            weights.astype(jnp.bfloat16),
            gathered[..., head_size:],
            preferred_element_type=jnp.float32,
        )
        return (blended / totals[..., None]).astype(jnp.bfloat16)

    strip_out = lax.map(attend_group, (query_groups, pick_groups, live_groups, slot_of_group))
    outgoing_out = strip_out.reshape(per_rank, strip_cap, block_rows, head_size)
    returned = lax.all_to_all(outgoing_out, "seq", split_axis=2, concat_axis=2, tiled=True)
    slot_mesh, step_mesh = np.meshgrid(np.arange(slot_total), positions, indexing="ij")
    live_slot = step_mesh < block_count[slot_mesh]
    placement_index = np.zeros((block_total, heads_local), np.int64)
    source_index = (
        slot_mesh % per_rank * strip_cap + step_mesh
    ) * rank_count + slot_mesh // per_rank
    placement_index[
        first_block[slot_mesh][live_slot] + step_mesh[live_slot], head_of[slot_mesh][live_slot]
    ] = source_index[live_slot]
    flat_back = returned.reshape(per_rank * strip_cap * rank_count, row_share, head_size)
    own_out = jnp.take(flat_back, jnp.asarray(placement_index.reshape(-1), jnp.int32), axis=0)
    own_out = own_out.reshape(block_total, heads_local, row_share, head_size)
    token_total = block_total * row_share
    token_out = own_out.transpose(0, 2, 1, 3).reshape(token_total, heads_local, head_size)
    partial_sum = jnp.einsum(
        "thd,hdo->to",
        token_out,
        lax.all_gather(out_weight, "seq", axis=1, tiled=True),
        preferred_element_type=jnp.float32,
    )
    summed = lax.psum_scatter(
        partial_sum.astype(jnp.bfloat16), "tp", scatter_dimension=1, tiled=True
    ).astype(jnp.float32)
    return summed.astype(jnp.bfloat16).reshape(block_total, row_share, summed.shape[1])


def fused_kernel(
    n,
    q_ref,
    k_ref,
    v_ref,
    mask_ref,
    w_ref,
    out_ref,
    q_buf,
    k_buf,
    v_buf,
    swap,
    o_buf,
    feat,
    w_cat,
    main_sum,
    late,
    own_sum,
    core_out,
    core_in,
    z_out,
    z_in,
    relay,
    local_sem,
    local_w_sem,
    main_send,
    main_recv,
    w_send,
    w_recv,
    wy_send,
    wy_recv,
    o_send,
    o_recv,
    x_send,
    x_recv,
    xe_send,
    xe_recv,
    core_send,
    core_recv,
    z_send,
    z_recv,
    relay_recv,
):
    me = lax.axis_index("seq")
    tp = lax.axis_index("tp")
    group = lax.axis_index("groups")
    heads = w_ref.shape[0]
    blocks, rows, _ = q_ref.shape
    size = n * rows
    base, extra = heads // n, heads % n
    share = out_ref.shape[2]
    core = lax.rem(tp, 2)
    chip = lax.div(tp, 2)
    core_mate = tp + 1 - 2 * core
    chip_mate = lax.rem(tp + 2, 4)
    shift = lax.rem(tp * extra, n)
    peers = [lax.rem(me + k, n) for k in range(n)]

    def extra_rank(rank):
        return lax.rem(rank - shift + n, n)

    barrier = pltpu.get_barrier_semaphore()
    for k in range(1, n):
        pl.semaphore_signal(
            barrier, inc=1, device_id={"seq": peers[k]}, device_id_type=MESH
        )
    for mate in (core_mate, chip_mate):
        pl.semaphore_signal(barrier, inc=1, device_id={"tp": mate}, device_id_type=MESH)
    pl.semaphore_signal(
        barrier, inc=1, device_id={"groups": 1 - group}, device_id_type=MESH
    )
    pl.semaphore_wait(barrier, n + 2)

    pairs = ((k_ref, k_buf), (q_ref, q_buf), (v_ref, v_buf))

    def column(rank, slot):
        head = rank * base + slot if slot < base else n * base + extra_rank(rank)
        return pl.ds(pl.multiple_of(head * size, size), size)

    def qkv_copy(item, k):
        slot, i = item
        source, buf = pairs[i]
        return pltpu.make_async_remote_copy(
            src_ref=source.at[:, :, column(peers[k], slot)],
            dst_ref=buf.at[slot, me],
            send_sem=main_send.at[slot, i, k],
            recv_sem=main_recv.at[slot, i, k],
            device_id={"seq": peers[k]},
            device_id_type=MESH,
        )

    def qkv_start(item, k):
        if item[0] < base:
            qkv_copy(item, k).start()
        else:

            @pl.when(extra_rank(peers[k]) < extra)
            def _():
                qkv_copy(item, k).start()

    def qkv_wait_send(item, k):
        if item[0] < base:
            qkv_copy(item, k).wait_send()
        else:

            @pl.when(extra_rank(peers[k]) < extra)
            def _():
                qkv_copy(item, k).wait_send()

    def qkv_wait_recv(slot):
        for i in range(3):
            local_copy(slot, i).wait()
            for k in near:
                there = pairs[i][1].at[slot, me]
                pltpu.make_async_remote_copy(
                    src_ref=there,
                    dst_ref=there,
                    send_sem=main_send.at[slot, i, k],
                    recv_sem=main_recv.at[slot, i, k],
                    device_id={"seq": peers[k]},
                    device_id_type=MESH,
                ).wait_recv()

    def local_copy(slot, i):
        source, buf = pairs[i]
        return pltpu.make_async_copy(
            source.at[:, :, column(me, slot)], buf.at[slot, me], local_sem.at[slot, i]
        )

    has_extra = extra_rank(me) < extra
    order = sorted(range(1, n), key=lambda k: -min(k, n - k))
    near = order[::-1]
    slots = base + 1 if extra else base
    items = [(slot, i) for slot in range(slots) for i in range(3)]
    window = len(items)
    sent = [0]

    def advance(count):
        for _ in range(count):
            old = sent[0]
            sent[0] += 1
            for k in near:
                qkv_wait_send(items[old], k)
                if old + window < len(items):
                    qkv_start(items[old + window], k)

    def w_columns(to_chip, half):
        which = core if half == 0 else 1 - core
        return pl.ds(pl.multiple_of((to_chip * 2 + which) * share, size), share)

    full = n * base
    spots = [(0, full, 0, full)]
    if extra:
        spots.append((full, extra, 2 * full, 2 * full + extra))
    w_rows = pl.ds(pl.multiple_of(group * (rows // 2), rows // 2), rows // 2)
    w_copies = []
    for part, (first, count, _, there) in enumerate(spots):
        for half in range(2):
            w_copies.append(
                pltpu.make_async_remote_copy(
                    src_ref=w_ref.at[pl.ds(first, count), w_rows, w_columns(1 - chip, half)],
                    dst_ref=w_cat.at[pl.ds(there, count), w_rows, pl.ds(half * share, share)],
                    send_sem=w_send.at[part, half],
                    recv_sem=w_recv.at[part, half],
                    device_id={"tp": chip_mate},
                    device_id_type=MESH,
                )
            )
            w_copies[-1].start()
    w_shares = []
    for part, (_, count, _, there) in enumerate(spots):
        place = w_cat.at[pl.ds(there, count), w_rows]
        w_shares.append(
            pltpu.make_async_remote_copy(
                src_ref=place,
                dst_ref=place,
                send_sem=wy_send.at[part],
                recv_sem=wy_recv.at[part],
                device_id={"groups": 1 - group},
                device_id_type=MESH,
            )
        )

    for item in items[:window]:
        for k in order:
            qkv_start(item, k)

    locals_w = []
    for slot in range(base):
        for i in range(3):
            local_copy(slot, i).start()

    if extra:

        @pl.when(has_extra)
        def _():
            for i in range(3):
                local_copy(base, i).start()

    for part, (first, count, here, _) in enumerate(spots):
        for half in range(2):
            locals_w.append(
                pltpu.make_async_copy(
                    w_ref.at[pl.ds(first, count), :, w_columns(chip, half)],
                    w_cat.at[pl.ds(here, count), :, pl.ds(half * share, share)],
                    local_w_sem.at[part, half],
                )
            )
            locals_w[-1].start()

    span = n * size
    row_id = lax.broadcasted_iota(jnp.int32, (span, span), 0)
    col_id = lax.broadcasted_iota(jnp.int32, (span, span), 1)
    outer, inside = lax.div(row_id, size), lax.rem(row_id, size)
    goal = lax.div(inside, rows) * size + outer * rows + lax.rem(inside, rows)
    swap[...] = jnp.where(goal == col_id, 1.0, 0.0).astype(jnp.bfloat16)

    token_total = n * blocks * rows
    key_block = lax.rem(
        lax.div(lax.broadcasted_iota(jnp.int32, (1, token_total), 1), rows), blocks
    )
    rate = float(size ** (-0.5) * np.log2(np.e))

    def head_bias(head):
        is_head = lax.broadcasted_iota(jnp.int32, mask_ref.shape, 2) == head
        live = jnp.where(is_head, mask_ref[...], 0).astype(jnp.float32)
        live = jnp.sum(live, axis=2, keepdims=True)
        allowed = jnp.zeros((blocks, token_total), jnp.float32)
        for other in range(blocks):
            allowed = jnp.where(key_block == other, live[:, other, :], allowed)
        return jnp.where(allowed > 0.5, 0.0, -jnp.inf)

    def blend(query, keys, values, bias):
        scores = lax.dot_general(
            query, keys, (((1,), (1,)), ((), ())), preferred_element_type=jnp.float32
        )
        scores = scores + bias
        largest = jnp.max(scores, axis=1, keepdims=True)
        weights = jnp.exp2((scores - largest) * rate)
        totals = jnp.sum(weights, axis=1, keepdims=True)
        blended = jnp.dot(
            weights.astype(jnp.bfloat16), values, preferred_element_type=jnp.float32
        )
        return (blended / totals).astype(jnp.bfloat16)

    def swapped(pieces):
        return jnp.dot(
            jnp.concatenate(pieces, axis=1), swap[...], preferred_element_type=jnp.float32
        ).astype(jnp.bfloat16)

    my_columns = pl.ds(pl.multiple_of(me * size, size), size)

    def peer_columns(k):
        return pl.ds(pl.multiple_of(peers[k] * size, size), size)

    my_extra = extra_rank(me)

    def place_of(slot):
        return me * base + slot if slot < base else 2 * full + my_extra

    def o_copy(slot, k):
        return pltpu.make_async_remote_copy(
            src_ref=o_buf.at[slot, :, peer_columns(k)],
            dst_ref=feat.at[place_of(slot)],
            send_sem=o_send.at[slot, k],
            recv_sem=o_recv.at[slot, k],
            device_id={"seq": peers[k]},
            device_id_type=MESH,
        )

    def x_copy(head):
        return pltpu.make_async_remote_copy(
            src_ref=feat.at[head],
            dst_ref=feat.at[full + head],
            send_sem=x_send.at[head],
            recv_sem=x_recv.at[head],
            device_id={"tp": chip_mate},
            device_id_type=MESH,
        )

    def xe_copy(j):
        return pltpu.make_async_remote_copy(
            src_ref=feat.at[2 * full + j],
            dst_ref=feat.at[2 * full + extra + j],
            send_sem=xe_send.at[j],
            recv_sem=xe_recv.at[j],
            device_id={"tp": chip_mate},
            device_id_type=MESH,
        )

    def attend(slot, head):
        keys = k_buf[slot].reshape(token_total, size)
        values = v_buf[slot].reshape(token_total, size)
        bias = head_bias(head)
        o_buf[slot] = swapped(
            [
                blend(
                    q_buf[slot, :, block].reshape(n * rows, size),
                    keys,
                    values,
                    bias[block : block + 1, :],
                )
                for block in range(blocks)
            ]
        )
        for k in order:
            o_copy(slot, k).start()
        feat[place_of(slot)] = o_buf[slot, :, my_columns]

    def forward(j):
        for k in near:
            o_copy(j, k).wait_recv()
            x_copy(lax.rem(me + n - k, n) * base + j).start()

    for j in range(base):
        advance(3 if j == 0 else min(2, len(items) - window - 3))
        qkv_wait_recv(j)
        attend(j, me * base + j)
        if j == 0:
            for copy in w_copies:
                copy.wait_recv()
            for copy in w_shares:
                copy.start()
        x_copy(me * base + j).start()
        if j >= 1:
            forward(j - 1)
    if extra:

        @pl.when(has_extra)
        def _():
            qkv_wait_recv(base)
            attend(base, full + my_extra)
            xe_copy(my_extra).start()

    forward(base - 1)
    for j in range(extra):
        owner = lax.rem(shift + j, n)

        @pl.when(owner != me)
        def _():
            gap = lax.rem(me - owner + n, n)
            there = feat.at[2 * full + j]
            pltpu.make_async_remote_copy(
                src_ref=there,
                dst_ref=there,
                send_sem=o_send.at[base, gap],
                recv_sem=o_recv.at[base, gap],
                device_id={"seq": owner},
                device_id_type=MESH,
            ).wait_recv()
            xe_copy(j).start()

    for head in range(full):
        x_copy(head).wait_recv()
    for copy in locals_w:
        copy.wait()
    for copy in w_shares:
        copy.wait_recv()
    groups = 2 * base
    tokens = blocks * rows

    def strip_order(pieces):
        wide = [jnp.concatenate(p, axis=1) for p in pieces]
        return jnp.concatenate(
            [wide[b][r * rows : (r + 1) * rows] for r in range(n) for b in range(blocks)],
            axis=0,
        )

    def cut_blocks(mixes):
        return [[m[:, b * size : (b + 1) * size] for m in mixes] for b in range(blocks)]

    taken = strip_order(
        cut_blocks([swapped([feat[g * n + a] for a in range(n)]) for g in range(groups)])
    )
    deep = 2 * full * rows
    for half in range(2):
        main_sum[half] = jnp.dot(
            taken,
            w_cat[: 2 * full, :, half * share : (half + 1) * share].reshape(deep, share),
            preferred_element_type=jnp.float32,
        ).reshape(n, tokens, share)
    if extra:
        for j in range(extra):
            xe_copy(j).wait_recv()
        late[...] = strip_order(
            cut_blocks([swapped([feat[2 * full + a] for a in range(2 * extra)])])
        ).reshape(n, tokens, size)

    half_n = n // 2
    left = me < half_n
    firsts = [jnp.where(left, half_n, 0), jnp.where(left, 0, half_n)]

    def core_copy(batch):
        there = pl.ds(batch * half_n, half_n)
        return pltpu.make_async_remote_copy(
            src_ref=core_out.at[there],
            dst_ref=core_in.at[there],
            send_sem=core_send.at[batch],
            recv_sem=core_recv.at[batch],
            device_id={"tp": core_mate},
            device_id_type=MESH,
        )

    half_mate = me + 1 - 2 * lax.rem(me, 2)
    at_end = jnp.logical_or(me == 0, me == n - 1)
    far = [firsts[0] + t for t in range(half_n)]
    my_spot = half_n + lax.rem(me, half_n)
    mate_spot = half_n + lax.rem(half_mate, half_n)
    piece = tokens // 2

    def part_of(p):
        return pl.ds(p * piece, piece)

    def relay_copy(t, p):
        return pltpu.make_async_remote_copy(
            src_ref=z_out.at[t, part_of(p)],
            dst_ref=relay.at[t, part_of(p)],
            send_sem=z_send.at[t, p],
            recv_sem=relay_recv.at[t, p],
            device_id={"seq": half_mate},
            device_id_type=MESH,
        )

    def far_copy(t, p):
        return pltpu.make_async_remote_copy(
            src_ref=z_out.at[t, part_of(p)],
            dst_ref=z_in.at[0, part_of(p)],
            send_sem=z_send.at[t, p],
            recv_sem=z_recv.at[0, p],
            device_id={"seq": far[t]},
            device_id_type=MESH,
        )

    def near_copy():
        return pltpu.make_async_remote_copy(
            src_ref=z_out.at[half_n],
            dst_ref=z_in.at[1],
            send_sem=z_send.at[half_n, 0],
            recv_sem=z_recv.at[1, 0],
            device_id={"seq": half_mate},
            device_id_type=MESH,
        )

    def batch_sum(batch, half):
        chosen = pl.ds(firsts[batch], half_n)
        found = main_sum[half, chosen].reshape(half_n * tokens, share)
        if extra:
            found = found + jnp.dot(
                late[chosen].reshape(half_n * tokens, size),
                w_cat[2 * full :, :, half * share : (half + 1) * share].reshape(
                    2 * extra * rows, share
                ),
                preferred_element_type=jnp.float32,
            )
        return found.reshape(half_n, tokens, share)

    for batch in range(2):
        spot = slice(batch * half_n, (batch + 1) * half_n)
        core_out[spot] = batch_sum(batch, 1).astype(jnp.bfloat16)
        core_copy(batch).start()
    for batch in range(2):
        spot = slice(batch * half_n, (batch + 1) * half_n)
        own_sum[spot] = batch_sum(batch, 0)
    core_copy(0).wait_recv()

    @pl.when(at_end)
    def _():
        for t in range(half_n):
            z_out[t] = (own_sum[t] + core_in[t].astype(jnp.float32)).astype(jnp.bfloat16)
            for p in range(2):
                relay_copy(t, p).start()

    core_copy(1).wait_recv()
    z_out[half_n] = (
        own_sum[mate_spot] + core_in[mate_spot].astype(jnp.float32)
    ).astype(jnp.bfloat16)
    near_copy().start()

    @pl.when(jnp.logical_not(at_end))
    def _():
        for t in range(half_n):
            for p in range(2):
                relay_copy(t, p).wait_recv()
                joint = own_sum[t, part_of(p)] + core_in[t, part_of(p)].astype(jnp.float32)
                z_out[t, part_of(p)] = (
                    joint + relay[t, part_of(p)].astype(jnp.float32)
                ).astype(jnp.bfloat16)
                far_copy(t, p).start()

    mine = own_sum[my_spot] + core_in[my_spot].astype(jnp.float32)
    near_copy().wait_recv()
    for p in range(2):
        far_copy(0, p).wait_recv()
    result = mine + z_in[1].astype(jnp.float32) + z_in[0].astype(jnp.float32)
    out_ref[...] = result.astype(jnp.bfloat16).reshape(blocks, rows, share)
    near_copy().wait_send()
    for t in range(half_n):
        for p in range(2):
            relay_copy(t, p).wait_send()

    while sent[0] < len(items):
        advance(1)
    for k in order:
        for j in range(base):
            o_copy(j, k).wait_send()
        if extra:

            @pl.when(has_extra)
            def _():
                o_copy(base, k).wait_send()

    for copy in w_copies + w_shares:
        copy.wait_send()
    for head in range(full):
        x_copy(head).wait_send()
    for j in range(extra):
        xe_copy(j).wait_send()
    for batch in range(2):
        core_copy(batch).wait_send()


def fused_body(queries, key_vectors, value_vectors, block_mask, out_weight):
    n = lax.axis_size("seq")
    blocks, rows, _ = queries.shape
    heads = block_mask.shape[0]
    size = n * rows
    base, extra = heads // n, heads % n
    share = out_weight.shape[2] // lax.axis_size("tp")
    kind = jnp.bfloat16
    dma = pltpu.SemaphoreType.DMA
    whole = pl.BlockSpec(memory_space=pl.ANY)
    return pl.pallas_call(
        functools.partial(fused_kernel, n),
        out_shape=jax.ShapeDtypeStruct((blocks, rows, share), kind),
        in_specs=[whole, whole, whole, pl.BlockSpec(memory_space=pltpu.VMEM), whole],
        out_specs=pl.BlockSpec(memory_space=pltpu.VMEM),
        scratch_shapes=[pltpu.VMEM((base + 1, n, blocks, rows, size), kind)] * 3
        + [
            pltpu.VMEM((n * size, n * size), kind),
            pltpu.VMEM((base + 1, size, n * size), kind),
            pltpu.VMEM((2 * heads, size, size), kind),
            pltpu.VMEM((2 * heads, rows, 2 * share), kind),
            pltpu.VMEM((2, n, blocks * rows, share), jnp.float32),
            pltpu.VMEM((n, blocks * rows, size), kind),
            pltpu.VMEM((n, blocks * rows, share), jnp.float32),
        ]
        + [pltpu.VMEM((n, blocks * rows, share), kind)] * 5
        + [dma((base + 1, 3))]
        + [dma((2, 2))]
        + [dma((base + 1, 3, n))] * 2
        + [dma((2, 2))] * 2
        + [dma((2,))] * 2
        + [dma((base + 1, n))] * 2
        + [dma((n * base,))] * 2
        + [dma((extra + 1,))] * 2
        + [dma((n,))] * 2
        + [dma((n, 2))] * 3,
        compiler_params=pltpu.CompilerParams(
            collective_id=0, has_side_effects=True, vmem_limit_bytes=60 * 1024 * 1024
        ),
    )(queries, key_vectors, value_vectors, block_mask.transpose(1, 2, 0), out_weight)


def body(queries, key_vectors, value_vectors, block_mask, out_weight):
    n, tp = lax.axis_size("seq"), lax.axis_size("tp")
    blocks, rows, features = queries.shape
    heads = block_mask.shape[0]
    size = features // heads
    share = out_weight.shape[2] // tp
    fits = (
        n // 2 == 2
        and n % 2 == 0
        and tp // 2 == 2
        and tp % 2 == 0
        and blocks == n
        and rows % 32 == 0
        and lax.axis_size("groups") == 2
        and size == n * rows
        and size % 128 == 0
        and share % size == 0
        and heads // n > 0
        and 2 * (heads % n) in (0, n)
    )
    if fits:
        return fused_body(queries, key_vectors, value_vectors, block_mask, out_weight)
    return plain_body(queries, key_vectors, value_vectors, block_mask, out_weight)


def solution(mesh):
    return jax.shard_map(
        body,
        mesh=mesh,
        in_specs=(
            P("groups", "seq", "tp"),
            P("groups", "seq", "tp"),
            P("groups", "seq", "tp"),
            P("tp", None, None),
            P("tp", "seq", None),
        ),
        out_specs=P("groups", "seq", "tp"),
        check_vma=False,
    )
```

```python
import functools

import jax
import jax.numpy as jnp
import numpy as np
from jax import lax
from jax.experimental import pallas as pl
from jax.experimental.pallas import tpu as pltpu
from jax.sharding import PartitionSpec as P

MESH = pl.DeviceIdType.MESH

KEYS = 28


def strip_tables(heads_local, blocks, slot_total):
    slot_ids = np.arange(slot_total)
    head_of = slot_ids * heads_local // slot_total
    per_head = np.bincount(head_of, minlength=heads_local)
    head_begin = np.cumsum(per_head) - per_head
    order_in_head = slot_ids - head_begin[head_of]
    head_share = per_head[head_of]
    first_block = order_in_head * blocks // head_share
    block_count = (order_in_head + 1) * blocks // head_share - first_block
    return (head_of, first_block, block_count)


def plain_body(queries, key_vectors, value_vectors, block_mask, out_weight):
    rank_count = lax.axis_size("seq")
    my_rank = lax.axis_index("seq")
    block_total, row_share, feature_width = queries.shape
    heads_local = block_mask.shape[0]
    head_size = feature_width // heads_local
    block_rows = row_share * rank_count
    per_rank = (heads_local + rank_count - 1) // rank_count
    slot_total = rank_count * per_rank
    least_share = slot_total // heads_local
    strip_cap = ((block_total + least_share - 1) // least_share + 1) // 2 * 2
    key_cap = min(KEYS, block_total)
    head_of, first_block, block_count = strip_tables(heads_local, block_total, slot_total)
    slot_grid = np.arange(slot_total).reshape(rank_count, per_rank).T
    paired = jnp.concatenate(
        [
            key_vectors.reshape(block_total, row_share, heads_local, head_size),
            value_vectors.reshape(block_total, row_share, heads_local, head_size),
        ],
        axis=3,
    )
    send_heads = jnp.asarray(head_of[slot_grid].reshape(-1), jnp.int32)
    chosen = jnp.take(paired, send_heads, axis=2)
    chosen = chosen.reshape(block_total, row_share, per_rank, rank_count, 2 * head_size)
    outgoing_pairs = chosen.transpose(2, 0, 3, 1, 4).reshape(
        per_rank, block_total, block_rows, 2 * head_size
    )
    flat_queries = queries.reshape(block_total, row_share, heads_local, head_size).transpose(
        0, 2, 1, 3
    )
    flat_queries = flat_queries.reshape(block_total * heads_local, row_share, head_size)
    positions = np.arange(strip_cap)
    unit_block = first_block[slot_grid][:, None, :] + positions[None, :, None]
    is_live = positions[None, :, None] < block_count[slot_grid][:, None, :]
    unit_index = np.where(is_live, unit_block * heads_local + head_of[slot_grid][:, None, :], 0)
    picked = jnp.take(flat_queries, jnp.asarray(unit_index.reshape(-1), jnp.int32), axis=0)
    picked = jnp.where(
        jnp.asarray(is_live.reshape(-1))[:, None, None], picked, jnp.zeros_like(picked)
    )
    outgoing_queries = picked.reshape(per_rank, strip_cap, block_rows, head_size)
    strip_queries, strip_pairs = (
        lax.all_to_all(outgoing_queries, "seq", split_axis=2, concat_axis=2, tiled=True),
        lax.all_to_all(outgoing_pairs, "seq", split_axis=2, concat_axis=2, tiled=True),
    )
    my_slots = my_rank * per_rank + jnp.arange(per_rank, dtype=jnp.int32)
    my_heads = jnp.asarray(head_of, jnp.int32)[my_slots]
    my_first = jnp.asarray(first_block, jnp.int32)[my_slots]
    query_blocks = jnp.minimum(
        my_first[:, None] + jnp.arange(strip_cap, dtype=jnp.int32)[None, :], block_total - 1
    )
    mask_rows = block_mask[my_heads[:, None], query_blocks]
    column_ids = jnp.arange(block_total, dtype=jnp.int32)
    ranking = (1 - mask_rows) * block_total + column_ids
    key_pick = jnp.argsort(ranking, axis=-1)[..., :key_cap]
    key_live = jnp.take_along_axis(mask_rows, key_pick, axis=-1)
    group_total = per_rank * strip_cap // 2
    query_groups = strip_queries.reshape(group_total, 2, block_rows, head_size)
    pick_groups = key_pick.reshape(group_total, 2, key_cap)
    live_groups = key_live.reshape(group_total, 2, key_cap)
    slot_of_group = jnp.arange(group_total, dtype=jnp.int32) // (strip_cap // 2)
    score_scale = head_size ** (-0.5)

    def attend_group(inputs):
        query_tile, pick_tile, live_tile, slot_index = inputs
        pairs_here = strip_pairs[slot_index]
        gathered = pairs_here[pick_tile]
        scores = (
            jnp.einsum(
                "qid,qkjd->qikj",
                query_tile,
                gathered[..., :head_size],
                preferred_element_type=jnp.float32,
            )
            * score_scale
        )
        allowed = (live_tile > 0)[:, None, :, None]
        scores = jnp.where(allowed, scores, -jnp.inf)
        largest = jnp.max(scores, axis=(2, 3), keepdims=True)
        weights = jnp.exp(scores - largest)
        totals = jnp.sum(weights, axis=(2, 3))
        blended = jnp.einsum(
            "qikj,qkjd->qid",
            weights.astype(jnp.bfloat16),
            gathered[..., head_size:],
            preferred_element_type=jnp.float32,
        )
        return (blended / totals[..., None]).astype(jnp.bfloat16)

    strip_out = lax.map(attend_group, (query_groups, pick_groups, live_groups, slot_of_group))
    outgoing_out = strip_out.reshape(per_rank, strip_cap, block_rows, head_size)
    returned = lax.all_to_all(outgoing_out, "seq", split_axis=2, concat_axis=2, tiled=True)
    slot_mesh, step_mesh = np.meshgrid(np.arange(slot_total), positions, indexing="ij")
    live_slot = step_mesh < block_count[slot_mesh]
    placement_index = np.zeros((block_total, heads_local), np.int64)
    source_index = (
        slot_mesh % per_rank * strip_cap + step_mesh
    ) * rank_count + slot_mesh // per_rank
    placement_index[
        first_block[slot_mesh][live_slot] + step_mesh[live_slot], head_of[slot_mesh][live_slot]
    ] = source_index[live_slot]
    flat_back = returned.reshape(per_rank * strip_cap * rank_count, row_share, head_size)
    own_out = jnp.take(flat_back, jnp.asarray(placement_index.reshape(-1), jnp.int32), axis=0)
    own_out = own_out.reshape(block_total, heads_local, row_share, head_size)
    token_total = block_total * row_share
    token_out = own_out.transpose(0, 2, 1, 3).reshape(token_total, heads_local, head_size)
    partial_sum = jnp.einsum(
        "thd,hdo->to",
        token_out,
        lax.all_gather(out_weight, "seq", axis=1, tiled=True),
        preferred_element_type=jnp.float32,
    )
    summed = lax.psum_scatter(
        partial_sum.astype(jnp.bfloat16), "tp", scatter_dimension=1, tiled=True
    ).astype(jnp.float32)
    return summed.astype(jnp.bfloat16).reshape(block_total, row_share, summed.shape[1])


def fused_kernel(
    n,
    q_ref,
    k_ref,
    v_ref,
    mask_ref,
    w_ref,
    out_ref,
    q_buf,
    k_buf,
    v_buf,
    swap,
    o_buf,
    feat,
    w_cat,
    main_sum,
    late,
    own_sum,
    core_out,
    core_in,
    z_out,
    z_in,
    relay,
    local_sem,
    local_w_sem,
    main_send,
    main_recv,
    w_send,
    w_recv,
    o_send,
    o_recv,
    x_send,
    x_recv,
    xe_send,
    xe_recv,
    core_send,
    core_recv,
    z_send,
    z_recv,
    relay_recv,
):
    me = lax.axis_index("seq")
    tp = lax.axis_index("tp")
    heads = w_ref.shape[0]
    blocks, rows, _ = q_ref.shape
    size = n * rows
    base, extra = heads // n, heads % n
    share = out_ref.shape[2]
    core = lax.rem(tp, 2)
    chip = lax.div(tp, 2)
    core_mate = tp + 1 - 2 * core
    chip_mate = lax.rem(tp + 2, 4)
    shift = lax.rem(tp * extra, n)
    peers = [lax.rem(me + k, n) for k in range(n)]

    def extra_rank(rank):
        return lax.rem(rank - shift + n, n)

    barrier = pltpu.get_barrier_semaphore()
    for k in range(1, n):
        pl.semaphore_signal(
            barrier, inc=1, device_id={"seq": peers[k]}, device_id_type=MESH
        )
    for mate in (core_mate, chip_mate):
        pl.semaphore_signal(barrier, inc=1, device_id={"tp": mate}, device_id_type=MESH)
    pl.semaphore_wait(barrier, n + 1)

    pairs = ((k_ref, k_buf), (q_ref, q_buf), (v_ref, v_buf))

    def column(rank, slot):
        head = rank * base + slot if slot < base else n * base + extra_rank(rank)
        return pl.ds(pl.multiple_of(head * size, size), size)

    def qkv_copy(item, k):
        slot, i = item
        source, buf = pairs[i]
        return pltpu.make_async_remote_copy(
            src_ref=source.at[:, :, column(peers[k], slot)],
            dst_ref=buf.at[slot, me],
            send_sem=main_send.at[slot, i, k],
            recv_sem=main_recv.at[slot, i, k],
            device_id={"seq": peers[k]},
            device_id_type=MESH,
        )

    def qkv_start(item, k):
        if item[0] < base:
            qkv_copy(item, k).start()
        else:

            @pl.when(extra_rank(peers[k]) < extra)
            def _():
                qkv_copy(item, k).start()

    def qkv_wait_send(item, k):
        if item[0] < base:
            qkv_copy(item, k).wait_send()
        else:

            @pl.when(extra_rank(peers[k]) < extra)
            def _():
                qkv_copy(item, k).wait_send()

    def qkv_wait_recv(slot):
        for i in range(3):
            local_copy(slot, i).wait()
            for k in near:
                there = pairs[i][1].at[slot, me]
                pltpu.make_async_remote_copy(
                    src_ref=there,
                    dst_ref=there,
                    send_sem=main_send.at[slot, i, k],
                    recv_sem=main_recv.at[slot, i, k],
                    device_id={"seq": peers[k]},
                    device_id_type=MESH,
                ).wait_recv()

    def local_copy(slot, i):
        source, buf = pairs[i]
        return pltpu.make_async_copy(
            source.at[:, :, column(me, slot)], buf.at[slot, me], local_sem.at[slot, i]
        )

    has_extra = extra_rank(me) < extra
    order = sorted(range(1, n), key=lambda k: -min(k, n - k))
    near = order[::-1]
    slots = base + 1 if extra else base
    items = [(slot, i) for slot in range(slots) for i in range(3)]
    window = len(items)
    sent = [0]

    def advance(count):
        for _ in range(count):
            old = sent[0]
            sent[0] += 1
            for k in near:
                qkv_wait_send(items[old], k)
                if old + window < len(items):
                    qkv_start(items[old + window], k)

    for item in items[:window]:
        for k in order:
            qkv_start(item, k)

    def w_columns(to_chip, half):
        which = core if half == 0 else 1 - core
        return pl.ds(pl.multiple_of((to_chip * 2 + which) * share, size), share)

    full = n * base
    spots = [(0, full, 0, full)]
    if extra:
        spots.append((full, extra, 2 * full, 2 * full + extra))
    w_copies = []
    for part, (first, count, _, there) in enumerate(spots):
        for half in range(2):
            w_copies.append(
                pltpu.make_async_remote_copy(
                    src_ref=w_ref.at[pl.ds(first, count), :, w_columns(1 - chip, half)],
                    dst_ref=w_cat.at[pl.ds(there, count), :, pl.ds(half * share, share)],
                    send_sem=w_send.at[part, half],
                    recv_sem=w_recv.at[part, half],
                    device_id={"tp": chip_mate},
                    device_id_type=MESH,
                )
            )
            w_copies[-1].start()
    locals_w = []
    for slot in range(base):
        for i in range(3):
            local_copy(slot, i).start()

    if extra:

        @pl.when(has_extra)
        def _():
            for i in range(3):
                local_copy(base, i).start()

    for part, (first, count, here, _) in enumerate(spots):
        for half in range(2):
            locals_w.append(
                pltpu.make_async_copy(
                    w_ref.at[pl.ds(first, count), :, w_columns(chip, half)],
                    w_cat.at[pl.ds(here, count), :, pl.ds(half * share, share)],
                    local_w_sem.at[part, half],
                )
            )
            locals_w[-1].start()

    span = n * size
    row_id = lax.broadcasted_iota(jnp.int32, (span, span), 0)
    col_id = lax.broadcasted_iota(jnp.int32, (span, span), 1)
    outer, inside = lax.div(row_id, size), lax.rem(row_id, size)
    goal = lax.div(inside, rows) * size + outer * rows + lax.rem(inside, rows)
    swap[...] = jnp.where(goal == col_id, 1.0, 0.0).astype(jnp.bfloat16)

    token_total = n * blocks * rows
    key_block = lax.rem(
        lax.div(lax.broadcasted_iota(jnp.int32, (1, token_total), 1), rows), blocks
    )
    rate = float(size ** (-0.5) * np.log2(np.e))

    def head_bias(head):
        is_head = lax.broadcasted_iota(jnp.int32, mask_ref.shape, 2) == head
        live = jnp.where(is_head, mask_ref[...], 0).astype(jnp.float32)
        live = jnp.sum(live, axis=2, keepdims=True)
        allowed = jnp.zeros((blocks, token_total), jnp.float32)
        for other in range(blocks):
            allowed = jnp.where(key_block == other, live[:, other, :], allowed)
        return jnp.where(allowed > 0.5, 0.0, -jnp.inf)

    def blend(query, keys, values, bias):
        scores = lax.dot_general(
            query, keys, (((1,), (1,)), ((), ())), preferred_element_type=jnp.float32
        )
        scores = scores + bias
        largest = jnp.max(scores, axis=1, keepdims=True)
        weights = jnp.exp2((scores - largest) * rate)
        totals = jnp.sum(weights, axis=1, keepdims=True)
        blended = jnp.dot(
            weights.astype(jnp.bfloat16), values, preferred_element_type=jnp.float32
        )
        return (blended / totals).astype(jnp.bfloat16)

    def swapped(pieces):
        return jnp.dot(
            jnp.concatenate(pieces, axis=1), swap[...], preferred_element_type=jnp.float32
        ).astype(jnp.bfloat16)

    my_columns = pl.ds(pl.multiple_of(me * size, size), size)

    def peer_columns(k):
        return pl.ds(pl.multiple_of(peers[k] * size, size), size)

    my_extra = extra_rank(me)

    def place_of(slot):
        return me * base + slot if slot < base else 2 * full + my_extra

    def o_copy(slot, k):
        return pltpu.make_async_remote_copy(
            src_ref=o_buf.at[slot, :, peer_columns(k)],
            dst_ref=feat.at[place_of(slot)],
            send_sem=o_send.at[slot, k],
            recv_sem=o_recv.at[slot, k],
            device_id={"seq": peers[k]},
            device_id_type=MESH,
        )

    def x_copy(head):
        return pltpu.make_async_remote_copy(
            src_ref=feat.at[head],
            dst_ref=feat.at[full + head],
            send_sem=x_send.at[head],
            recv_sem=x_recv.at[head],
            device_id={"tp": chip_mate},
            device_id_type=MESH,
        )

    def xe_copy(j):
        return pltpu.make_async_remote_copy(
            src_ref=feat.at[2 * full + j],
            dst_ref=feat.at[2 * full + extra + j],
            send_sem=xe_send.at[j],
            recv_sem=xe_recv.at[j],
            device_id={"tp": chip_mate},
            device_id_type=MESH,
        )

    def attend(slot, head):
        keys = k_buf[slot].reshape(token_total, size)
        values = v_buf[slot].reshape(token_total, size)
        bias = head_bias(head)
        o_buf[slot] = swapped(
            [
                blend(
                    q_buf[slot, :, block].reshape(n * rows, size),
                    keys,
                    values,
                    bias[block : block + 1, :],
                )
                for block in range(blocks)
            ]
        )
        for k in order:
            o_copy(slot, k).start()
        feat[place_of(slot)] = o_buf[slot, :, my_columns]

    def forward(j):
        for k in near:
            o_copy(j, k).wait_recv()
            x_copy(lax.rem(me + n - k, n) * base + j).start()

    for j in range(base):
        advance(3 if j == 0 else min(2, len(items) - window - 3))
        qkv_wait_recv(j)
        attend(j, me * base + j)
        x_copy(me * base + j).start()
        if j >= 1:
            forward(j - 1)
    forward(base - 1)
    if extra:

        @pl.when(has_extra)
        def _():
            qkv_wait_recv(base)
            attend(base, full + my_extra)
            xe_copy(my_extra).start()

    for j in range(extra):
        owner = lax.rem(shift + j, n)

        @pl.when(owner != me)
        def _():
            gap = lax.rem(me - owner + n, n)
            there = feat.at[2 * full + j]
            pltpu.make_async_remote_copy(
                src_ref=there,
                dst_ref=there,
                send_sem=o_send.at[base, gap],
                recv_sem=o_recv.at[base, gap],
                device_id={"seq": owner},
                device_id_type=MESH,
            ).wait_recv()
            xe_copy(j).start()

    for head in range(full):
        x_copy(head).wait_recv()
    for copy in locals_w:
        copy.wait()
    for copy in w_copies:
        copy.wait_recv()
    groups = 2 * base
    tokens = blocks * rows

    def strip_order(pieces):
        wide = [jnp.concatenate(p, axis=1) for p in pieces]
        return jnp.concatenate(
            [wide[b][r * rows : (r + 1) * rows] for r in range(n) for b in range(blocks)],
            axis=0,
        )

    def cut_blocks(mixes):
        return [[m[:, b * size : (b + 1) * size] for m in mixes] for b in range(blocks)]

    taken = strip_order(
        cut_blocks([swapped([feat[g * n + a] for a in range(n)]) for g in range(groups)])
    )
    deep = 2 * full * rows
    for half in range(2):
        main_sum[half] = jnp.dot(
            taken,
            w_cat[: 2 * full, :, half * share : (half + 1) * share].reshape(deep, share),
            preferred_element_type=jnp.float32,
        ).reshape(n, tokens, share)
    if extra:
        for j in range(extra):
            xe_copy(j).wait_recv()
        late[...] = strip_order(
            cut_blocks([swapped([feat[2 * full + a] for a in range(2 * extra)])])
        ).reshape(n, tokens, size)

    half_n = n // 2
    left = me < half_n
    firsts = [jnp.where(left, half_n, 0), jnp.where(left, 0, half_n)]

    def core_copy(batch):
        there = pl.ds(batch * half_n, half_n)
        return pltpu.make_async_remote_copy(
            src_ref=core_out.at[there],
            dst_ref=core_in.at[there],
            send_sem=core_send.at[batch],
            recv_sem=core_recv.at[batch],
            device_id={"tp": core_mate},
            device_id_type=MESH,
        )

    half_mate = me + 1 - 2 * lax.rem(me, 2)
    at_end = jnp.logical_or(me == 0, me == n - 1)
    far = [firsts[0] + t for t in range(half_n)]
    my_spot = half_n + lax.rem(me, half_n)
    mate_spot = half_n + lax.rem(half_mate, half_n)
    piece = tokens // 2

    def part_of(p):
        return pl.ds(p * piece, piece)

    def relay_copy(t, p):
        return pltpu.make_async_remote_copy(
            src_ref=z_out.at[t, part_of(p)],
            dst_ref=relay.at[t, part_of(p)],
            send_sem=z_send.at[t, p],
            recv_sem=relay_recv.at[t, p],
            device_id={"seq": half_mate},
            device_id_type=MESH,
        )

    def far_copy(t, p):
        return pltpu.make_async_remote_copy(
            src_ref=z_out.at[t, part_of(p)],
            dst_ref=z_in.at[0, part_of(p)],
            send_sem=z_send.at[t, p],
            recv_sem=z_recv.at[0, p],
            device_id={"seq": far[t]},
            device_id_type=MESH,
        )

    def near_copy():
        return pltpu.make_async_remote_copy(
            src_ref=z_out.at[half_n],
            dst_ref=z_in.at[1],
            send_sem=z_send.at[half_n, 0],
            recv_sem=z_recv.at[1, 0],
            device_id={"seq": half_mate},
            device_id_type=MESH,
        )

    def batch_sum(batch, half):
        chosen = pl.ds(firsts[batch], half_n)
        found = main_sum[half, chosen].reshape(half_n * tokens, share)
        if extra:
            found = found + jnp.dot(
                late[chosen].reshape(half_n * tokens, size),
                w_cat[2 * full :, :, half * share : (half + 1) * share].reshape(
                    2 * extra * rows, share
                ),
                preferred_element_type=jnp.float32,
            )
        return found.reshape(half_n, tokens, share)

    for batch in range(2):
        spot = slice(batch * half_n, (batch + 1) * half_n)
        core_out[spot] = batch_sum(batch, 1).astype(jnp.bfloat16)
        core_copy(batch).start()
    for batch in range(2):
        spot = slice(batch * half_n, (batch + 1) * half_n)
        own_sum[spot] = batch_sum(batch, 0)
    core_copy(0).wait_recv()

    @pl.when(at_end)
    def _():
        for t in range(half_n):
            z_out[t] = (own_sum[t] + core_in[t].astype(jnp.float32)).astype(jnp.bfloat16)
            for p in range(2):
                relay_copy(t, p).start()

    core_copy(1).wait_recv()
    z_out[half_n] = (
        own_sum[mate_spot] + core_in[mate_spot].astype(jnp.float32)
    ).astype(jnp.bfloat16)
    near_copy().start()

    @pl.when(jnp.logical_not(at_end))
    def _():
        for t in range(half_n):
            for p in range(2):
                relay_copy(t, p).wait_recv()
                joint = own_sum[t, part_of(p)] + core_in[t, part_of(p)].astype(jnp.float32)
                z_out[t, part_of(p)] = (
                    joint + relay[t, part_of(p)].astype(jnp.float32)
                ).astype(jnp.bfloat16)
                far_copy(t, p).start()

    mine = own_sum[my_spot] + core_in[my_spot].astype(jnp.float32)
    near_copy().wait_recv()
    for p in range(2):
        far_copy(0, p).wait_recv()
    result = mine + z_in[1].astype(jnp.float32) + z_in[0].astype(jnp.float32)
    out_ref[...] = result.astype(jnp.bfloat16).reshape(blocks, rows, share)
    near_copy().wait_send()
    for t in range(half_n):
        for p in range(2):
            relay_copy(t, p).wait_send()

    while sent[0] < len(items):
        advance(1)
    for k in order:
        for j in range(base):
            o_copy(j, k).wait_send()
        if extra:

            @pl.when(has_extra)
            def _():
                o_copy(base, k).wait_send()

    for copy in w_copies:
        copy.wait_send()
    for head in range(full):
        x_copy(head).wait_send()
    for j in range(extra):
        xe_copy(j).wait_send()
    for batch in range(2):
        core_copy(batch).wait_send()


def fused_body(queries, key_vectors, value_vectors, block_mask, out_weight):
    n = lax.axis_size("seq")
    blocks, rows, _ = queries.shape
    heads = block_mask.shape[0]
    size = n * rows
    base, extra = heads // n, heads % n
    share = out_weight.shape[2] // lax.axis_size("tp")
    kind = jnp.bfloat16
    dma = pltpu.SemaphoreType.DMA
    whole = pl.BlockSpec(memory_space=pl.ANY)
    return pl.pallas_call(
        functools.partial(fused_kernel, n),
        out_shape=jax.ShapeDtypeStruct((blocks, rows, share), kind),
        in_specs=[whole, whole, whole, pl.BlockSpec(memory_space=pltpu.VMEM), whole],
        out_specs=pl.BlockSpec(memory_space=pltpu.VMEM),
        scratch_shapes=[pltpu.VMEM((base + 1, n, blocks, rows, size), kind)] * 3
        + [
            pltpu.VMEM((n * size, n * size), kind),
            pltpu.VMEM((base + 1, size, n * size), kind),
            pltpu.VMEM((2 * heads, size, size), kind),
            pltpu.VMEM((2 * heads, rows, 2 * share), kind),
            pltpu.VMEM((2, n, blocks * rows, share), jnp.float32),
            pltpu.VMEM((n, blocks * rows, size), kind),
            pltpu.VMEM((n, blocks * rows, share), jnp.float32),
        ]
        + [pltpu.VMEM((n, blocks * rows, share), kind)] * 5
        + [dma((base + 1, 3))]
        + [dma((2, 2))]
        + [dma((base + 1, 3, n))] * 2
        + [dma((2, 2))] * 2
        + [dma((base + 1, n))] * 2
        + [dma((n * base,))] * 2
        + [dma((extra + 1,))] * 2
        + [dma((n,))] * 2
        + [dma((n, 2))] * 3,
        compiler_params=pltpu.CompilerParams(
            collective_id=0, has_side_effects=True, vmem_limit_bytes=60 * 1024 * 1024
        ),
    )(queries, key_vectors, value_vectors, block_mask.transpose(1, 2, 0), out_weight)


def body(queries, key_vectors, value_vectors, block_mask, out_weight):
    n, tp = lax.axis_size("seq"), lax.axis_size("tp")
    blocks, rows, features = queries.shape
    heads = block_mask.shape[0]
    size = features // heads
    share = out_weight.shape[2] // tp
    fits = (
        n // 2 == 2
        and n % 2 == 0
        and tp // 2 == 2
        and tp % 2 == 0
        and blocks == n
        and rows % 16 == 0
        and size == n * rows
        and size % 128 == 0
        and share % size == 0
        and heads // n > 0
        and 2 * (heads % n) in (0, n)
    )
    if fits:
        return fused_body(queries, key_vectors, value_vectors, block_mask, out_weight)
    return plain_body(queries, key_vectors, value_vectors, block_mask, out_weight)


def solution(mesh):
    return jax.shard_map(
        body,
        mesh=mesh,
        in_specs=(
            P("groups", "seq", "tp"),
            P("groups", "seq", "tp"),
            P("groups", "seq", "tp"),
            P("tp", None, None),
            P("tp", "seq", None),
        ),
        out_specs=P("groups", "seq", "tp"),
        check_vma=False,
    )
```
